512 devices in a mesh: dom: 512 (over z, x, y, core).
Axes of the slice: x: 4, y: 8, z: 8, core: 2. Of those that a mesh axis runs over, the one named last changes fastest.
Arguments:
- velocity: float32 [3, 3, 8192, 512], P(None, None, 'dom'), may hold values from -6 to 6
- conv_past: float32 [2, 3, 8192, 512], P(None, None, 'dom'), may hold values from -0.6 to 0.6
- metric: float32 [3, 8192, 512], P(None, 'dom'), may hold values from 0.5 to 2
- jacobian: float32 [8192, 512], P('dom'), may hold values from 0.5 to 2
- element_slot: int32 [8192], P('dom'), may hold values from 0 to 15, as said below
Outputs:
- pressure: float32 [4096, 896], P('dom')
- residual: float32 [4096, 896], P('dom')
The draws below stay inside these ranges and needn't reach their ends.
Inputs may be any that keep to these rules, and one draw needn't show every extreme that they name: `element_slot`: within each aligned block of 16 entries (one slab's elements) the entries are a permutation of 0 to 15.
All inputs are finite; a program needn't handle non-finite values.
Results may differ from the reference program's by a relative error of at most 0.0003.
Values sent between devices are 32-bit elements; how exact they have to be, the bound alone decides.
No kernel may reach another device: no remote copies, remote signals or barrier semaphores. Data moves between devices by JAX's collectives and lax.ppermute only.
A program may use at most 64 MiB of HBM per device.

```python
import math
import jax
import jax.numpy as jnp
import numpy as np
from jax import lax

NP = 8
NF = 12
EA = 1
ES = 16
ER = 1
ITERS = 3
E_DEV = 16
ELEMS = 8192
A0 = 8
A1 = 112
A2 = 8


def draw_element_slot(key, part):
    key = jax.random.fold_in(key, 11)
    keys = jax.random.split(key, ELEMS // E_DEV)
    orders = jax.vmap(lambda single: jax.random.permutation(single, E_DEV))(keys)
    return orders.reshape(-1).astype(jnp.int32)


def level_of(own_key, dims, shards, least, top_value):
    def one(dim, shards_of):
        steps = jax.random.uniform(jax.random.fold_in(jax.random.fold_in(own_key, 6), dim), (shards_of,), jnp.float32, least / len(shards), top_value / len(shards))
        return jnp.repeat(jnp.exp(steps), dims[dim] // shards_of).reshape((-1,) + (1,) * (len(dims) - dim - 1))

    factor_of = one(*shards[0])
    for cut in shards[1:]:
        factor_of = factor_of * one(*cut)
    return factor_of


def scatter_about(stream_key, shape, deviation, reach, shards=(), held_as=jnp.bfloat16):
    values = deviation * jax.random.normal(stream_key, shape, jnp.float32)
    if shards:
        values = values * level_of(stream_key, shape, shards, -0.22, 0.18)
    return jnp.clip(values, -reach, reach).astype(held_as)


def setup_inputs(seed: int = 0) -> dict:
    arg_keys = jax.random.split(jax.random.key(seed), 6)
    velocity = scatter_about(arg_keys[0], (3, 3, ELEMS, NP * NP * NP), 1.0, 6.0, ((2, 512),), jnp.float32)
    conv_past = scatter_about(arg_keys[1], (2, 3, ELEMS, NP * NP * NP), 0.1, 0.6, ((2, 512),), jnp.float32)
    metric = jnp.clip(jnp.exp(math.log(2.0) - 1.3862944 * jax.random.uniform(arg_keys[2], (3, ELEMS, NP * NP * NP), jnp.float32) ** level_of(arg_keys[2], (3, ELEMS, NP * NP * NP), ((1, 512),), -0.2, 0.2)), 0.5, 2.0)
    jacobian = jnp.clip(jnp.exp(math.log(2.0) - 1.3862944 * jax.random.uniform(arg_keys[3], (ELEMS, NP * NP * NP), jnp.float32) ** level_of(arg_keys[3], (ELEMS, NP * NP * NP), ((0, 512),), -0.2, 0.2)), 0.5, 2.0)
    element_slot = draw_element_slot(jax.random.fold_in(arg_keys[5], 71), 0)
    return dict(velocity=velocity, conv_past=conv_past, metric=metric, jacobian=jacobian, element_slot=element_slot)


HIGHEST = lax.Precision.HIGHEST
time_step = 0.25
viscosity = 0.05
mass_shift = 0.001

def legendre_pair(points, order):
    before = np.ones(points.shape)
    current = points * 1.0
    for level in range(2, order + 1):
        nextone = ((2 * level - 1) * points * current - (level - 1) * before) / level
        before = current
        current = nextone
    return (current, before)

def jacobi_eigen(matrix):
    size = matrix.shape[0]
    work = matrix * 1.0
    vectors = np.eye(size)
    for sweep in range(30):
        for first in range(size - 1):
            for second in range(first + 1, size):
                off = float(work[first, second])
                if abs(off) > 1e-300:
                    tau = (float(work[second, second]) - float(work[first, first])) / (2.0 * off)
                    if tau >= 0.0:
                        tangent = 1.0 / (tau + (1.0 + tau * tau) ** 0.5)
                    else:
                        tangent = -1.0 / (-tau + (1.0 + tau * tau) ** 0.5)
                    cosine = 1.0 / (1.0 + tangent * tangent) ** 0.5
                    sine = tangent * cosine
                    rotation = np.eye(size)
                    rotation[first, first] = cosine
                    rotation[second, second] = cosine
                    rotation[first, second] = sine
                    rotation[second, first] = -sine
                    work = rotation.T @ work @ rotation
                    vectors = vectors @ rotation
    diagonal_index = np.arange(size)
    return (work[diagonal_index, diagonal_index], vectors)

def build_tables(points_edge, points_fine):
    degree = points_edge - 1
    points = -np.cos(np.pi * np.arange(points_edge) / degree)
    for sweep in range(100):
        top, below = legendre_pair(points, degree)
        points = points - (points * top - below) / (points_edge * top)
    top, below = legendre_pair(points, degree)
    weight_gll = 2.0 / (degree * points_edge * top ** 2)
    spacing = points[:, None] - points[None, :] + np.eye(points_edge)
    barycentric = 1.0 / np.prod(spacing, axis=1)
    derivative = barycentric[None, :] / barycentric[:, None] / spacing
    derivative = derivative * (1.0 - np.eye(points_edge))
    derivative = derivative - np.eye(points_edge) * derivative.sum(axis=1)[:, None]
    fine_points = np.cos(np.pi * (np.arange(points_fine) + 0.75) / (points_fine + 0.5))
    for sweep in range(100):
        top, below = legendre_pair(fine_points, points_fine)
        slope = points_fine * (fine_points * top - below) / (fine_points * fine_points - 1.0)
        fine_points = fine_points - top / slope
    top, below = legendre_pair(fine_points, points_fine)
    slope = points_fine * (fine_points * top - below) / (fine_points * fine_points - 1.0)
    fine_weight = 2.0 / ((1.0 - fine_points * fine_points) * slope * slope)
    fine_points = fine_points[::-1]
    fine_weight = fine_weight[::-1]
    interpolate = np.ones((points_fine, points_edge))
    for column in range(points_edge):
        for other in range(points_edge):
            if other != column:
                interpolate[:, column] = interpolate[:, column] * (fine_points - points[other]) / (points[column] - points[other])
    stiffness = derivative.T @ (weight_gll[:, None] * derivative)
    extent = 3 * degree + 1
    joined_stiff = np.zeros((extent, extent))
    joined_mass = np.zeros(extent)
    for segment in range(3):
        offset = segment * degree
        joined_stiff[offset:offset + points_edge, offset:offset + points_edge] += stiffness
        joined_mass[offset:offset + points_edge] += weight_gll
    low = degree - 1
    high = 2 * degree + 2
    root_mass = np.sqrt(joined_mass[low:high])
    scaled = joined_stiff[low:high, low:high] / root_mass[:, None] / root_mass[None, :]
    scaled = 0.5 * (scaled + scaled.T)
    eigen_values, eigen_vectors = jacobi_eigen(scaled)
    solve_mat = eigen_vectors / root_mass[:, None]
    breadth = high - low
    identity = np.eye(points_edge)
    operator_tables = {'derivative': derivative, 'dpair': np.concatenate([np.kron(derivative, identity).T, np.kron(identity, derivative).T], axis=1), 'interpolate': interpolate, 'ipair': np.kron(interpolate, interpolate).T, 'mass_three': (weight_gll[:, None, None] * weight_gll[None, :, None] * weight_gll[None, None, :]).reshape(points_edge, points_edge * points_edge), 'fine_three': (fine_weight[:, None, None] * fine_weight[None, :, None] * fine_weight[None, None, :]).reshape(points_fine, points_fine * points_fine), 'solve_mat': solve_mat, 'solve_pair': np.kron(solve_mat, solve_mat), 'eigen_axial': eigen_values, 'eigen_around': np.repeat(eigen_values, breadth), 'eigen_radial': np.tile(eigen_values, breadth)}
    return {entry_name: jnp.asarray(entry_value, jnp.float32) for entry_name, entry_value in operator_tables.items()}

def matmul(left, right):
    return jnp.dot(left, right, precision=HIGHEST, preferred_element_type=jnp.float32)

def along_first(field, matrix, form):
    return jnp.einsum(form, field, matrix, precision=HIGHEST, preferred_element_type=jnp.float32)

def gradient(field, operator_tables):
    paired = matmul(field, operator_tables['dpair'])
    streamwise_piece = along_first(field, operator_tables['derivative'], 'ebx,ab->eax')
    return (streamwise_piece, paired[..., :NP * NP], paired[..., NP * NP:])

def gradient_t(streamwise_piece, azimuthal_piece, radial_piece, operator_tables):
    paired = matmul(jnp.concatenate([azimuthal_piece, radial_piece], axis=-1), operator_tables['dpair'].T)
    return paired + along_first(streamwise_piece, operator_tables['derivative'], 'eax,ab->ebx')

def coarse_to_dealiased(field, operator_tables):
    return along_first(matmul(field, operator_tables['ipair']), operator_tables['interpolate'], 'ebx,ab->eax')

def from_fine(field, operator_tables):
    return matmul(along_first(field, operator_tables['interpolate'], 'eax,ab->ebx'), operator_tables['ipair'].T)

def element_forcing(velocity, conv_past, metric, jacobian, operator_tables):
    mass_node = jacobian * operator_tables['mass_three']
    fine_jacobian = coarse_to_dealiased(jacobian, operator_tables) * operator_tables['fine_three']
    advecting_velocities = [coarse_to_dealiased(velocity[0, velocity_component] * metric[velocity_component], operator_tables) for velocity_component in range(3)]
    factors = [mass_node * metric[velocity_component] * metric[velocity_component] for velocity_component in range(3)]
    outputs = []
    for velocity_component in range(3):
        streamwise_piece, azimuthal_piece, radial_piece = gradient(velocity[0, velocity_component], operator_tables)
        pointwise_product = advecting_velocities[0] * coarse_to_dealiased(streamwise_piece, operator_tables) + advecting_velocities[1] * coarse_to_dealiased(azimuthal_piece, operator_tables) + advecting_velocities[2] * coarse_to_dealiased(radial_piece, operator_tables)
        convect = from_fine(fine_jacobian * pointwise_product, operator_tables)
        extrap_term = 3.0 * convect - 3.0 * conv_past[0, velocity_component] + conv_past[1, velocity_component]
        history = 3.0 * velocity[0, velocity_component] - 1.5 * velocity[1, velocity_component] + velocity[2, velocity_component] / 3.0
        guessed = 3.0 * velocity[0, velocity_component] - 3.0 * velocity[1, velocity_component] + velocity[2, velocity_component]
        streamwise_piece, azimuthal_piece, radial_piece = gradient(guessed, operator_tables)
        stiff_term = gradient_t(factors[0] * streamwise_piece, factors[1] * azimuthal_piece, factors[2] * radial_piece, operator_tables)
        helmholtz = viscosity * stiff_term + 11.0 / (6.0 * time_step) * mass_node * guessed
        outputs.append(mass_node * history / time_step - extrap_term - helmholtz)
    outputs.append(mass_node)
    return jnp.stack(outputs)

def element_divergence(accel, metric, jacobian, operator_tables):
    mass_node = jacobian * operator_tables['mass_three']
    return gradient_t(mass_node * metric[0] * accel[0], mass_node * metric[1] * accel[1], mass_node * metric[2] * accel[2], operator_tables)

def element_pressure(values, metric, jacobian, operator_tables):
    mass_node = jacobian * operator_tables['mass_three']
    streamwise_piece, azimuthal_piece, radial_piece = gradient(values, operator_tables)
    stiff_term = gradient_t(mass_node * metric[0] * metric[0] * streamwise_piece, mass_node * metric[1] * metric[1] * azimuthal_piece, mass_node * metric[2] * metric[2] * radial_piece, operator_tables)
    return stiff_term + mass_shift * mass_node * values

def local_solve(extended, metric, jacobian, operator_tables):
    mass_node = jacobian * operator_tables['mass_three']
    scales = [lax.optimization_barrier(jnp.sum(mass_node * metric[velocity_component] * metric[velocity_component], axis=(1, 2))) / 8.0 for velocity_component in range(3)]
    average = lax.optimization_barrier(jnp.sum(mass_node, axis=(1, 2))) / 8.0
    breadth = operator_tables['solve_mat'].shape[0]
    spectra = extended.reshape(-1, breadth, breadth * breadth)
    spectra = along_first(matmul(spectra, operator_tables['solve_pair']), operator_tables['solve_mat'], 'eax,ab->ebx')
    denom = scales[0][:, None, None] * operator_tables['eigen_axial'][None, :, None] + scales[1][:, None, None] * operator_tables['eigen_around'][None, None, :] + scales[2][:, None, None] * operator_tables['eigen_radial'][None, None, :] + mass_shift * average[:, None, None]
    spectra = spectra / denom
    restored = matmul(along_first(spectra, operator_tables['solve_mat'], 'ebx,ab->eax'), operator_tables['solve_pair'].T)
    return restored.reshape(extended.shape)

def element_index(slots, row_base, row_total, breadth, margin, radial_total):
    position = slots.astype(jnp.int32)
    along = (position // (ES * ER))[:, None, None, None]
    beside_all = (position // ER % ES)[:, None, None, None]
    radial = (position % ER)[:, None, None, None]
    offsets = jnp.arange(breadth, dtype=jnp.int32)
    row_index = (row_base + (NP - 1) * along + offsets[None, :, None, None] - margin) % row_total
    turn_index = ((NP - 1) * beside_all + offsets[None, None, :, None] - margin) % A1
    depth_index = (NP - 1) * radial + offsets[None, None, None, :] - margin + (radial_total - A2) // 2
    flat_index = (row_index * A1 + turn_index) * radial_total + depth_index
    return flat_index.reshape(position.shape[0], breadth, breadth * breadth).astype(jnp.int32)

def scatter_rows(values, index, grid_size):
    flat = values.reshape(values.shape[0], -1)
    return jnp.zeros((values.shape[0], grid_size), jnp.float32).at[:, index.reshape(-1)].add(flat)

def reference(velocity, conv_past, metric, jacobian, element_slot):
    operator_tables = build_tables(NP, NF)
    blocks_total = ELEMS // E_DEV
    grid_rows = (NP - 1) * EA * blocks_total
    grid_size = grid_rows * A1 * A2

    def by_block(array, lead):
        shaped = array.reshape(array.shape[:lead] + (blocks_total, E_DEV, NP, NP * NP))
        return jnp.moveaxis(shaped, lead, 0)
    velocity_blocks = by_block(velocity, 2)
    past_blocks = by_block(conv_past, 2)
    metric_blocks = by_block(metric, 1)
    jacobian_blocks = by_block(jacobian, 0)
    slot_blocks = element_slot.reshape(blocks_total, E_DEV)
    row_starts = jnp.arange(blocks_total, dtype=jnp.int32) * ((NP - 1) * EA)
    node_blocks = jax.vmap(lambda slots, row_start: element_index(slots, row_start, grid_rows, NP, 0, A2))(slot_blocks, row_starts)
    ext_blocks = jax.vmap(lambda slots, row_start: element_index(slots, row_start, grid_rows, NP + 2, 1, A2 + 2))(slot_blocks, row_starts)
    forcing = lax.map(lambda group: element_forcing(group[0], group[1], group[2], group[3], operator_tables), (velocity_blocks, past_blocks, metric_blocks, jacobian_blocks))
    summed = scatter_rows(jnp.moveaxis(forcing, 1, 0), node_blocks, grid_size)
    accel = summed[:3] / summed[3:]
    divergence = lax.map(lambda group: element_divergence(accel[:, group[2]], group[0], group[1], operator_tables), (metric_blocks, jacobian_blocks, node_blocks))
    source = scatter_rows(divergence[None], node_blocks, grid_size)[0]

    def operate(vector):
        values = lax.map(lambda group: element_pressure(vector[group[2]], group[0], group[1], operator_tables), (metric_blocks, jacobian_blocks, node_blocks))
        return scatter_rows(values[None], node_blocks, grid_size)[0]

    def schwarz(vector):
        padded = jnp.pad(vector.reshape(grid_rows, A1, A2), ((0, 0), (0, 0), (1, 1))).reshape(-1)
        solved = lax.map(lambda group: local_solve(padded[group[2]], group[0], group[1], operator_tables), (metric_blocks, jacobian_blocks, ext_blocks))
        spread = scatter_rows(solved[None], ext_blocks, grid_rows * A1 * (A2 + 2))[0]
        return spread.reshape(grid_rows, A1, A2 + 2)[:, :, 1:-1].reshape(-1)
    solution = jnp.zeros((grid_size,), jnp.float32)
    residual = source
    direction = source
    previous_sum = jnp.float32(1.0)
    for step in range(ITERS):
        smoothed = schwarz(residual)
        precond_sum = jnp.sum(residual * smoothed)
        direction = smoothed if step == 0 else smoothed + precond_sum / previous_sum * direction
        image = operate(direction)
        step_size = precond_sum / jnp.sum(direction * image)
        solution = solution + step_size * direction
        residual = residual - step_size * image
        previous_sum = precond_sum
    rows = (jnp.arange(blocks_total, dtype=jnp.int32)[:, None] * ((NP - 1) * EA) + jnp.arange(A0, dtype=jnp.int32)[None, :]) % grid_rows
    rows = rows.reshape(-1)
    pressure = solution.reshape(grid_rows, A1 * A2)[rows]
    residual_out = residual.reshape(grid_rows, A1 * A2)[rows]
    return (pressure, residual_out)
```

```python
import functools

import jax
import jax.numpy as jnp
import numpy as np
from jax import lax
from jax.experimental import pallas as pl
from jax.experimental.pallas import tpu as pltpu
from jax.sharding import PartitionSpec as P

NP = 8
NF = 12
ES = 16
LANES = 128
HIGHEST = lax.Precision.HIGHEST
time_step = 0.25
viscosity = 0.05
mass_shift = 0.001
STEPS = (0.45, 0.3)
VMEM = 48 * 1024 * 1024


def legendre_pair(points, order):
    before = np.ones(points.shape)
    current = points * 1.0
    for level in range(2, order + 1):
        nextone = ((2 * level - 1) * points * current - (level - 1) * before) / level
        before = current
        current = nextone
    return (current, before)


def jacobi_eigen(matrix):
    size = matrix.shape[0]
    work = matrix * 1.0
    vectors = np.eye(size)
    for sweep in range(30):
        for first in range(size - 1):
            for second in range(first + 1, size):
                off = float(work[first, second])
                if abs(off) > 1e-300:
                    tau = (float(work[second, second]) - float(work[first, first])) / (2.0 * off)
                    if tau >= 0.0:
                        tangent = 1.0 / (tau + (1.0 + tau * tau) ** 0.5)
                    else:
                        tangent = -1.0 / (-tau + (1.0 + tau * tau) ** 0.5)
                    cosine = 1.0 / (1.0 + tangent * tangent) ** 0.5
                    sine = tangent * cosine
                    rotation = np.eye(size)
                    rotation[first, first] = cosine
                    rotation[second, second] = cosine
                    rotation[first, second] = sine
                    rotation[second, first] = -sine
                    work = rotation.T @ work @ rotation
                    vectors = vectors @ rotation
    diagonal_index = np.arange(size)
    return (work[diagonal_index, diagonal_index], vectors)


def base_tables(points_edge, points_fine):
    degree = points_edge - 1
    points = -np.cos(np.pi * np.arange(points_edge) / degree)
    for sweep in range(100):
        top, below = legendre_pair(points, degree)
        points = points - (points * top - below) / (points_edge * top)
    top, below = legendre_pair(points, degree)
    weight_gll = 2.0 / (degree * points_edge * top**2)
    spacing = points[:, None] - points[None, :] + np.eye(points_edge)
    barycentric = 1.0 / np.prod(spacing, axis=1)
    derivative = barycentric[None, :] / barycentric[:, None] / spacing
    derivative = derivative * (1.0 - np.eye(points_edge))
    derivative = derivative - np.eye(points_edge) * derivative.sum(axis=1)[:, None]
    fine_points = np.cos(np.pi * (np.arange(points_fine) + 0.75) / (points_fine + 0.5))
    for sweep in range(100):
        top, below = legendre_pair(fine_points, points_fine)
        slope = points_fine * (fine_points * top - below) / (fine_points * fine_points - 1.0)
        fine_points = fine_points - top / slope
    top, below = legendre_pair(fine_points, points_fine)
    slope = points_fine * (fine_points * top - below) / (fine_points * fine_points - 1.0)
    fine_weight = 2.0 / ((1.0 - fine_points * fine_points) * slope * slope)
    fine_points = fine_points[::-1]
    fine_weight = fine_weight[::-1]
    interpolate = np.ones((points_fine, points_edge))
    for column in range(points_edge):
        for other in range(points_edge):
            if other != column:
                interpolate[:, column] = (
                    interpolate[:, column]
                    * (fine_points - points[other])
                    / (points[column] - points[other])
                )
    stiffness = derivative.T @ (weight_gll[:, None] * derivative)
    extent = 3 * degree + 1
    joined_stiff = np.zeros((extent, extent))
    joined_mass = np.zeros(extent)
    for segment in range(3):
        offset = segment * degree
        joined_stiff[offset : offset + points_edge, offset : offset + points_edge] += stiffness
        joined_mass[offset : offset + points_edge] += weight_gll
    low = degree - 1
    high = 2 * degree + 2
    root_mass = np.sqrt(joined_mass[low:high])
    scaled = joined_stiff[low:high, low:high] / root_mass[:, None] / root_mass[None, :]
    scaled = 0.5 * (scaled + scaled.T)
    eigen_values, eigen_vectors = jacobi_eigen(scaled)
    solve_mat = eigen_vectors / root_mass[:, None]
    breadth = high - low
    return dict(
        derivative=derivative,
        interpolate=interpolate,
        weight=weight_gll,
        fine_weight=fine_weight,
        solve=solve_mat,
        eigen=eigen_values,
    )


def f32(value):
    return np.ascontiguousarray(value, dtype=np.float32)


def make_tables():
    base = base_tables(NP, NF)
    deriv, interp, solve, eigen = base["derivative"], base["interpolate"], base["solve"], base["eigen"]
    w, wf = base["weight"], base["fine_weight"]
    out = {}
    index = np.arange(NP)

    def sublane(matrix):
        rows = [matrix[index, (index + shift) % NP] for shift in range(NP)]
        return f32(np.broadcast_to(np.stack(rows)[:, :, None], (NP, NP, LANES)))

    def lane(matrix):
        rows = []
        for shift in range(-(NP - 1), NP):
            row = np.zeros(NP)
            for q in range(NP):
                if 0 <= q + shift < NP:
                    row[q] = matrix[q, q + shift]
            rows.append(np.tile(row, ES))
        return f32(np.broadcast_to(np.stack(rows)[:, None, :], (2 * NP - 1, NP, LANES)))

    out["deriv"] = deriv
    out["ds"] = np.stack([sublane(deriv), sublane(deriv.T)])
    out["dq"] = np.stack([lane(deriv), lane(deriv.T)])
    out["w3"] = f32(np.einsum("a,s,q->asq", w, w, w).reshape(1, 512))
    out["jright"] = f32(np.kron(np.eye(ES), interp.T))
    out["jleft"] = f32(np.kron(interp, interp))
    out["wfine"] = f32(np.kron(np.kron(wf, wf)[:, None], np.tile(wf, ES)[None, :]))
    wide = NP + 2
    left = np.zeros((104, 3, wide, NP))
    back = np.zeros((3, wide, NP, 104))
    for i in range(wide):
        for j in range(wide):
            row = i * wide + j
            for a in range(wide):
                for s in range(NP):
                    left[row, 0, a, s] = solve[a, i] * solve[s + 1, j]
                    back[0, a, s, row] = solve[a, i] * solve[s + 1, j]
                left[row, 1, a, NP - 2] = solve[a, i] * solve[0, j]
                left[row, 2, a, 1] = solve[a, i] * solve[wide - 1, j]
                back[1, a, NP - 2, row] = solve[a, i] * solve[0, j]
                back[1, a, NP - 1, row] = solve[a, i] * solve[1, j]
                back[2, a, 1, row] = solve[a, i] * solve[wide - 1, j]
                back[2, a, 0, row] = solve[a, i] * solve[wide - 2, j]
    out["sleft"] = f32(left.reshape(104, 240))
    out["sback"] = f32(back.reshape(240, 104))
    out["sright"] = f32(np.kron(np.eye(ES), solve[1:-1, :]))
    out["srback"] = f32(np.kron(np.eye(ES), solve[1:-1, :].T))
    out["spread"] = f32(np.kron(np.eye(ES), np.ones((NP, wide))) / 8.0)
    lam_a = np.zeros((104, 1))
    lam_s = np.zeros((104, 1))
    lam_a[:100, 0] = np.repeat(eigen, wide)
    lam_s[:100, 0] = np.tile(eigen, wide)
    lam_q = np.tile(eigen, ES)[None, :]
    full = (104, ES * wide)
    out["lam"] = f32(np.stack([np.broadcast_to(lam_a, full), np.broadcast_to(lam_s, full), np.broadcast_to(lam_q, full)]))
    half = np.ones(NP)
    half[0] = half[-1] = 0.5
    out["ws"] = f32(np.broadcast_to(half[:, None], (NP, LANES)))
    return out


TAB = make_tables()
DERIV = [[float(x) for x in row] for row in TAB["deriv"]]
PARAMS = pltpu.CompilerParams(vmem_limit_bytes=VMEM)


def dot(left, right):
    return jnp.dot(left, right, precision=HIGHEST, preferred_element_type=jnp.float32)


def roll(x, shift, axis):
    return pltpu.roll(x, shift % x.shape[axis], axis)


def d_a(x, transposed):
    rows = []
    for a in range(NP):
        total = None
        for b in range(NP):
            term = (DERIV[b][a] if transposed else DERIV[a][b]) * x[b]
            total = term if total is None else total + term
        rows.append(total)
    return jnp.stack(rows)


def d_s(x, coef):
    total = coef[0][None] * x
    for shift in range(1, NP):
        total = total + coef[shift][None] * roll(x, -shift, 1)
    return total


def d_q(x, coef):
    total = coef[NP - 1][None] * x
    for shift in range(1, NP):
        total = total + coef[NP - 1 + shift][None] * roll(x, -shift, 2)
        total = total + coef[NP - 1 - shift][None] * roll(x, shift, 2)
    return total


def gradient(x, ds, dq):
    return d_a(x, False), d_s(x, ds[0]), d_q(x, dq[0])


def gradient_t(xa, xs, xq, ds, dq):
    return d_a(xa, True) + d_s(xs, ds[1]) + d_q(xq, dq[1])


def join_s(x):
    s = lax.broadcasted_iota(jnp.int32, x.shape, 1)
    from_before = roll(roll(x, NP, 2), 1, 1)
    from_after = roll(roll(x, -NP, 2), -1, 1)
    zero = jnp.zeros_like(x)
    return x + jnp.where(s == 0, from_before, jnp.where(s == NP - 1, from_after, zero))


def parity():
    return lax.rem(lax.axis_index("dom"), 2)


def put_payload(even, low, high, inner_ref, cross_ref):
    inner_ref[...] = jnp.where(even, high, low)
    cross_ref[...] = jnp.where(even, low, high)


def get_payload(even, inner_ref, cross_ref):
    inner, cross = inner_ref[...], cross_ref[...]
    return jnp.where(even, cross, inner), jnp.where(even, inner, cross)


def swap_inner(x, count):
    return lax.ppermute(x, "dom", [(i, i ^ 1) for i in range(count)])


def swap_cross(x, count):
    pairs = [(i, (i + 1) % count if i % 2 else (i - 1) % count) for i in range(count)]
    return lax.ppermute(x, "dom", pairs)


def to_lanes(x):
    shape = (x.shape[0], NP, LANES)
    lane = lax.broadcasted_iota(jnp.int32, shape, 2)
    pieces = []
    for tile in range(4):
        first = x[:, :8, tile * LANES : (tile + 1) * LANES]
        second = x[:, 8:, tile * LANES : (tile + 1) * LANES]
        pieces.append(jnp.where(lane < 64, first, roll(second, 64, 2)))
        pieces.append(jnp.where(lane < 64, roll(first, 64, 2), second))
    y = jnp.stack(pieces, axis=1).reshape(x.shape[0] * NP, NP, LANES)
    sub = lax.broadcasted_iota(jnp.int32, y.shape, 1)
    lane = lax.broadcasted_iota(jnp.int32, y.shape, 2)
    for bit in range(3):
        step = 1 << bit
        in_sub = (sub & step) != 0
        in_lane = (lane & (step * 8)) != 0
        up = roll(roll(y, -step, 1), step * 8, 2)
        down = roll(roll(y, step, 1), -step * 8, 2)
        y = jnp.where(in_sub == in_lane, y, jnp.where(in_lane, up, down))
    return y.reshape(x.shape[0], NP, NP, LANES)


def rows(x):
    return x.reshape(NP * NP, LANES)


def planes(x):
    return x.reshape(NP, NP, LANES)


def take_lanes(x, index):
    flat = x.reshape(-1, LANES)
    tiled = jnp.broadcast_to(index[None], x.shape).reshape(-1, LANES)
    return jnp.take_along_axis(flat, tiled, axis=1).reshape(x.shape)


def forcing_kernel(slot_ref, vel_ref, past_ref, metric_ref, jac_ref, w3_ref, ds_ref, dq_ref, jright_ref, jleft_ref, wfine_ref, force_ref, static_ref, inner_ref, cross_ref):
    even = parity() == 0
    ds, dq = ds_ref[...], dq_ref[...]
    jac = jac_ref[...]
    new, mid, old = vel_ref[0], vel_ref[1], vel_ref[2]
    guess = 3.0 * (new - mid) + old
    direct = (jac * w3_ref[...])[None] * (-10.0 * new + 16.0 * mid - 6.0 * old) + 3.0 * past_ref[0] - past_ref[1]
    metric = metric_ref[...]
    lanes = to_lanes(jnp.concatenate([new, guess, direct, metric, jac[None]], axis=0))
    mass_w = to_lanes(jnp.broadcast_to(w3_ref[...], (16, 512))[None])[0]
    new, guess, direct, metric, jac = lanes[0:3], lanes[3:6], lanes[6:9], lanes[9:12], lanes[12]
    fields = [rows(jac)] + [rows(new[d] * metric[d]) for d in range(3)]
    for i in range(3):
        fields.extend(rows(part) for part in gradient(new[i], ds, dq))
    wide = dot(jnp.concatenate(fields, axis=0), jright_ref[...])
    jleft = jleft_ref[...]
    fine = [dot(jleft, wide[64 * k : 64 * k + 64]) for k in range(13)]
    scale = fine[0] * wfine_ref[...]
    products = []
    for i in range(3):
        total = fine[1] * fine[4 + 3 * i] + fine[2] * fine[5 + 3 * i] + fine[3] * fine[6 + 3 * i]
        products.append(lax.dot_general(jleft, scale * total, (((0,), (0,)), ((), ())), precision=HIGHEST, preferred_element_type=jnp.float32))
    coarse = lax.dot_general(jnp.concatenate(products, axis=0), jright_ref[...], (((1,), (1,)), ((), ())), precision=HIGHEST, preferred_element_type=jnp.float32)
    mass = jac * mass_w
    factor = [mass * metric[d] * metric[d] for d in range(3)]
    result = []
    for i in range(3):
        ga, gs, gq = gradient(guess[i], ds, dq)
        stiff = gradient_t(factor[0] * ga, factor[1] * gs, factor[2] * gq, ds, dq)
        result.append(direct[i] - 3.0 * planes(coarse[64 * i : 64 * i + 64]) - viscosity * stiff)
    result.append(mass)
    result.extend([metric[0], metric[1], metric[2]])
    lane = lax.broadcasted_iota(jnp.int32, (NP, LANES), 1)
    index = jnp.zeros((NP, LANES), jnp.int32)
    for e in range(ES):
        index = jnp.where(lane // NP == slot_ref[e], e * NP, index)
    index = index + lane % NP
    result = [take_lanes(x, index) for x in result]
    force = jnp.stack([join_s(x) for x in result[:4]])
    force_ref[...] = force
    static_ref[...] = jnp.stack(result[3:])
    put_payload(even, force[:, 0], force[:, NP - 1], inner_ref, cross_ref)


def factor_kernel(static_ref, spread_ref, lam_ref, op_ref, grad_ref, inv_ref):
    mass = static_ref[0]
    lam = lam_ref[...]
    denom = None
    sums = []
    for d in range(3):
        one = mass * static_ref[1 + d]
        two = one * static_ref[1 + d]
        grad_ref[d] = one
        op_ref[d] = two
        sums.append(jnp.sum(rows(two), axis=0, keepdims=True))
    op_ref[3] = mass_shift * mass
    sums.append(jnp.sum(rows(mass), axis=0, keepdims=True))
    sums.append(jnp.zeros((4, LANES), jnp.float32))
    level = dot(jnp.concatenate(sums, axis=0), spread_ref[...])
    denom = level[0:1] * lam[0] + level[1:2] * lam[1] + level[2:3] * lam[2] + mass_shift * level[3:4]
    inv_ref[...] = 1.0 / denom


def divergence_kernel(force_ref, inner_in, cross_in, grad_ref, ds_ref, dq_ref, div_ref, inner_ref, cross_ref):
    even = parity() == 0
    low, high = get_payload(even, inner_in, cross_in)
    force = force_ref[...]
    whole = jnp.concatenate([(force[:, 0] + low)[:, None], force[:, 1:-1], (force[:, -1] + high)[:, None]], axis=1)
    inv = 1.0 / whole[3]
    parts = [grad_ref[d] * (whole[d] * inv) for d in range(3)]
    div = join_s(gradient_t(parts[0], parts[1], parts[2], ds_ref[...], dq_ref[...]))
    div_ref[...] = div
    put_payload(even, div[:2], div[6:], inner_ref, cross_ref)


def assemble_rows(local, low, high):
    return jnp.concatenate(
        [low[:1], (local[0] + low[1])[None], local[1:-1], (local[-1] + high[0])[None], high[1:]], axis=0
    )


def schwarz(ext, even, inv_ref, sleft_ref, sright_ref, srback_ref, sback_ref, z_ref, inner_ref, cross_ref):
    flat = ext.reshape(80, LANES)
    stacked = jnp.concatenate([flat, roll(flat, NP, 1), roll(flat, -NP, 1)], axis=0)
    spectra = dot(dot(sleft_ref[...], stacked), sright_ref[...]) * inv_ref[...]
    blocks = dot(sback_ref[...], dot(spectra, srback_ref[...]))
    z = blocks[:80] + roll(blocks[80:160], -NP, 1) + roll(blocks[160:], NP, 1)
    z = z.reshape(NP + 2, NP, LANES)
    z_ref[...] = z[1:-1]
    put_payload(even, z[:2], z[8:], inner_ref, cross_ref)


def first_smooth_kernel(div_ref, inner_in, cross_in, inv_ref, sleft_ref, sright_ref, srback_ref, sback_ref, ext_ref, z_ref, inner_ref, cross_ref):
    even = parity() == 0
    low, high = get_payload(even, inner_in, cross_in)
    ext = assemble_rows(div_ref[...], low, high)
    ext_ref[...] = ext
    schwarz(ext, even, inv_ref, sleft_ref, sright_ref, srback_ref, sback_ref, z_ref, inner_ref, cross_ref)


def smooth_kernel(step, before_ref, local_ref, inner_in, cross_in, inv_ref, sleft_ref, sright_ref, srback_ref, sback_ref, image_ref, ext_ref, z_ref, inner_ref, cross_ref):
    even = parity() == 0
    low, high = get_payload(even, inner_in, cross_in)
    image = assemble_rows(local_ref[...], low, high)
    image_ref[...] = image[1:-1]
    ext = before_ref[...] - step * image
    ext_ref[...] = ext
    schwarz(ext, even, inv_ref, sleft_ref, sright_ref, srback_ref, sback_ref, z_ref, inner_ref, cross_ref)


def finish_smooth(even, z_ref, inner_in, cross_in):
    low, high = get_payload(even, inner_in, cross_in)
    z = z_ref[...]
    return jnp.concatenate([z[:2] + low, z[2:6], z[6:] + high], axis=0)


def operate(v, op_ref, ds_ref, dq_ref):
    ds, dq = ds_ref[...], dq_ref[...]
    ga, gs, gq = gradient(v, ds, dq)
    local = gradient_t(op_ref[0] * ga, op_ref[1] * gs, op_ref[2] * gq, ds, dq) + op_ref[3] * v
    return join_s(local)


def operator_kernel(z_ref, inner_in, cross_in, op_ref, ds_ref, dq_ref, v_ref, local_ref, inner_ref, cross_ref):
    even = parity() == 0
    v = finish_smooth(even, z_ref, inner_in, cross_in)
    v_ref[...] = v
    local = operate(v, op_ref, ds_ref, dq_ref)
    local_ref[...] = local
    put_payload(even, local[:2], local[6:], inner_ref, cross_ref)


def last_operator_kernel(z_ref, inner_in, cross_in, op_ref, ds_ref, dq_ref, ws_ref, ext_ref, v0_ref, v1_ref, l0_ref, l1_ref, v_ref, local_ref, inner_ref, cross_ref, sums_ref):
    even = parity() == 0
    v2 = finish_smooth(even, z_ref, inner_in, cross_in)
    v_ref[...] = v2
    l2 = operate(v2, op_ref, ds_ref, dq_ref)
    local_ref[...] = l2
    put_payload(even, l2[:2], l2[6:], inner_ref, cross_ref)
    ws = ws_ref[...]
    v = [v0_ref[...], v1_ref[...], v2]
    images = [l0_ref[...], l1_ref[...], l2]
    residual = ext_ref[...][1:-1]
    residual = jnp.concatenate([0.5 * residual[:1], residual[1:-1], 0.5 * residual[-1:]], axis=0)
    pairs = [(v[i], images[j]) for i, j in ((0, 0), (0, 1), (0, 2), (1, 1), (1, 2), (2, 2))]
    pairs.extend((v[i], residual) for i in range(3))
    lane = lax.broadcasted_iota(jnp.int32, (1, LANES), 1)
    line = jnp.zeros((1, LANES), jnp.float32)
    for k, (left, right) in enumerate(pairs):
        line = jnp.where(lane == k, jnp.sum(jnp.sum(left * right, axis=0) * ws), line)
    sums_ref[...] = jnp.broadcast_to(line, sums_ref.shape)


def to_output(x):
    by_s = [jnp.concatenate([x[a][s : s + 1] for a in range(NP)], axis=0) for s in range(NP - 1)]
    tiles = []
    for tile in range(7):
        at = lax.broadcasted_iota(jnp.int32, (NP, LANES), 1) + tile * LANES
        element = at // 56
        s = (at - element * 56) // NP
        index = element * NP + at % NP
        value = jnp.take_along_axis(by_s[0], index, axis=1)
        for k in range(1, NP - 1):
            value = jnp.where(s == k, jnp.take_along_axis(by_s[k], index, axis=1), value)
        tiles.append(value)
    return jnp.concatenate(tiles, axis=1)


def combine_kernel(sums_ref, ext_ref, v0_ref, v1_ref, v2_ref, w0_ref, w1_ref, local_ref, inner_in, cross_in, p_ref, r_ref):
    even = parity() == 0
    low, high = get_payload(even, inner_in, cross_in)
    w2 = assemble_rows(local_ref[...], low, high)[1:-1]
    line = jnp.sum(sums_ref[...], axis=0, keepdims=True)
    h00, h01, h02, h11, h12, h22, g0, g1, g2 = [line[:, k : k + 1] for k in range(9)]
    m1, m2 = h01 / h00, h02 / h00
    k11, k12, k22 = h11 - m1 * h01, h12 - m1 * h02, h22 - m2 * h02
    f1, f2 = g1 - m1 * g0, g2 - m2 * g0
    n2 = k12 / k11
    c2 = (f2 - n2 * f1) / (k22 - n2 * k12)
    c1 = (f1 - k12 * c2) / k11
    c0 = (g0 - h01 * c1 - h02 * c2) / h00
    v = [v0_ref[...], v1_ref[...], v2_ref[...]]
    pressure = (c0 + STEPS[0])[None] * v[0] + (c1 + STEPS[1])[None] * v[1] + c2[None] * v[2]
    residual = ext_ref[...][1:-1] - (c0[None] * w0_ref[...] + c1[None] * w1_ref[...] + c2[None] * w2)
    p_ref[...] = to_output(pressure)
    r_ref[...] = to_output(residual)


def call(kernel, shapes, *args, smem=()):
    specs = [pl.BlockSpec(memory_space=pltpu.SMEM if k in smem else pltpu.VMEM) for k in range(len(args))]
    return pl.pallas_call(
        kernel,
        out_shape=[jax.ShapeDtypeStruct(shape, jnp.float32) for shape in shapes],
        in_specs=specs,
        out_specs=[pl.BlockSpec(memory_space=pltpu.VMEM)] * len(shapes),
        compiler_params=PARAMS,
    )(*args)


def gather_sums(sums, count):
    if count == 512:
        near = [[16 * i + j for j in range(16)] for i in range(32)]
        far = [[16 * i + j for i in range(32)] for j in range(16)]
        first = lax.all_to_all(sums, "dom", 0, 0, tiled=True, axis_index_groups=near)
        again = jnp.broadcast_to(jnp.sum(first, axis=0, keepdims=True), (32, LANES))
        return lax.all_to_all(again, "dom", 0, 0, tiled=True, axis_index_groups=far)
    return lax.all_to_all(sums, "dom", 0, 0, tiled=True)


def shards(velocity, conv_past, metric, jacobian, element_slot):
    count = lax.axis_size("dom")
    t = {key: jnp.asarray(value) for key, value in TAB.items()}
    field = (NP, NP, LANES)
    edge = (2, NP, LANES)
    ext_shape = (NP + 2, NP, LANES)

    def swap(inner, cross):
        far = swap_cross(cross, count)
        return swap_inner(inner, count), far

    force, static, inner, cross = call(
        forcing_kernel,
        [(4,) + field, (4,) + field, (4, NP, LANES), (4, NP, LANES)],
        element_slot, velocity, conv_past, metric, jacobian,
        t["w3"], t["ds"], t["dq"], t["jright"], t["jleft"], t["wfine"],
        smem=(0,),
    )
    inner, cross = swap(inner, cross)
    op, grad, inv = call(
        factor_kernel, [(4,) + field, (3,) + field, (104, ES * (NP + 2))], static, t["spread"], t["lam"]
    )
    div, inner, cross = call(
        divergence_kernel, [field, edge, edge], force, inner, cross, grad, t["ds"], t["dq"]
    )
    inner, cross = swap(inner, cross)
    solve = (inv, t["sleft"], t["sright"], t["srback"], t["sback"])
    ext, z, inner, cross = call(
        first_smooth_kernel, [ext_shape, field, edge, edge], div, inner, cross, *solve
    )
    vectors, locals_, images = [], [], []
    for step in range(2):
        inner, cross = swap(inner, cross)
        v, local, inner, cross = call(
            operator_kernel, [field, field, edge, edge], z, inner, cross, op, t["ds"], t["dq"]
        )
        vectors.append(v)
        locals_.append(local)
        inner, cross = swap(inner, cross)
        image, ext, z, inner, cross = call(
            functools.partial(smooth_kernel, STEPS[step]),
            [field, ext_shape, field, edge, edge],
            ext, local, inner, cross, *solve,
        )
        images.append(image)
    inner, cross = swap(inner, cross)
    wide = 16 if count == 512 else count
    v, local, inner, cross, sums = call(
        last_operator_kernel,
        [field, field, edge, edge, (wide, LANES)],
        z, inner, cross, op, t["ds"], t["dq"], t["ws"], ext, vectors[0], vectors[1], locals_[0], locals_[1],
    )
    inner, cross = swap(inner, cross)
    sums = gather_sums(sums, count)
    return tuple(
        call(
            combine_kernel,
            [(NP, 896), (NP, 896)],
            sums, ext, vectors[0], vectors[1], v, images[0], images[1], local, inner, cross,
        )
    )


def solution(mesh):
    return jax.shard_map(
        shards,
        mesh=mesh,
        in_specs=(
            P(None, None, "dom", None),
            P(None, None, "dom", None),
            P(None, "dom", None),
            P("dom", None),
            P("dom"),
        ),
        out_specs=(P("dom", None), P("dom", None)),
        check_vma=False,
    )
```

```python
import functools

import jax
import jax.numpy as jnp
import numpy as np
from jax import lax
from jax.experimental import pallas as pl
from jax.experimental.pallas import tpu as pltpu
from jax.sharding import PartitionSpec as P

NP = 8
NF = 12
ES = 16
LANES = 128
time_step = 0.25
viscosity = 0.05
mass_shift = 0.001
STEPS = (0.45, 0.3)
VMEM = 48 * 1024 * 1024
ROWS = 2 * NP - 1
WINDOW = 4 * (NP - 1) + 3
EDGE = NP + 1
MODES = 112


def legendre_pair(points, order):
    before = np.ones(points.shape)
    current = points * 1.0
    for level in range(2, order + 1):
        nextone = ((2 * level - 1) * points * current - (level - 1) * before) / level
        before = current
        current = nextone
    return (current, before)


def jacobi_eigen(matrix):
    size = matrix.shape[0]
    work = matrix * 1.0
    vectors = np.eye(size)
    for sweep in range(30):
        for first in range(size - 1):
            for second in range(first + 1, size):
                off = float(work[first, second])
                if abs(off) > 1e-300:
                    tau = (float(work[second, second]) - float(work[first, first])) / (2.0 * off)
                    if tau >= 0.0:
                        tangent = 1.0 / (tau + (1.0 + tau * tau) ** 0.5)
                    else:
                        tangent = -1.0 / (-tau + (1.0 + tau * tau) ** 0.5)
                    cosine = 1.0 / (1.0 + tangent * tangent) ** 0.5
                    sine = tangent * cosine
                    rotation = np.eye(size)
                    rotation[first, first] = cosine
                    rotation[second, second] = cosine
                    rotation[first, second] = sine
                    rotation[second, first] = -sine
                    work = rotation.T @ work @ rotation
                    vectors = vectors @ rotation
    diagonal_index = np.arange(size)
    return (work[diagonal_index, diagonal_index], vectors)


def base_tables(points_edge, points_fine):
    degree = points_edge - 1
    points = -np.cos(np.pi * np.arange(points_edge) / degree)
    for sweep in range(100):
        top, below = legendre_pair(points, degree)
        points = points - (points * top - below) / (points_edge * top)
    top, below = legendre_pair(points, degree)
    weight_gll = 2.0 / (degree * points_edge * top**2)
    spacing = points[:, None] - points[None, :] + np.eye(points_edge)
    barycentric = 1.0 / np.prod(spacing, axis=1)
    derivative = barycentric[None, :] / barycentric[:, None] / spacing
    derivative = derivative * (1.0 - np.eye(points_edge))
    derivative = derivative - np.eye(points_edge) * derivative.sum(axis=1)[:, None]
    fine_points = np.cos(np.pi * (np.arange(points_fine) + 0.75) / (points_fine + 0.5))
    for sweep in range(100):
        top, below = legendre_pair(fine_points, points_fine)
        slope = points_fine * (fine_points * top - below) / (fine_points * fine_points - 1.0)
        fine_points = fine_points - top / slope
    top, below = legendre_pair(fine_points, points_fine)
    slope = points_fine * (fine_points * top - below) / (fine_points * fine_points - 1.0)
    fine_weight = 2.0 / ((1.0 - fine_points * fine_points) * slope * slope)
    fine_points = fine_points[::-1]
    fine_weight = fine_weight[::-1]
    interpolate = np.ones((points_fine, points_edge))
    for column in range(points_edge):
        for other in range(points_edge):
            if other != column:
                interpolate[:, column] = (
                    interpolate[:, column]
                    * (fine_points - points[other])
                    / (points[column] - points[other])
                )
    stiffness = derivative.T @ (weight_gll[:, None] * derivative)
    extent = 3 * degree + 1
    joined_stiff = np.zeros((extent, extent))
    joined_mass = np.zeros(extent)
    for segment in range(3):
        offset = segment * degree
        joined_stiff[offset : offset + points_edge, offset : offset + points_edge] += stiffness
        joined_mass[offset : offset + points_edge] += weight_gll
    low = degree - 1
    high = 2 * degree + 2
    root_mass = np.sqrt(joined_mass[low:high])
    scaled = joined_stiff[low:high, low:high] / root_mass[:, None] / root_mass[None, :]
    scaled = 0.5 * (scaled + scaled.T)
    eigen_values, eigen_vectors = jacobi_eigen(scaled)
    solve_mat = eigen_vectors / root_mass[:, None]
    breadth = high - low
    return dict(
        derivative=derivative,
        interpolate=interpolate,
        weight=weight_gll,
        fine_weight=fine_weight,
        solve=solve_mat,
        eigen=eigen_values,
    )


def f32(value):
    return np.ascontiguousarray(value, dtype=np.float32)


def halves(value):
    value = np.asarray(value, dtype=np.float32)
    high = value.astype(jnp.bfloat16)
    rest = (value - high.astype(np.float32)).astype(jnp.bfloat16)
    return np.stack([high, rest])


def make_tables():
    base = base_tables(NP, NF)
    deriv, interp, solve, eigen = base["derivative"], base["interpolate"], base["solve"], base["eigen"]
    w, wf = base["weight"], base["fine_weight"]
    out = {}
    index = np.arange(NP)

    def sublane(matrix):
        rows = [matrix[index, (index + shift) % NP] for shift in range(NP)]
        return f32(np.broadcast_to(np.stack(rows)[:, :, None], (NP, NP, LANES)))

    def lane(matrix):
        rows = []
        for shift in range(-(NP - 1), NP):
            row = np.zeros(NP)
            for q in range(NP):
                if 0 <= q + shift < NP:
                    row[q] = matrix[q, q + shift]
            rows.append(np.tile(row, ES))
        return f32(np.broadcast_to(np.stack(rows)[:, None, :], (2 * NP - 1, NP, LANES)))

    out["ds"] = np.stack([sublane(deriv), sublane(deriv.T)])
    out["dq"] = np.stack([lane(deriv), lane(deriv.T)])
    out["w3"] = f32(np.einsum("a,s,q->asq", w, w, w).reshape(1, 512))
    out["wmass"] = f32(np.tile(np.einsum("a,s,q->asq", w, w, w), (1, 1, ES)))
    out["jright"] = halves(np.kron(np.eye(ES), interp.T))
    out["jright_t"] = halves(np.kron(np.eye(ES), interp))
    out["jleft"] = halves(np.kron(interp, interp))
    out["jleft_t"] = halves(np.kron(interp, interp).T)
    out["wfine"] = f32(np.kron(np.kron(wf, wf)[:, None], np.tile(wf, ES)[None, :]))
    wide = NP + 2
    left = np.zeros((MODES, 3, wide, NP))
    back = np.zeros((3, wide, NP, MODES))
    for i in range(wide):
        for j in range(wide):
            row = i * wide + j
            for a in range(wide):
                for s in range(NP):
                    left[row, 0, a, s] = solve[a, i] * solve[s + 1, j]
                    back[0, a, s, row] = solve[a, i] * solve[s + 1, j]
                left[row, 1, a, NP - 2] = solve[a, i] * solve[0, j]
                left[row, 2, a, 1] = solve[a, i] * solve[wide - 1, j]
                back[1, a, NP - 2, row] = solve[a, i] * solve[0, j]
                back[1, a, NP - 1, row] = solve[a, i] * solve[1, j]
                back[2, a, 1, row] = solve[a, i] * solve[wide - 1, j]
                back[2, a, 0, row] = solve[a, i] * solve[wide - 2, j]
    out["sleft"] = halves(left.reshape(MODES, 240))
    out["sback"] = halves(back.reshape(240, MODES))
    out["sright"] = halves(np.kron(np.eye(ES), solve[1:-1, :]))
    out["srback"] = halves(np.kron(np.eye(ES), solve[1:-1, :].T))
    out["spread"] = f32(np.kron(np.eye(ES), np.ones((NP, wide))) / 8.0)
    lam_a = np.zeros((MODES, 1))
    lam_s = np.zeros((MODES, 1))
    lam_a[:100, 0] = np.repeat(eigen, wide)
    lam_s[:100, 0] = np.tile(eigen, wide)
    lam_q = np.tile(eigen, ES)[None, :]
    full = (MODES, ES * wide)
    out["lam"] = f32(np.stack([np.broadcast_to(lam_a, full), np.broadcast_to(lam_s, full), np.broadcast_to(lam_q, full)]))
    half = np.ones(NP)
    half[0] = half[-1] = 0.5
    out["ws"] = f32(np.broadcast_to(half[:, None], (NP, LANES)))
    return out


TAB = make_tables()
DERIV = [[float(x) for x in row] for row in base_tables(NP, NF)["derivative"].astype(np.float32)]
PARAMS = pltpu.CompilerParams(vmem_limit_bytes=VMEM)


def full_dot(left, right):
    return jnp.dot(left, right, precision=lax.Precision.HIGHEST, preferred_element_type=jnp.float32)


def short_dot(left, right):
    return jnp.dot(left, right, preferred_element_type=jnp.float32)


def split(x):
    high = x.astype(jnp.bfloat16)
    return high, (x - high.astype(jnp.float32)).astype(jnp.bfloat16)


def left_dot(table, x):
    high, rest = split(x)
    return short_dot(table[0], high) + (short_dot(table[1], high) + short_dot(table[0], rest))


def right_dot(x, table):
    high, rest = split(x)
    return short_dot(high, table[0]) + (short_dot(high, table[1]) + short_dot(rest, table[0]))


def roll(x, shift, axis):
    return pltpu.roll(x, shift % x.shape[axis], axis)


def d_a(x, transposed):
    rows = []
    for a in range(NP):
        total = None
        for b in range(NP):
            term = (DERIV[b][a] if transposed else DERIV[a][b]) * x[b]
            total = term if total is None else total + term
        rows.append(total)
    return jnp.stack(rows)


def d_s(x, coef):
    total = coef[0][None] * x
    for shift in range(1, NP):
        total = total + coef[shift][None] * roll(x, -shift, 1)
    return total


def d_q(x, coef):
    total = coef[NP - 1][None] * x
    for shift in range(1, NP):
        total = total + coef[NP - 1 + shift][None] * roll(x, -shift, 2)
        total = total + coef[NP - 1 - shift][None] * roll(x, shift, 2)
    return total


def gradient(x, ds, dq):
    return d_a(x, False), d_s(x, ds[0]), d_q(x, dq[0])


def gradient_t(xa, xs, xq, ds, dq):
    return d_a(xa, True) + d_s(xs, ds[1]) + d_q(xq, dq[1])


def join_s(x):
    s = lax.broadcasted_iota(jnp.int32, x.shape, 1)
    from_before = roll(roll(x, NP, 2), 1, 1)
    from_after = roll(roll(x, -NP, 2), -1, 1)
    zero = jnp.zeros_like(x)
    return x + jnp.where(s == 0, from_before, jnp.where(s == NP - 1, from_after, zero))


def parity():
    return lax.rem(lax.axis_index("dom"), 2)


def swap_inner(x, count):
    return lax.ppermute(x, "dom", [(i, i ^ 1) for i in range(count)])


def swap_cross(x, count):
    pairs = [(i, (i + 1) % count if i % 2 else (i - 1) % count) for i in range(count)]
    return lax.ppermute(x, "dom", pairs)


def to_lanes(x):
    shape = (x.shape[0], NP, LANES)
    lane = lax.broadcasted_iota(jnp.int32, shape, 2)
    pieces = []
    for tile in range(4):
        first = x[:, :8, tile * LANES : (tile + 1) * LANES]
        second = x[:, 8:, tile * LANES : (tile + 1) * LANES]
        pieces.append(jnp.where(lane < 64, first, roll(second, 64, 2)))
        pieces.append(jnp.where(lane < 64, roll(first, 64, 2), second))
    y = jnp.stack(pieces, axis=1).reshape(x.shape[0] * NP, NP, LANES)
    sub = lax.broadcasted_iota(jnp.int32, y.shape, 1)
    lane = lax.broadcasted_iota(jnp.int32, y.shape, 2)
    for bit in range(3):
        step = 1 << bit
        in_sub = (sub & step) != 0
        in_lane = (lane & (step * 8)) != 0
        up = roll(roll(y, -step, 1), step * 8, 2)
        down = roll(roll(y, step, 1), -step * 8, 2)
        y = jnp.where(in_sub == in_lane, y, jnp.where(in_lane, up, down))
    return y.reshape(x.shape[0], NP, NP, LANES)


def rows(x):
    return x.reshape(NP * NP, LANES)


def planes(x):
    return x.reshape(NP, NP, LANES)


def take_lanes(x, index):
    flat = x.reshape(-1, LANES)
    tiled = jnp.broadcast_to(index[None], x.shape).reshape(-1, LANES)
    return jnp.take_along_axis(flat, tiled, axis=1).reshape(x.shape)


def forcing_kernel(slot_in, vel_in, past_in, metric_in, jac_in, w3_in, wmass_in, ds_in, dq_in, jright_in, jright_t_in, jleft_in, jleft_t_in, wfine_in, pack_ref, cross_ref, slot_ref, vel_ref, past_ref, metric_ref, jac_ref, w3_ref, wmass_ref, ds_ref, dq_ref, jright_ref, jright_t_ref, jleft_ref, jleft_t_ref, wfine_ref, sems):
    sources = (slot_in, vel_in, past_in, metric_in, jac_in, w3_in, wmass_in, ds_in, dq_in, jright_in, jright_t_in, jleft_in, jleft_t_in, wfine_in)
    targets = (slot_ref, vel_ref, past_ref, metric_ref, jac_ref, w3_ref, wmass_ref, ds_ref, dq_ref, jright_ref, jright_t_ref, jleft_ref, jleft_t_ref, wfine_ref)
    copies = [pltpu.make_async_copy(x, y, sems.at[k]) for k, (x, y) in enumerate(zip(sources, targets))]
    for copy in copies:
        copy.start()
    for copy in copies:
        copy.wait()
    even = parity() == 0
    ds, dq = ds_ref[...], dq_ref[...]
    jac = jac_ref[...]
    new, mid, old = vel_ref[0], vel_ref[1], vel_ref[2]
    guess = 3.0 * (new - mid) + old
    direct = (jac * w3_ref[...])[None] * (-10.0 * new + 16.0 * mid - 6.0 * old) + 3.0 * past_ref[0] - past_ref[1]
    lanes = to_lanes(jnp.concatenate([new, guess, direct, metric_ref[...], jac[None]], axis=0))
    new, guess, direct, metric, jac = lanes[0:3], lanes[3:6], lanes[6:9], lanes[9:12], lanes[12]
    fields = [rows(jac)] + [rows(new[d] * metric[d]) for d in range(3)]
    for i in range(3):
        fields.extend(rows(part) for part in gradient(new[i], ds, dq))
    wide = right_dot(jnp.concatenate(fields, axis=0), jright_ref)
    fine = [left_dot(jleft_ref, wide[64 * k : 64 * k + 64]) for k in range(13)]
    scale = fine[0] * wfine_ref[...]
    products = []
    for i in range(3):
        total = fine[1] * fine[4 + 3 * i] + fine[2] * fine[5 + 3 * i] + fine[3] * fine[6 + 3 * i]
        products.append(left_dot(jleft_t_ref, scale * total))
    coarse = right_dot(jnp.concatenate(products, axis=0), jright_t_ref)
    mass = jac * wmass_ref[...]
    factor = [mass * metric[d] * metric[d] for d in range(3)]
    result = []
    for i in range(3):
        ga, gs, gq = gradient(guess[i], ds, dq)
        stiff = gradient_t(factor[0] * ga, factor[1] * gs, factor[2] * gq, ds, dq)
        result.append(direct[i] - 3.0 * planes(coarse[64 * i : 64 * i + 64]) - viscosity * stiff)
    result.extend([mass, metric[0], metric[1], metric[2]])
    lane = lax.broadcasted_iota(jnp.int32, (NP, LANES), 1)
    index = jnp.zeros((NP, LANES), jnp.int32)
    for e in range(ES):
        index = jnp.where(lane // NP == slot_ref[e], e * NP, index)
    index = index + lane % NP
    result = [take_lanes(x, index) for x in result]
    for k in range(4):
        joined = join_s(result[k])
        cross_ref[k] = jnp.where(even, joined[0], joined[NP - 1])
        pack_ref[NP * k : NP * k + NP] = joined if k < 3 else result[k]
    for k in range(4, 7):
        pack_ref[NP * k : NP * k + NP] = result[k]


def pair_kernel(pack_ref, cross_in, out_ref):
    out_ref[: 7 * NP] = pack_ref[...]
    out_ref[7 * NP :] = cross_in[...]


def chip_rows(first, second):
    return jnp.concatenate([first[:-1], (first[-1] + second[0])[None], second[1:]], axis=0)


def own_rows(even, x):
    return jnp.where(even, x[:NP], x[NP - 1 :])


def edge_rows(even, x):
    return jnp.where(even, x[:EDGE], x[ROWS - EDGE :])


def divergence_kernel(own_ref, mate_ref, ds_ref, dq_ref, div_ref, op_ref, level_ref, cross_ref):
    even = parity() == 0
    own, mate = own_ref[...], mate_ref[...]
    packs = [jnp.where(even, own, mate), jnp.where(even, mate, own)]
    parts = [[pack[NP * k : NP * k + NP] for k in range(7)] for pack in packs]
    low, high = packs[0][7 * NP :], packs[1][7 * NP :]
    sides = []
    for k in range(4):
        first, second = parts[0][k], parts[1][k]
        if k == 3:
            first, second = join_s(first), join_s(second)
        whole = chip_rows(first, second)
        sides.append(jnp.concatenate([(whole[0] + low[k])[None], whole[1:-1], (whole[-1] + high[k])[None]], axis=0))
    inv = 1.0 / sides[3]
    accel = [sides[d] * inv for d in range(3)]
    div = []
    levels = []
    for layer in range(2):
        mass = parts[layer][3]
        at = (NP - 1) * layer
        sums = []
        terms = []
        for d in range(3):
            one = mass * parts[layer][4 + d]
            two = one * parts[layer][4 + d]
            op_ref[layer, d] = two
            sums.append(jnp.sum(rows(two), axis=0, keepdims=True))
            terms.append(one * accel[d][at : at + NP])
        op_ref[layer, 3] = mass_shift * mass
        sums.append(jnp.sum(rows(mass), axis=0, keepdims=True))
        sums.append(jnp.zeros((4, LANES), jnp.float32))
        levels.append(jnp.concatenate(sums, axis=0))
        level_ref[layer] = levels[layer]
        div.append(join_s(gradient_t(terms[0], terms[1], terms[2], ds_ref[...], dq_ref[...])))
    whole = chip_rows(div[0], div[1])
    div_ref[...] = whole
    cross_ref[:EDGE] = edge_rows(even, whole)
    cross_ref[EDGE] = jnp.where(even, levels[0], levels[1])


def window(local, low, high):
    return jnp.concatenate(
        [low[: EDGE - 1], (low[EDGE - 1] + local[0])[None], local[1:-1], (local[-1] + high[0])[None], high[1:EDGE]],
        axis=0,
    )


def inverse_levels(levels, spread_ref, lam_ref):
    result = []
    for level in levels:
        level = full_dot(level, spread_ref[...])
        denom = level[0:1] * lam_ref[0] + level[1:2] * lam_ref[1] + level[2:3] * lam_ref[2] + mass_shift * level[3:4]
        result.append(1.0 / denom)
    return result


def schwarz(wide, inv_ref, sleft_ref, sright_ref, srback_ref, sback_ref):
    before, after = roll(wide, NP, 2), roll(wide, -NP, 2)
    columns = []
    for layer in range(4):
        at = (NP - 1) * layer
        columns.append(jnp.concatenate([x[at : at + NP + 2].reshape(80, LANES) for x in (wide, before, after)], axis=0))
    spectra = left_dot(sleft_ref, jnp.concatenate(columns, axis=1))
    spectra = jnp.concatenate([spectra[:, LANES * k : LANES * k + LANES] for k in range(4)], axis=0)
    spectra = right_dot(right_dot(spectra, sright_ref) * inv_ref[...], srback_ref)
    spectra = jnp.concatenate([spectra[MODES * k : MODES * k + MODES] for k in range(4)], axis=1)
    blocks = left_dot(sback_ref, spectra)
    z = []
    for layer in range(4):
        part = blocks[:, LANES * layer : LANES * layer + LANES]
        part = part[:80] + roll(part[80:160], -NP, 1) + roll(part[160:], NP, 1)
        z.append(part.reshape(NP + 2, NP, LANES))
    middle = jnp.concatenate([z[1][1:8], (z[1][8] + z[2][1])[None], z[2][2:9]], axis=0)
    first = jnp.concatenate([z[0][8:10], jnp.zeros((4, NP, LANES), jnp.float32), z[2][0:1], jnp.zeros((1, NP, LANES), jnp.float32), z[1][9:10], jnp.zeros((4, NP, LANES), jnp.float32), z[3][0:2]], axis=0)
    return middle + first


def operate(v, op_ref, ds_ref, dq_ref):
    ds, dq = ds_ref[...], dq_ref[...]
    parts = []
    for layer in range(2):
        x = v[(NP - 1) * layer : (NP - 1) * layer + NP]
        ga, gs, gq = gradient(x, ds, dq)
        local = gradient_t(op_ref[layer, 0] * ga, op_ref[layer, 1] * gs, op_ref[layer, 2] * gq, ds, dq)
        parts.append(join_s(local + op_ref[layer, 3] * x))
    return chip_rows(parts[0], parts[1])


def sides_of(even, own_in, mate_in):
    own, mate = own_in[...], mate_in[...]
    return jnp.where(even, own, mate), jnp.where(even, mate, own)


def first_kernel(div_ref, own_in, mate_in, level_ref, spread_ref, lam_ref, op_ref, ds_ref, dq_ref, sleft_ref, sright_ref, srback_ref, sback_ref, wide_ref, inv_ref, v_ref, local_ref, cross_ref):
    even = parity() == 0
    low, high = sides_of(even, own_in, mate_in)
    wide = window(div_ref[...], low, high)
    wide_ref[...] = wide
    for k, inv in enumerate(inverse_levels([low[EDGE], level_ref[0], level_ref[1], high[EDGE]], spread_ref, lam_ref)):
        inv_ref[MODES * k : MODES * k + MODES] = inv
    v = schwarz(wide, inv_ref, sleft_ref, sright_ref, srback_ref, sback_ref)
    v_ref[...] = v
    local = operate(v, op_ref, ds_ref, dq_ref)
    local_ref[...] = local
    cross_ref[...] = edge_rows(even, local)


def next_kernel(step, before_ref, image_ref, own_in, mate_in, inv_ref, op_ref, ds_ref, dq_ref, sleft_ref, sright_ref, srback_ref, sback_ref, own_image_ref, wide_ref, v_ref, local_ref, cross_ref):
    even = parity() == 0
    low, high = sides_of(even, own_in, mate_in)
    image = window(image_ref[...], low, high)
    own_image_ref[...] = own_rows(even, image[NP : NP + ROWS])
    wide = before_ref[...] - step * image
    wide_ref[...] = wide
    v = schwarz(wide, inv_ref, sleft_ref, sright_ref, srback_ref, sback_ref)
    v_ref[...] = v
    local = operate(v, op_ref, ds_ref, dq_ref)
    local_ref[...] = local
    cross_ref[...] = edge_rows(even, local)


def last_kernel(step, before_ref, image_ref, own_in, mate_in, inv_ref, op_ref, ds_ref, dq_ref, sleft_ref, sright_ref, srback_ref, sback_ref, ws_ref, v0_ref, v1_ref, l0_ref, own_image_ref, own_ref, sums_ref):
    even = parity() == 0
    low, high = sides_of(even, own_in, mate_in)
    image = window(image_ref[...], low, high)
    own_image_ref[...] = own_rows(even, image[NP : NP + ROWS])
    residual = before_ref[NP : NP + ROWS] - step * image[NP : NP + ROWS]
    wide = before_ref[...] - step * image
    v2 = schwarz(wide, inv_ref, sleft_ref, sright_ref, srback_ref, sback_ref)
    l2 = operate(v2, op_ref, ds_ref, dq_ref)
    v = [v0_ref[...], v1_ref[...], v2]
    images = [l0_ref[...], image_ref[...], l2]
    for k, x in enumerate((v[0], v[1], v2, l2, residual)):
        own_ref[k] = own_rows(even, x)
    weighted = jnp.concatenate([0.5 * residual[:1], residual[1:-1], 0.5 * residual[-1:]], axis=0)
    ws = ws_ref[...]
    pairs = [(v[i], images[j]) for i, j in ((0, 0), (0, 1), (0, 2), (1, 1), (1, 2), (2, 2))]
    pairs.extend((v[i], weighted) for i in range(3))
    lane = lax.broadcasted_iota(jnp.int32, (NP, LANES), 1)
    line = jnp.zeros((NP, LANES), jnp.float32)
    for k, (left, right) in enumerate(pairs):
        line = jnp.where(lane == k, jnp.sum(jnp.sum(left * right, axis=0) * ws), line)
    face = jnp.where(even, l2[0], l2[-1])
    for k in range(sums_ref.shape[0]):
        sums_ref[k, 0] = face
        sums_ref[k, 1] = line


def relay_kernel(near_ref, out_ref):
    total = jnp.sum(near_ref[:, 1], axis=0)
    device = lax.axis_index("dom")
    count = near_ref.shape[0]
    chip = lax.rem(device // 2, count)
    face = near_ref[chip, 0]
    for k in range(out_ref.shape[0]):
        out_ref[k, 0] = face
        out_ref[k, 1] = total


def to_output(x):
    by_s = [jnp.concatenate([x[a][s : s + 1] for a in range(NP)], axis=0) for s in range(NP - 1)]
    tiles = []
    for tile in range(7):
        at = lax.broadcasted_iota(jnp.int32, (NP, LANES), 1) + tile * LANES
        element = at // 56
        s = (at - element * 56) // NP
        index = element * NP + at % NP
        value = jnp.take_along_axis(by_s[0], index, axis=1)
        for k in range(1, NP - 1):
            value = jnp.where(s == k, jnp.take_along_axis(by_s[k], index, axis=1), value)
        tiles.append(value)
    return jnp.concatenate(tiles, axis=1)


def combine_kernel(near_ref, far_ref, own_ref, w0_ref, w1_ref, p_ref, r_ref):
    device = lax.axis_index("dom")
    even = lax.rem(device, 2) == 0
    near, far = near_ref.shape[0], far_ref.shape[0]
    chips = near * far
    chip = device // 2
    partner = lax.rem(jnp.where(even, chip + chips - 1, chip + 1), chips)
    inside = partner // near == chip // near
    face = jnp.where(inside, near_ref[lax.rem(partner, near), 0], far_ref[partner // near, 0])
    local = own_ref[3]
    first = jnp.where(even, local[0] + face, local[0])
    last = jnp.where(even, local[-1], local[-1] + face)
    w2 = jnp.concatenate([first[None], local[1:-1], last[None]], axis=0)
    line = jnp.sum(far_ref[:, 1], axis=0)[:1]
    h00, h01, h02, h11, h12, h22, g0, g1, g2 = [line[:, k : k + 1] for k in range(9)]
    m1, m2 = h01 / h00, h02 / h00
    k11, k12, k22 = h11 - m1 * h01, h12 - m1 * h02, h22 - m2 * h02
    f1, f2 = g1 - m1 * g0, g2 - m2 * g0
    n2 = k12 / k11
    c2 = (f2 - n2 * f1) / (k22 - n2 * k12)
    c1 = (f1 - k12 * c2) / k11
    c0 = (g0 - h01 * c1 - h02 * c2) / h00
    pressure = (c0 + STEPS[0])[None] * own_ref[0] + (c1 + STEPS[1])[None] * own_ref[1] + c2[None] * own_ref[2]
    residual = own_ref[4] - (c0[None] * w0_ref[...] + c1[None] * w1_ref[...] + c2[None] * w2)
    p_ref[...] = to_output(pressure)
    r_ref[...] = to_output(residual)


def call(kernel, shapes, *args):
    return pl.pallas_call(
        kernel,
        out_shape=[jax.ShapeDtypeStruct(shape, jnp.float32) for shape in shapes],
        in_specs=[pl.BlockSpec(memory_space=pltpu.VMEM)] * len(args),
        out_specs=[pl.BlockSpec(memory_space=pltpu.VMEM)] * len(shapes),
        compiler_params=PARAMS,
    )(*args)


def call_forcing(*args):
    shapes = [(7 * NP, NP, LANES), (4, NP, LANES)]
    scratch = [pltpu.SMEM(args[0].shape, jnp.int32)]
    scratch.extend(pltpu.VMEM(x.shape, x.dtype) for x in args[1:])
    scratch.append(pltpu.SemaphoreType.DMA((len(args),)))
    return pl.pallas_call(
        forcing_kernel,
        out_shape=[jax.ShapeDtypeStruct(shape, jnp.float32) for shape in shapes],
        in_specs=[pl.BlockSpec(memory_space=pl.ANY)] * len(args),
        out_specs=[pl.BlockSpec(memory_space=pltpu.VMEM)] * len(shapes),
        scratch_shapes=scratch,
        compiler_params=PARAMS,
    )(*args)


def groups_of(count):
    chips = count // 2
    near = {256: 16, 16: 4, 4: 2}[chips]
    far = chips // near
    first, second = [], []
    for team in range(2):
        member = [2 * c + (team + c) % 2 for c in range(chips)]
        first.extend([member[near * i + j] for j in range(near)] for i in range(far))
        second.extend([member[near * i + (j if i % 2 == 0 else near - 1 - j)] for i in range(far)] for j in range(near))
    return near, far, first, second


def shards(velocity, conv_past, metric, jacobian, element_slot):
    count = lax.axis_size("dom")
    t = {key: jnp.asarray(value) for key, value in TAB.items()}
    field = (NP, NP, LANES)
    chip = (ROWS, NP, LANES)
    wide_shape = (WINDOW, NP, LANES)
    edge = (EDGE, NP, LANES)

    def exchange(x):
        own = swap_cross(x, count)
        return own, swap_inner(own, count)

    pack, cross = call_forcing(
        element_slot, velocity, conv_past, metric, jacobian,
        t["w3"], t["wmass"], t["ds"], t["dq"], t["jright"], t["jright_t"], t["jleft"], t["jleft_t"], t["wfine"],
    )
    (own,) = call(pair_kernel, [(7 * NP + 4, NP, LANES)], pack, swap_cross(cross, count))
    mate = swap_inner(own, count)
    div, op, level, cross = call(
        divergence_kernel,
        [chip, (2, 4) + field, (2, NP, LANES), (EDGE + 1, NP, LANES)],
        own, mate, t["ds"], t["dq"],
    )
    tables = (op, t["ds"], t["dq"], t["sleft"], t["sright"], t["srback"], t["sback"])
    wide, inv, v0, local0, cross = call(
        first_kernel,
        [wide_shape, (4 * MODES, ES * (NP + 2)), chip, chip, edge],
        div, *exchange(cross), level, t["spread"], t["lam"], *tables,
    )
    image0, wide, v1, local1, cross = call(
        functools.partial(next_kernel, STEPS[0]),
        [field, wide_shape, chip, chip, edge],
        wide, local0, *exchange(cross), inv, *tables,
    )
    near, far, first, second = groups_of(count)
    image1, own, sums = call(
        functools.partial(last_kernel, STEPS[1]),
        [field, (5,) + field, (near, 2, NP, LANES)],
        wide, local1, *exchange(cross), inv, *tables, t["ws"], v0, v1, local0,
    )
    near_sums = lax.all_to_all(sums, "dom", 0, 0, tiled=True, axis_index_groups=first)
    (sums,) = call(relay_kernel, [(far, 2, NP, LANES)], near_sums)
    far_sums = lax.all_to_all(sums, "dom", 0, 0, tiled=True, axis_index_groups=second)
    return tuple(
        call(combine_kernel, [(NP, 896), (NP, 896)], near_sums, far_sums, own, image0, image1)
    )


def solution(mesh):
    return jax.shard_map(
        shards,
        mesh=mesh,
        in_specs=(
            P(None, None, "dom", None),
            P(None, None, "dom", None),
            P(None, "dom", None),
            P("dom", None),
            P("dom"),
        ),
        out_specs=(P("dom", None), P("dom", None)),
        check_vma=False,
    )
```

```python
import functools

import jax
import jax.numpy as jnp
import numpy as np
from jax import lax
from jax.experimental import pallas as pl
from jax.experimental.pallas import tpu as pltpu
from jax.sharding import PartitionSpec as P

NP = 8
NF = 12
ES = 16
LANES = 128
time_step = 0.25
viscosity = 0.05
mass_shift = 0.001
STEPS = (0.45, 0.3)
VMEM = 48 * 1024 * 1024
ROWS = 2 * NP - 1
WINDOW = 4 * (NP - 1) + 3
EDGE = NP + 1
MODES = 112


def legendre_pair(points, order):
    before = np.ones(points.shape)
    current = points * 1.0
    for level in range(2, order + 1):
        nextone = ((2 * level - 1) * points * current - (level - 1) * before) / level
        before = current
        current = nextone
    return (current, before)


def jacobi_eigen(matrix):
    size = matrix.shape[0]
    work = matrix * 1.0
    vectors = np.eye(size)
    for sweep in range(30):
        for first in range(size - 1):
            for second in range(first + 1, size):
                off = float(work[first, second])
                if abs(off) > 1e-300:
                    tau = (float(work[second, second]) - float(work[first, first])) / (2.0 * off)
                    if tau >= 0.0:
                        tangent = 1.0 / (tau + (1.0 + tau * tau) ** 0.5)
                    else:
                        tangent = -1.0 / (-tau + (1.0 + tau * tau) ** 0.5)
                    cosine = 1.0 / (1.0 + tangent * tangent) ** 0.5
                    sine = tangent * cosine
                    rotation = np.eye(size)
                    rotation[first, first] = cosine
                    rotation[second, second] = cosine
                    rotation[first, second] = sine
                    rotation[second, first] = -sine
                    work = rotation.T @ work @ rotation
                    vectors = vectors @ rotation
    diagonal_index = np.arange(size)
    return (work[diagonal_index, diagonal_index], vectors)


def base_tables(points_edge, points_fine):
    degree = points_edge - 1
    points = -np.cos(np.pi * np.arange(points_edge) / degree)
    for sweep in range(100):
        top, below = legendre_pair(points, degree)
        points = points - (points * top - below) / (points_edge * top)
    top, below = legendre_pair(points, degree)
    weight_gll = 2.0 / (degree * points_edge * top**2)
    spacing = points[:, None] - points[None, :] + np.eye(points_edge)
    barycentric = 1.0 / np.prod(spacing, axis=1)
    derivative = barycentric[None, :] / barycentric[:, None] / spacing
    derivative = derivative * (1.0 - np.eye(points_edge))
    derivative = derivative - np.eye(points_edge) * derivative.sum(axis=1)[:, None]
    fine_points = np.cos(np.pi * (np.arange(points_fine) + 0.75) / (points_fine + 0.5))
    for sweep in range(100):
        top, below = legendre_pair(fine_points, points_fine)
        slope = points_fine * (fine_points * top - below) / (fine_points * fine_points - 1.0)
        fine_points = fine_points - top / slope
    top, below = legendre_pair(fine_points, points_fine)
    slope = points_fine * (fine_points * top - below) / (fine_points * fine_points - 1.0)
    fine_weight = 2.0 / ((1.0 - fine_points * fine_points) * slope * slope)
    fine_points = fine_points[::-1]
    fine_weight = fine_weight[::-1]
    interpolate = np.ones((points_fine, points_edge))
    for column in range(points_edge):
        for other in range(points_edge):
            if other != column:
                interpolate[:, column] = (
                    interpolate[:, column]
                    * (fine_points - points[other])
                    / (points[column] - points[other])
                )
    stiffness = derivative.T @ (weight_gll[:, None] * derivative)
    extent = 3 * degree + 1
    joined_stiff = np.zeros((extent, extent))
    joined_mass = np.zeros(extent)
    for segment in range(3):
        offset = segment * degree
        joined_stiff[offset : offset + points_edge, offset : offset + points_edge] += stiffness
        joined_mass[offset : offset + points_edge] += weight_gll
    low = degree - 1
    high = 2 * degree + 2
    root_mass = np.sqrt(joined_mass[low:high])
    scaled = joined_stiff[low:high, low:high] / root_mass[:, None] / root_mass[None, :]
    scaled = 0.5 * (scaled + scaled.T)
    eigen_values, eigen_vectors = jacobi_eigen(scaled)
    solve_mat = eigen_vectors / root_mass[:, None]
    breadth = high - low
    return dict(
        derivative=derivative,
        interpolate=interpolate,
        weight=weight_gll,
        fine_weight=fine_weight,
        solve=solve_mat,
        eigen=eigen_values,
    )


def f32(value):
    return np.ascontiguousarray(value, dtype=np.float32)


def halves(value):
    value = np.asarray(value, dtype=np.float32)
    high = value.astype(jnp.bfloat16)
    rest = (value - high.astype(np.float32)).astype(jnp.bfloat16)
    return high, rest


def for_left(value):
    high, rest = halves(value)
    return np.concatenate([high, rest, high], axis=1)


def for_right(value):
    high, rest = halves(value)
    return np.concatenate([high, rest, high], axis=0)


def pair(value):
    return np.stack(halves(value))


def make_tables():
    base = base_tables(NP, NF)
    deriv, interp, solve, eigen = base["derivative"], base["interpolate"], base["solve"], base["eigen"]
    w, wf = base["weight"], base["fine_weight"]
    out = {}
    index = np.arange(NP)

    def sublane(matrix):
        rows = [matrix[index, (index + shift) % NP] for shift in range(NP)]
        return f32(np.broadcast_to(np.stack(rows)[:, :, None], (NP, NP, LANES)))

    def lane(matrix):
        rows = []
        for shift in range(-(NP - 1), NP):
            row = np.zeros(NP)
            for q in range(NP):
                if 0 <= q + shift < NP:
                    row[q] = matrix[q, q + shift]
            rows.append(np.tile(row, ES))
        return f32(np.broadcast_to(np.stack(rows)[:, None, :], (2 * NP - 1, NP, LANES)))

    out["ds"] = np.stack([sublane(deriv), sublane(deriv.T)])
    out["dq"] = np.stack([lane(deriv), lane(deriv.T)])
    out["w3"] = f32(np.einsum("a,s,q->asq", w, w, w).reshape(1, 512))
    out["wmass"] = f32(np.tile(np.einsum("a,s,q->asq", w, w, w), (1, 1, ES)))
    both = interp @ deriv
    pad = np.zeros((16 - NF, NP))
    line = np.concatenate([interp, pad])
    slope = np.concatenate([both, pad])
    out["jright"] = for_right(np.kron(np.eye(ES), line.T))
    out["jslope"] = for_right(np.kron(np.eye(ES), slope.T))
    out["jright_t"] = pair(np.kron(np.eye(ES), line))
    out["jleft"] = for_left(np.kron(interp, interp))
    out["jleft_a"] = for_left(np.kron(both, interp))
    out["jleft_s"] = for_left(np.kron(interp, both))
    out["jleft_t"] = for_left(np.kron(interp, interp).T)
    wide_wf = np.concatenate([wf, np.zeros(16 - NF)])
    out["wfine"] = f32(np.kron(np.kron(wf, wf)[:, None], np.tile(wide_wf, ES)[None, :]))
    at = np.arange(7 * LANES)
    element, within = at // 56, at % 56
    order = np.stack([element * NP + within % NP, within // NP]).reshape(2, 7, 1, LANES)
    out["order"] = np.ascontiguousarray(np.broadcast_to(order, (2, 7, NP, LANES)), dtype=np.int32)
    wide = NP + 2
    left = np.zeros((MODES, 3, wide, NP))
    back = np.zeros((3, wide, NP, MODES))
    for i in range(wide):
        for j in range(wide):
            row = i * wide + j
            for a in range(wide):
                for s in range(NP):
                    left[row, 0, a, s] = solve[a, i] * solve[s + 1, j]
                    back[0, a, s, row] = solve[a, i] * solve[s + 1, j]
                left[row, 1, a, NP - 2] = solve[a, i] * solve[0, j]
                left[row, 2, a, 1] = solve[a, i] * solve[wide - 1, j]
                back[1, a, NP - 2, row] = solve[a, i] * solve[0, j]
                back[1, a, NP - 1, row] = solve[a, i] * solve[1, j]
                back[2, a, 1, row] = solve[a, i] * solve[wide - 1, j]
                back[2, a, 0, row] = solve[a, i] * solve[wide - 2, j]
    out["sleft"] = for_left(left.reshape(MODES, 240))
    out["sback"] = for_left(back.reshape(240, MODES))
    out["sright"] = for_right(np.kron(np.eye(ES), solve[1:-1, :]))
    out["srback"] = pair(np.kron(np.eye(ES), solve[1:-1, :].T))
    out["spread"] = f32(np.kron(np.eye(ES), np.ones((NP, wide))) / 8.0)
    lam_a = np.zeros((MODES, 1))
    lam_s = np.zeros((MODES, 1))
    lam_a[:100, 0] = np.repeat(eigen, wide)
    lam_s[:100, 0] = np.tile(eigen, wide)
    lam_q = np.tile(eigen, ES)[None, :]
    full = (MODES, ES * wide)
    out["lam"] = f32(np.stack([np.broadcast_to(lam_a, full), np.broadcast_to(lam_s, full), np.broadcast_to(lam_q, full)]))
    half = np.ones(NP)
    half[0] = half[-1] = 0.5
    out["ws"] = f32(np.broadcast_to(half[:, None], (NP, LANES)))
    return out


TAB = make_tables()
DERIV = [[float(x) for x in row] for row in base_tables(NP, NF)["derivative"].astype(np.float32)]
PARAMS = pltpu.CompilerParams(vmem_limit_bytes=VMEM)


def full_dot(left, right):
    return jnp.dot(left, right, precision=lax.Precision.HIGHEST, preferred_element_type=jnp.float32)


def short_dot(left, right):
    return jnp.dot(left, right, preferred_element_type=jnp.float32)


def split(x):
    high = x.astype(jnp.bfloat16)
    return high, (x - high.astype(jnp.float32)).astype(jnp.bfloat16)


def left_dot(table_ref, x):
    high, rest = split(x)
    return short_dot(table_ref[...], jnp.concatenate([high, high, rest], axis=0))


def right_dot(x, table_ref):
    high, rest = split(x)
    return short_dot(jnp.concatenate([high, high, rest], axis=1), table_ref[...])


def pair_dot(x, table_ref):
    high, rest = split(x)
    return short_dot(high, table_ref[0]) + (short_dot(high, table_ref[1]) + short_dot(rest, table_ref[0]))


def roll(x, shift, axis):
    return pltpu.roll(x, shift % x.shape[axis], axis)


def d_a(x, transposed):
    rows = []
    for a in range(NP):
        total = None
        for b in range(NP):
            term = (DERIV[b][a] if transposed else DERIV[a][b]) * x[b]
            total = term if total is None else total + term
        rows.append(total)
    return jnp.stack(rows)


def d_s(x, coef):
    total = coef[0][None] * x
    for shift in range(1, NP):
        total = total + coef[shift][None] * roll(x, -shift, 1)
    return total


def d_q(x, coef):
    total = coef[NP - 1][None] * x
    for shift in range(1, NP):
        total = total + coef[NP - 1 + shift][None] * roll(x, -shift, 2)
        total = total + coef[NP - 1 - shift][None] * roll(x, shift, 2)
    return total


def gradient(x, ds, dq):
    return d_a(x, False), d_s(x, ds[0]), d_q(x, dq[0])


def gradient_t(xa, xs, xq, ds, dq):
    return d_a(xa, True) + d_s(xs, ds[1]) + d_q(xq, dq[1])


def join_s(x):
    s = lax.broadcasted_iota(jnp.int32, x.shape, 1)
    from_before = roll(roll(x, NP, 2), 1, 1)
    from_after = roll(roll(x, -NP, 2), -1, 1)
    zero = jnp.zeros_like(x)
    return x + jnp.where(s == 0, from_before, jnp.where(s == NP - 1, from_after, zero))


def parity():
    return lax.rem(lax.axis_index("dom"), 2)


def swap_inner(x, count):
    return lax.ppermute(x, "dom", [(i, i ^ 1) for i in range(count)])


def swap_cross(x, count):
    pairs = [(i, (i + 1) % count if i % 2 else (i - 1) % count) for i in range(count)]
    return lax.ppermute(x, "dom", pairs)


def to_lanes(x):
    shape = (x.shape[0], NP, LANES)
    lane = lax.broadcasted_iota(jnp.int32, shape, 2)
    pieces = []
    for tile in range(4):
        first = x[:, :8, tile * LANES : (tile + 1) * LANES]
        second = x[:, 8:, tile * LANES : (tile + 1) * LANES]
        pieces.append(jnp.where(lane < 64, first, roll(second, 64, 2)))
        pieces.append(jnp.where(lane < 64, roll(first, 64, 2), second))
    y = jnp.stack(pieces, axis=1).reshape(x.shape[0] * NP, NP, LANES)
    sub = lax.broadcasted_iota(jnp.int32, y.shape, 1)
    lane = lax.broadcasted_iota(jnp.int32, y.shape, 2)
    for bit in range(3):
        step = 1 << bit
        in_sub = (sub & step) != 0
        in_lane = (lane & (step * 8)) != 0
        up = roll(roll(y, -step, 1), step * 8, 2)
        down = roll(roll(y, step, 1), -step * 8, 2)
        y = jnp.where(in_sub == in_lane, y, jnp.where(in_lane, up, down))
    return y.reshape(x.shape[0], NP, NP, LANES)


def rows(x):
    return x.reshape(NP * NP, LANES)


def planes(x):
    return x.reshape(NP, NP, LANES)


def take_lanes(x, index):
    flat = x.reshape(-1, LANES)
    tiled = jnp.broadcast_to(index[None], x.shape).reshape(-1, LANES)
    return jnp.take_along_axis(flat, tiled, axis=1).reshape(x.shape)


def forcing_kernel(slot_in, vel_in, past_in, metric_in, jac_in, w3_in, wmass_in, ds_in, dq_in, jright_in, jslope_in, jright_t_in, jleft_in, jleft_a_in, jleft_s_in, jleft_t_in, wfine_in, pack_ref, cross_ref, slot_ref, vel_ref, past_ref, metric_ref, jac_ref, w3_ref, wmass_ref, ds_ref, dq_ref, jright_ref, jslope_ref, jright_t_ref, jleft_ref, jleft_a_ref, jleft_s_ref, jleft_t_ref, wfine_ref, sems):
    sources = (slot_in, vel_in, past_in, metric_in, jac_in, w3_in, wmass_in, ds_in, dq_in, jright_in, jslope_in, jright_t_in, jleft_in, jleft_a_in, jleft_s_in, jleft_t_in, wfine_in)
    targets = (slot_ref, vel_ref, past_ref, metric_ref, jac_ref, w3_ref, wmass_ref, ds_ref, dq_ref, jright_ref, jslope_ref, jright_t_ref, jleft_ref, jleft_a_ref, jleft_s_ref, jleft_t_ref, wfine_ref)
    copies = [pltpu.make_async_copy(x, y, sems.at[k]) for k, (x, y) in enumerate(zip(sources, targets))]
    for copy in copies:
        copy.start()
    for copy in copies:
        copy.wait()
    even = parity() == 0
    ds, dq = ds_ref[...], dq_ref[...]
    jac = jac_ref[...]
    new, mid, old = vel_ref[0], vel_ref[1], vel_ref[2]
    guess = 3.0 * (new - mid) + old
    direct = (jac * w3_ref[...])[None] * (-10.0 * new + 16.0 * mid - 6.0 * old) + 3.0 * past_ref[0] - past_ref[1]
    lanes = to_lanes(jnp.concatenate([new, guess, direct, metric_ref[...], jac[None]], axis=0))
    new, guess, direct, metric, jac = lanes[0:3], lanes[3:6], lanes[6:9], lanes[9:12], lanes[12]
    moved = [rows(new[i]) for i in range(3)]
    plain = moved + [rows(jac)] + [rows(new[d] * metric[d]) for d in range(3)]
    wide = right_dot(jnp.concatenate(plain, axis=0), jright_ref)
    slope = right_dot(jnp.concatenate(moved, axis=0), jslope_ref)
    scale = left_dot(jleft_ref, wide[192:256]) * wfine_ref[...]
    carry = [left_dot(jleft_ref, wide[256 + 64 * d : 320 + 64 * d]) for d in range(3)]
    products = []
    for i in range(3):
        part = wide[64 * i : 64 * i + 64]
        total = carry[0] * left_dot(jleft_a_ref, part) + carry[1] * left_dot(jleft_s_ref, part)
        total = total + carry[2] * left_dot(jleft_ref, slope[64 * i : 64 * i + 64])
        products.append(scale * total)
    coarse = left_dot(jleft_t_ref, jnp.concatenate(products, axis=1))
    coarse = pair_dot(jnp.concatenate([coarse[:, 256 * i : 256 * i + 256] for i in range(3)], axis=0), jright_t_ref)
    mass = jac * wmass_ref[...]
    factor = [mass * metric[d] * metric[d] for d in range(3)]
    result = []
    for i in range(3):
        ga, gs, gq = gradient(guess[i], ds, dq)
        stiff = gradient_t(factor[0] * ga, factor[1] * gs, factor[2] * gq, ds, dq)
        result.append(direct[i] - 3.0 * planes(coarse[64 * i : 64 * i + 64]) - viscosity * stiff)
    result.extend([mass, metric[0], metric[1], metric[2]])
    lane = lax.broadcasted_iota(jnp.int32, (NP, LANES), 1)
    index = jnp.zeros((NP, LANES), jnp.int32)
    for e in range(ES):
        index = jnp.where((lane >> 3) == slot_ref[e], e * NP, index)
    index = index + (lane & 7)
    result = [take_lanes(x, index) for x in result]
    for k in range(4):
        joined = join_s(result[k])
        cross_ref[k] = jnp.where(even, joined[0], joined[NP - 1])
        pack_ref[NP * k : NP * k + NP] = joined if k < 3 else result[k]
    for k in range(4, 7):
        pack_ref[NP * k : NP * k + NP] = result[k]


def pair_kernel(pack_ref, cross_in, out_ref):
    out_ref[: 7 * NP] = pack_ref[...]
    out_ref[7 * NP :] = cross_in[...]


def chip_rows(first, second):
    return jnp.concatenate([first[:-1], (first[-1] + second[0])[None], second[1:]], axis=0)


def own_rows(even, x):
    return jnp.where(even, x[:NP], x[NP - 1 :])


def edge_rows(even, x):
    return jnp.where(even, x[:EDGE], x[ROWS - EDGE :])


def divergence_kernel(own_ref, mate_ref, ds_ref, dq_ref, div_ref, op_ref, level_ref, cross_ref):
    even = parity() == 0
    own, mate = own_ref[...], mate_ref[...]
    packs = [jnp.where(even, own, mate), jnp.where(even, mate, own)]
    parts = [[pack[NP * k : NP * k + NP] for k in range(7)] for pack in packs]
    low, high = packs[0][7 * NP :], packs[1][7 * NP :]
    sides = []
    for k in range(4):
        first, second = parts[0][k], parts[1][k]
        if k == 3:
            first, second = join_s(first), join_s(second)
        whole = chip_rows(first, second)
        sides.append(jnp.concatenate([(whole[0] + low[k])[None], whole[1:-1], (whole[-1] + high[k])[None]], axis=0))
    inv = 1.0 / sides[3]
    accel = [sides[d] * inv for d in range(3)]
    div = []
    levels = []
    for layer in range(2):
        mass = parts[layer][3]
        at = (NP - 1) * layer
        sums = []
        terms = []
        for d in range(3):
            one = mass * parts[layer][4 + d]
            two = one * parts[layer][4 + d]
            op_ref[layer, d] = two
            sums.append(jnp.sum(rows(two), axis=0, keepdims=True))
            terms.append(one * accel[d][at : at + NP])
        op_ref[layer, 3] = mass_shift * mass
        sums.append(jnp.sum(rows(mass), axis=0, keepdims=True))
        sums.append(jnp.zeros((4, LANES), jnp.float32))
        levels.append(jnp.concatenate(sums, axis=0))
        level_ref[layer] = levels[layer]
        div.append(join_s(gradient_t(terms[0], terms[1], terms[2], ds_ref[...], dq_ref[...])))
    whole = chip_rows(div[0], div[1])
    div_ref[...] = whole
    cross_ref[:EDGE] = edge_rows(even, whole)
    cross_ref[EDGE] = jnp.where(even, levels[0], levels[1])


def window(local, low, high):
    return jnp.concatenate(
        [low[: EDGE - 1], (low[EDGE - 1] + local[0])[None], local[1:-1], (local[-1] + high[0])[None], high[1:EDGE]],
        axis=0,
    )


def inverse_levels(levels, spread_ref, lam_ref):
    result = []
    for level in levels:
        level = full_dot(level, spread_ref[...])
        denom = level[0:1] * lam_ref[0] + level[1:2] * lam_ref[1] + level[2:3] * lam_ref[2] + mass_shift * level[3:4]
        result.append(1.0 / denom)
    return result


def schwarz(wide, inv_ref, sleft_ref, sright_ref, srback_ref, sback_ref):
    before, after = roll(wide, NP, 2), roll(wide, -NP, 2)
    columns = []
    for layer in range(4):
        at = (NP - 1) * layer
        columns.append(jnp.concatenate([x[at : at + NP + 2].reshape(80, LANES) for x in (wide, before, after)], axis=0))
    spectra = left_dot(sleft_ref, jnp.concatenate(columns, axis=1))
    spectra = jnp.concatenate([spectra[:, LANES * k : LANES * k + LANES] for k in range(4)], axis=0)
    spectra = pair_dot(right_dot(spectra, sright_ref) * inv_ref[...], srback_ref)
    spectra = jnp.concatenate([spectra[MODES * k : MODES * k + MODES] for k in range(4)], axis=1)
    blocks = left_dot(sback_ref, spectra)
    z = []
    for layer in range(4):
        part = blocks[:, LANES * layer : LANES * layer + LANES]
        part = part[:80] + roll(part[80:160], -NP, 1) + roll(part[160:], NP, 1)
        z.append(part.reshape(NP + 2, NP, LANES))
    middle = jnp.concatenate([z[1][1:8], (z[1][8] + z[2][1])[None], z[2][2:9]], axis=0)
    first = jnp.concatenate([z[0][8:10], jnp.zeros((4, NP, LANES), jnp.float32), z[2][0:1], jnp.zeros((1, NP, LANES), jnp.float32), z[1][9:10], jnp.zeros((4, NP, LANES), jnp.float32), z[3][0:2]], axis=0)
    return middle + first


def operate(v, op_ref, ds_ref, dq_ref):
    ds, dq = ds_ref[...], dq_ref[...]
    parts = []
    for layer in range(2):
        x = v[(NP - 1) * layer : (NP - 1) * layer + NP]
        ga, gs, gq = gradient(x, ds, dq)
        local = gradient_t(op_ref[layer, 0] * ga, op_ref[layer, 1] * gs, op_ref[layer, 2] * gq, ds, dq)
        parts.append(join_s(local + op_ref[layer, 3] * x))
    return chip_rows(parts[0], parts[1])


def sides_of(even, own_in, mate_in):
    own, mate = own_in[...], mate_in[...]
    return jnp.where(even, own, mate), jnp.where(even, mate, own)


def first_kernel(div_ref, own_in, mate_in, level_ref, spread_ref, lam_ref, op_ref, ds_ref, dq_ref, sleft_ref, sright_ref, srback_ref, sback_ref, wide_ref, inv_ref, v_ref, local_ref, cross_ref):
    even = parity() == 0
    low, high = sides_of(even, own_in, mate_in)
    wide = window(div_ref[...], low, high)
    wide_ref[...] = wide
    for k, inv in enumerate(inverse_levels([low[EDGE], level_ref[0], level_ref[1], high[EDGE]], spread_ref, lam_ref)):
        inv_ref[MODES * k : MODES * k + MODES] = inv
    v = schwarz(wide, inv_ref, sleft_ref, sright_ref, srback_ref, sback_ref)
    v_ref[...] = v
    local = operate(v, op_ref, ds_ref, dq_ref)
    local_ref[...] = local
    cross_ref[...] = edge_rows(even, local)


def next_kernel(step, before_ref, image_ref, own_in, mate_in, inv_ref, op_ref, ds_ref, dq_ref, sleft_ref, sright_ref, srback_ref, sback_ref, own_image_ref, wide_ref, v_ref, local_ref, cross_ref):
    even = parity() == 0
    low, high = sides_of(even, own_in, mate_in)
    image = window(image_ref[...], low, high)
    own_image_ref[...] = own_rows(even, image[NP : NP + ROWS])
    wide = before_ref[...] - step * image
    wide_ref[...] = wide
    v = schwarz(wide, inv_ref, sleft_ref, sright_ref, srback_ref, sback_ref)
    v_ref[...] = v
    local = operate(v, op_ref, ds_ref, dq_ref)
    local_ref[...] = local
    cross_ref[...] = edge_rows(even, local)


def last_kernel(step, before_ref, image_ref, own_in, mate_in, inv_ref, op_ref, ds_ref, dq_ref, sleft_ref, sright_ref, srback_ref, sback_ref, ws_ref, v0_ref, v1_ref, l0_ref, own_image_ref, own_ref, sums_ref):
    even = parity() == 0
    low, high = sides_of(even, own_in, mate_in)
    image = window(image_ref[...], low, high)
    own_image_ref[...] = own_rows(even, image[NP : NP + ROWS])
    residual = before_ref[NP : NP + ROWS] - step * image[NP : NP + ROWS]
    wide = before_ref[...] - step * image
    v2 = schwarz(wide, inv_ref, sleft_ref, sright_ref, srback_ref, sback_ref)
    l2 = operate(v2, op_ref, ds_ref, dq_ref)
    v = [v0_ref[...], v1_ref[...], v2]
    images = [l0_ref[...], image_ref[...], l2]
    for k, x in enumerate((v[0], v[1], v2, l2, residual)):
        own_ref[k] = own_rows(even, x)
    weighted = jnp.concatenate([0.5 * residual[:1], residual[1:-1], 0.5 * residual[-1:]], axis=0)
    ws = ws_ref[...]
    pairs = [(v[i], images[j]) for i, j in ((0, 0), (0, 1), (0, 2), (1, 1), (1, 2), (2, 2))]
    pairs.extend((v[i], weighted) for i in range(3))
    lane = lax.broadcasted_iota(jnp.int32, (NP, LANES), 1)
    line = jnp.zeros((NP, LANES), jnp.float32)
    for k, (left, right) in enumerate(pairs):
        line = jnp.where(lane == k, jnp.sum(jnp.sum(left * right, axis=0) * ws), line)
    put_sums(sums_ref, jnp.where(even, l2[0], l2[-1]), line)


def put_sums(sums_ref, face, line):
    sub = lax.broadcasted_iota(jnp.int32, (NP, LANES), 0)
    value = jnp.where(sub == NP - 1, line, face)
    for k in range(sums_ref.shape[0]):
        sums_ref[k] = value


def relay_kernel(near_ref, out_ref):
    count = near_ref.shape[0]
    chip = lax.rem(lax.axis_index("dom") // 2, count)
    put_sums(out_ref, near_ref[chip], jnp.sum(near_ref[...], axis=0))


def to_output(x, order_ref, scratch_ref):
    scratch_ref[...] = rows(x)
    by_s = [scratch_ref[pl.ds(s, NP, stride=NP), :] for s in range(NP - 1)]
    tiles = []
    for tile in range(7):
        index, s = order_ref[0, tile], order_ref[1, tile]
        value = jnp.take_along_axis(by_s[0], index, axis=1)
        for k in range(1, NP - 1):
            value = jnp.where(s == k, jnp.take_along_axis(by_s[k], index, axis=1), value)
        tiles.append(value)
    return jnp.concatenate(tiles, axis=1)


def combine_kernel(near_ref, far_ref, own_ref, w0_ref, w1_ref, order_ref, p_ref, r_ref, first_ref, second_ref):
    device = lax.axis_index("dom")
    even = lax.rem(device, 2) == 0
    near, far = near_ref.shape[0], far_ref.shape[0]
    chips = near * far
    chip = device // 2
    partner = lax.rem(jnp.where(even, chip + chips - 1, chip + 1), chips)
    inside = partner // near == chip // near
    face = jnp.where(inside, near_ref[lax.rem(partner, near)], far_ref[partner // near])
    local = own_ref[3]
    first = jnp.where(even, local[0] + face, local[0])
    last = jnp.where(even, local[-1], local[-1] + face)
    w2 = jnp.concatenate([first[None], local[1:-1], last[None]], axis=0)
    line = jnp.sum(far_ref[...], axis=0)[NP - 1 :]
    h00, h01, h02, h11, h12, h22, g0, g1, g2 = [line[:, k : k + 1] for k in range(9)]
    m1, m2 = h01 / h00, h02 / h00
    k11, k12, k22 = h11 - m1 * h01, h12 - m1 * h02, h22 - m2 * h02
    f1, f2 = g1 - m1 * g0, g2 - m2 * g0
    n2 = k12 / k11
    c2 = (f2 - n2 * f1) / (k22 - n2 * k12)
    c1 = (f1 - k12 * c2) / k11
    c0 = (g0 - h01 * c1 - h02 * c2) / h00
    pressure = (c0 + STEPS[0])[None] * own_ref[0] + (c1 + STEPS[1])[None] * own_ref[1] + c2[None] * own_ref[2]
    residual = own_ref[4] - (c0[None] * w0_ref[...] + c1[None] * w1_ref[...] + c2[None] * w2)
    p_ref[...] = to_output(pressure, order_ref, first_ref)
    r_ref[...] = to_output(residual, order_ref, second_ref)


def call(kernel, shapes, *args, scratch=()):
    return pl.pallas_call(
        kernel,
        out_shape=[jax.ShapeDtypeStruct(shape, jnp.float32) for shape in shapes],
        in_specs=[pl.BlockSpec(memory_space=pltpu.VMEM)] * len(args),
        out_specs=[pl.BlockSpec(memory_space=pltpu.VMEM)] * len(shapes),
        scratch_shapes=scratch,
        compiler_params=PARAMS,
    )(*args)


def call_forcing(*args):
    shapes = [(7 * NP, NP, LANES), (4, NP, LANES)]
    scratch = [pltpu.SMEM(args[0].shape, jnp.int32)]
    scratch.extend(pltpu.VMEM(x.shape, x.dtype) for x in args[1:])
    scratch.append(pltpu.SemaphoreType.DMA((len(args),)))
    return pl.pallas_call(
        forcing_kernel,
        out_shape=[jax.ShapeDtypeStruct(shape, jnp.float32) for shape in shapes],
        in_specs=[pl.BlockSpec(memory_space=pltpu.HBM)] * len(args),
        out_specs=[pl.BlockSpec(memory_space=pltpu.VMEM)] * len(shapes),
        scratch_shapes=scratch,
        compiler_params=PARAMS,
    )(*args)


FORCING_TABLES = ("w3", "wmass", "ds", "dq", "jright", "jslope", "jright_t", "jleft", "jleft_a", "jleft_s", "jleft_t", "wfine")


def groups_of(count):
    chips = count // 2
    near = {256: 16, 16: 4, 4: 2}[chips]
    far = chips // near
    first, second = [], []
    for team in range(2):
        member = [2 * c + (team + c) % 2 for c in range(chips)]
        first.extend([member[near * i + j] for j in range(near)] for i in range(far))
        for j in range(near):
            turned = near - 1 - j if j in (0, near - 1) else j
            second.append([member[near * i + (turned if i % 2 else j)] for i in range(far)])
    return near, far, first, second


def shards(velocity, conv_past, metric, jacobian, element_slot):
    count = lax.axis_size("dom")
    t = {key: jnp.asarray(value) for key, value in TAB.items()}
    field = (NP, NP, LANES)
    chip = (ROWS, NP, LANES)
    wide_shape = (WINDOW, NP, LANES)
    edge = (EDGE, NP, LANES)

    def exchange(x):
        own = swap_cross(x, count)
        return own, swap_inner(own, count)

    pack, cross = call_forcing(
        element_slot, velocity, conv_past, metric, jacobian,
        *(t[key] for key in FORCING_TABLES),
    )
    (own,) = call(pair_kernel, [(7 * NP + 4, NP, LANES)], pack, swap_cross(cross, count))
    mate = swap_inner(own, count)
    div, op, level, cross = call(
        divergence_kernel,
        [chip, (2, 4) + field, (2, NP, LANES), (EDGE + 1, NP, LANES)],
        own, mate, t["ds"], t["dq"],
    )
    tables = (op, t["ds"], t["dq"], t["sleft"], t["sright"], t["srback"], t["sback"])
    wide, inv, v0, local0, cross = call(
        first_kernel,
        [wide_shape, (4 * MODES, ES * (NP + 2)), chip, chip, edge],
        div, *exchange(cross), level, t["spread"], t["lam"], *tables,
    )
    image0, wide, v1, local1, cross = call(
        functools.partial(next_kernel, STEPS[0]),
        [field, wide_shape, chip, chip, edge],
        wide, local0, *exchange(cross), inv, *tables,
    )
    near, far, first, second = groups_of(count)
    image1, own, sums = call(
        functools.partial(last_kernel, STEPS[1]),
        [field, (5,) + field, (near, NP, LANES)],
        wide, local1, *exchange(cross), inv, *tables, t["ws"], v0, v1, local0,
    )
    near_sums = lax.all_to_all(sums, "dom", 0, 0, tiled=True, axis_index_groups=first)
    (sums,) = call(relay_kernel, [(far, NP, LANES)], near_sums)
    far_sums = lax.all_to_all(sums, "dom", 0, 0, tiled=True, axis_index_groups=second)
    return tuple(
        call(
            combine_kernel,
            [(NP, 896), (NP, 896)],
            near_sums, far_sums, own, image0, image1, t["order"],
            scratch=[pltpu.VMEM((NP * NP, LANES), jnp.float32)] * 2,
        )
    )


def solution(mesh):
    return jax.shard_map(
        shards,
        mesh=mesh,
        in_specs=(
            P(None, None, "dom", None),
            P(None, None, "dom", None),
            P(None, "dom", None),
            P("dom", None),
            P("dom"),
        ),
        out_specs=(P("dom", None), P("dom", None)),
        check_vma=False,
    )
```

```python
import functools

import jax
import jax.numpy as jnp
import numpy as np
from jax import lax
from jax.experimental import pallas as pl
from jax.experimental.pallas import tpu as pltpu
from jax.sharding import PartitionSpec as P

NP = 8
NF = 12
ES = 16
LANES = 128
time_step = 0.25
viscosity = 0.05
mass_shift = 0.001
STEPS = (0.45, 0.3)
VMEM = 48 * 1024 * 1024
FORCING_VMEM = 56 * 1024 * 1024
ROWS = 2 * NP - 1
EDGE = NP + 1
MODES = 112


def legendre_pair(points, order):
    before = np.ones(points.shape)
    current = points * 1.0
    for level in range(2, order + 1):
        nextone = ((2 * level - 1) * points * current - (level - 1) * before) / level
        before = current
        current = nextone
    return (current, before)


def jacobi_eigen(matrix):
    size = matrix.shape[0]
    work = matrix * 1.0
    vectors = np.eye(size)
    for sweep in range(30):
        for first in range(size - 1):
            for second in range(first + 1, size):
                off = float(work[first, second])
                if abs(off) > 1e-300:
                    tau = (float(work[second, second]) - float(work[first, first])) / (2.0 * off)
                    if tau >= 0.0:
                        tangent = 1.0 / (tau + (1.0 + tau * tau) ** 0.5)
                    else:
                        tangent = -1.0 / (-tau + (1.0 + tau * tau) ** 0.5)
                    cosine = 1.0 / (1.0 + tangent * tangent) ** 0.5
                    sine = tangent * cosine
                    rotation = np.eye(size)
                    rotation[first, first] = cosine
                    rotation[second, second] = cosine
                    rotation[first, second] = sine
                    rotation[second, first] = -sine
                    work = rotation.T @ work @ rotation
                    vectors = vectors @ rotation
    diagonal_index = np.arange(size)
    return (work[diagonal_index, diagonal_index], vectors)


def base_tables(points_edge, points_fine):
    degree = points_edge - 1
    points = -np.cos(np.pi * np.arange(points_edge) / degree)
    for sweep in range(100):
        top, below = legendre_pair(points, degree)
        points = points - (points * top - below) / (points_edge * top)
    top, below = legendre_pair(points, degree)
    weight_gll = 2.0 / (degree * points_edge * top**2)
    spacing = points[:, None] - points[None, :] + np.eye(points_edge)
    barycentric = 1.0 / np.prod(spacing, axis=1)
    derivative = barycentric[None, :] / barycentric[:, None] / spacing
    derivative = derivative * (1.0 - np.eye(points_edge))
    derivative = derivative - np.eye(points_edge) * derivative.sum(axis=1)[:, None]
    fine_points = np.cos(np.pi * (np.arange(points_fine) + 0.75) / (points_fine + 0.5))
    for sweep in range(100):
        top, below = legendre_pair(fine_points, points_fine)
        slope = points_fine * (fine_points * top - below) / (fine_points * fine_points - 1.0)
        fine_points = fine_points - top / slope
    top, below = legendre_pair(fine_points, points_fine)
    slope = points_fine * (fine_points * top - below) / (fine_points * fine_points - 1.0)
    fine_weight = 2.0 / ((1.0 - fine_points * fine_points) * slope * slope)
    fine_points = fine_points[::-1]
    fine_weight = fine_weight[::-1]
    interpolate = np.ones((points_fine, points_edge))
    for column in range(points_edge):
        for other in range(points_edge):
            if other != column:
                interpolate[:, column] = (
                    interpolate[:, column]
                    * (fine_points - points[other])
                    / (points[column] - points[other])
                )
    stiffness = derivative.T @ (weight_gll[:, None] * derivative)
    extent = 3 * degree + 1
    joined_stiff = np.zeros((extent, extent))
    joined_mass = np.zeros(extent)
    for segment in range(3):
        offset = segment * degree
        joined_stiff[offset : offset + points_edge, offset : offset + points_edge] += stiffness
        joined_mass[offset : offset + points_edge] += weight_gll
    low = degree - 1
    high = 2 * degree + 2
    root_mass = np.sqrt(joined_mass[low:high])
    scaled = joined_stiff[low:high, low:high] / root_mass[:, None] / root_mass[None, :]
    scaled = 0.5 * (scaled + scaled.T)
    eigen_values, eigen_vectors = jacobi_eigen(scaled)
    solve_mat = eigen_vectors / root_mass[:, None]
    breadth = high - low
    return dict(
        derivative=derivative,
        interpolate=interpolate,
        weight=weight_gll,
        fine_weight=fine_weight,
        solve=solve_mat,
        eigen=eigen_values,
    )


def f32(value):
    return np.ascontiguousarray(value, dtype=np.float32)


def halves(value):
    value = np.asarray(value, dtype=np.float32)
    high = value.astype(jnp.bfloat16)
    rest = (value - high.astype(np.float32)).astype(jnp.bfloat16)
    return high, rest


def for_left(value):
    high, rest = halves(value)
    return np.concatenate([high, rest, high], axis=1)


def for_right(value):
    high, rest = halves(value)
    return np.concatenate([high, rest, high], axis=0)


def pair(value):
    return np.stack(halves(value))


def make_tables():
    base = base_tables(NP, NF)
    deriv, interp, solve, eigen = base["derivative"], base["interpolate"], base["solve"], base["eigen"]
    w, wf = base["weight"], base["fine_weight"]
    out = {}
    index = np.arange(NP)

    def sublane(matrix):
        rows = [matrix[index, (index + shift) % NP] for shift in range(NP)]
        return f32(np.broadcast_to(np.stack(rows)[:, :, None], (NP, NP, LANES)))

    def lane(matrix):
        rows = []
        for shift in range(-(NP - 1), NP):
            row = np.zeros(NP)
            for q in range(NP):
                if 0 <= q + shift < NP:
                    row[q] = matrix[q, q + shift]
            rows.append(np.tile(row, ES))
        return f32(np.broadcast_to(np.stack(rows)[:, None, :], (2 * NP - 1, NP, LANES)))

    out["ds"] = np.stack([sublane(deriv), sublane(deriv.T)])
    out["dq"] = np.stack([lane(deriv), lane(deriv.T)])
    out["qright"] = for_right(np.kron(np.eye(ES), deriv.T))
    out["qright_t"] = for_right(np.kron(np.eye(ES), deriv))
    out["w3"] = f32(np.einsum("a,s,q->asq", w, w, w).reshape(1, 512))
    out["wmass"] = f32(np.tile(np.einsum("a,s,q->asq", w, w, w), (1, 1, ES)))
    both = interp @ deriv
    pad = np.zeros((16 - NF, NP))
    line = np.concatenate([interp, pad])
    slope = np.concatenate([both, pad])
    out["jright"] = for_right(np.kron(np.eye(ES), line.T))
    out["jslope"] = for_right(np.kron(np.eye(ES), slope.T))
    out["jright_t"] = pair(np.kron(np.eye(ES), line))
    out["jleft"] = for_left(np.kron(interp, interp))
    out["jleft_a"] = for_left(np.kron(both, interp))
    out["jleft_s"] = for_left(np.kron(interp, both))
    out["jleft_t"] = for_left(np.kron(interp, interp).T)
    wide_wf = np.concatenate([wf, np.zeros(16 - NF)])
    out["wfine"] = f32(np.kron(np.kron(wf, wf)[:, None], np.tile(wide_wf, ES)[None, :]))
    at = np.arange(7 * LANES)
    element, within = at // 56, at % 56
    order = np.stack([element * NP + within % NP, within // NP]).reshape(2, 7, 1, LANES)
    out["order"] = np.ascontiguousarray(np.broadcast_to(order, (2, 7, NP, LANES)), dtype=np.int32)
    wide = NP + 2
    left = np.zeros((MODES, 3, wide, NP))
    back = np.zeros((3, wide, NP, MODES))
    for i in range(wide):
        for j in range(wide):
            row = i * wide + j
            for a in range(wide):
                for s in range(NP):
                    left[row, 0, a, s] = solve[a, i] * solve[s + 1, j]
                    back[0, a, s, row] = solve[a, i] * solve[s + 1, j]
                left[row, 1, a, NP - 2] = solve[a, i] * solve[0, j]
                left[row, 2, a, 1] = solve[a, i] * solve[wide - 1, j]
                back[1, a, NP - 2, row] = solve[a, i] * solve[0, j]
                back[1, a, NP - 1, row] = solve[a, i] * solve[1, j]
                back[2, a, 1, row] = solve[a, i] * solve[wide - 1, j]
                back[2, a, 0, row] = solve[a, i] * solve[wide - 2, j]
    out["sleft"] = for_left(left.reshape(MODES, 240))
    out["sback"] = for_left(back.reshape(240, MODES))
    out["sright"] = for_right(np.kron(np.eye(ES), solve[1:-1, :]))
    out["srback"] = pair(np.kron(np.eye(ES), solve[1:-1, :].T))
    out["spread"] = f32(np.kron(np.eye(ES), np.ones((NP, wide))) / 8.0)
    lam_a = np.zeros((MODES, 1))
    lam_s = np.zeros((MODES, 1))
    lam_a[:100, 0] = np.repeat(eigen, wide)
    lam_s[:100, 0] = np.tile(eigen, wide)
    lam_q = np.tile(eigen, ES)[None, :]
    full = (MODES, ES * wide)
    out["lam"] = f32(np.stack([np.broadcast_to(lam_a, full), np.broadcast_to(lam_s, full), np.broadcast_to(lam_q, full)]))
    half = np.ones(NP)
    half[0] = half[-1] = 0.5
    out["ws"] = f32(np.broadcast_to(half[:, None], (NP, LANES)))
    return out


TAB = make_tables()
DERIV = [[float(x) for x in row] for row in base_tables(NP, NF)["derivative"].astype(np.float32)]
PARAMS = pltpu.CompilerParams(vmem_limit_bytes=VMEM)


def full_dot(left, right):
    return jnp.dot(left, right, precision=lax.Precision.HIGHEST, preferred_element_type=jnp.float32)


def short_dot(left, right):
    return jnp.dot(left, right, preferred_element_type=jnp.float32)


def split(x):
    high = x.astype(jnp.bfloat16)
    return high, (x - high.astype(jnp.float32)).astype(jnp.bfloat16)


def left_dot(table_ref, x):
    high, rest = split(x)
    return short_dot(table_ref[...], jnp.concatenate([high, high, rest], axis=0))


def right_dot(x, table_ref):
    high, rest = split(x)
    return short_dot(jnp.concatenate([high, high, rest], axis=1), table_ref[...])


def pair_dot(x, table_ref):
    high, rest = split(x)
    return short_dot(high, table_ref[0]) + (short_dot(high, table_ref[1]) + short_dot(rest, table_ref[0]))


def roll(x, shift, axis):
    return pltpu.roll(x, shift % x.shape[axis], axis)


def d_a(x, transposed):
    rows = []
    for a in range(NP):
        total = None
        for b in range(NP):
            term = (DERIV[b][a] if transposed else DERIV[a][b]) * x[b]
            total = term if total is None else total + term
        rows.append(total)
    return jnp.stack(rows)


def d_s(x, coef):
    total = coef[0][None] * x
    for shift in range(1, NP):
        total = total + coef[shift][None] * roll(x, -shift, 1)
    return total


def d_q(x, coef):
    total = coef[NP - 1][None] * x
    for shift in range(1, NP):
        total = total + coef[NP - 1 + shift][None] * roll(x, -shift, 2)
        total = total + coef[NP - 1 - shift][None] * roll(x, shift, 2)
    return total


def gradient(x, ds, dq):
    return d_a(x, False), d_s(x, ds[0]), d_q(x, dq[0])


def gradient_t(xa, xs, xq, ds, dq):
    return d_a(xa, True) + d_s(xs, ds[1]) + d_q(xq, dq[1])


def join_s(x):
    s = lax.broadcasted_iota(jnp.int32, x.shape, 1)
    from_before = roll(roll(x, NP, 2), 1, 1)
    from_after = roll(roll(x, -NP, 2), -1, 1)
    zero = jnp.zeros_like(x)
    return x + jnp.where(s == 0, from_before, jnp.where(s == NP - 1, from_after, zero))


def parity():
    return lax.rem(lax.axis_index("dom"), 2)


def swap_inner(x, count):
    return lax.ppermute(x, "dom", [(i, i ^ 1) for i in range(count)])


def swap_cross(x, count):
    pairs = [(i, (i + 1) % count if i % 2 else (i - 1) % count) for i in range(count)]
    return lax.ppermute(x, "dom", pairs)


def to_lanes(x):
    shape = (x.shape[0], NP, LANES)
    lane = lax.broadcasted_iota(jnp.int32, shape, 2)
    pieces = []
    for tile in range(4):
        first = x[:, :8, tile * LANES : (tile + 1) * LANES]
        second = x[:, 8:, tile * LANES : (tile + 1) * LANES]
        pieces.append(jnp.where(lane < 64, first, roll(second, 64, 2)))
        pieces.append(jnp.where(lane < 64, roll(first, 64, 2), second))
    y = jnp.stack(pieces, axis=1).reshape(x.shape[0] * NP, NP, LANES)
    sub = lax.broadcasted_iota(jnp.int32, y.shape, 1)
    lane = lax.broadcasted_iota(jnp.int32, y.shape, 2)
    for bit in range(3):
        step = 1 << bit
        in_sub = (sub & step) != 0
        in_lane = (lane & (step * 8)) != 0
        up = roll(roll(y, -step, 1), step * 8, 2)
        down = roll(roll(y, step, 1), -step * 8, 2)
        y = jnp.where(in_sub == in_lane, y, jnp.where(in_lane, up, down))
    return y.reshape(x.shape[0], NP, NP, LANES)


def rows(x):
    return x.reshape(NP * NP, LANES)


def planes(x):
    return x.reshape(NP, NP, LANES)


def take_lanes(x, index):
    flat = x.reshape(-1, LANES)
    tiled = jnp.broadcast_to(index[None], x.shape).reshape(-1, LANES)
    return jnp.take_along_axis(flat, tiled, axis=1).reshape(x.shape)


def forcing_kernel(slot_in, vel_in, past_in, metric_in, jac_in, w3_in, wmass_in, ds_in, dq_in, jright_in, jslope_in, jright_t_in, jleft_in, jleft_a_in, jleft_s_in, jleft_t_in, wfine_in, pack_ref, cross_ref, slot_ref, vel_ref, past_ref, metric_ref, jac_ref, w3_ref, wmass_ref, ds_ref, dq_ref, jright_ref, jslope_ref, jright_t_ref, jleft_ref, jleft_a_ref, jleft_s_ref, jleft_t_ref, wfine_ref, sems):
    sources = (slot_in, vel_in, past_in, metric_in, jac_in, w3_in, wmass_in, ds_in, dq_in, jright_in, jslope_in, jright_t_in, jleft_in, jleft_a_in, jleft_s_in, jleft_t_in, wfine_in)
    targets = (slot_ref, vel_ref, past_ref, metric_ref, jac_ref, w3_ref, wmass_ref, ds_ref, dq_ref, jright_ref, jslope_ref, jright_t_ref, jleft_ref, jleft_a_ref, jleft_s_ref, jleft_t_ref, wfine_ref)
    copies = [pltpu.make_async_copy(x, y, sems.at[k]) for k, (x, y) in enumerate(zip(sources, targets))]
    for copy in copies:
        copy.start()
    for copy in copies:
        copy.wait()
    even = parity() == 0
    ds, dq = ds_ref[...], dq_ref[...]
    jac = jac_ref[...]
    new, mid, old = vel_ref[0], vel_ref[1], vel_ref[2]
    guess = 3.0 * (new - mid) + old
    direct = (jac * w3_ref[...])[None] * (-10.0 * new + 16.0 * mid - 6.0 * old) + 3.0 * past_ref[0] - past_ref[1]
    lanes = to_lanes(jnp.concatenate([new, guess, direct, metric_ref[...], jac[None]], axis=0))
    new, guess, direct, metric, jac = lanes[0:3], lanes[3:6], lanes[6:9], lanes[9:12], lanes[12]
    moved = [rows(new[i]) for i in range(3)]
    plain = moved + [rows(jac)] + [rows(new[d] * metric[d]) for d in range(3)]
    wide = right_dot(jnp.concatenate(plain, axis=0), jright_ref)
    slope = right_dot(jnp.concatenate(moved, axis=0), jslope_ref)
    scale = left_dot(jleft_ref, wide[192:256]) * wfine_ref[...]
    carry = [left_dot(jleft_ref, wide[256 + 64 * d : 320 + 64 * d]) for d in range(3)]
    products = []
    for i in range(3):
        part = wide[64 * i : 64 * i + 64]
        total = carry[0] * left_dot(jleft_a_ref, part) + carry[1] * left_dot(jleft_s_ref, part)
        total = total + carry[2] * left_dot(jleft_ref, slope[64 * i : 64 * i + 64])
        products.append(scale * total)
    coarse = left_dot(jleft_t_ref, jnp.concatenate(products, axis=1))
    coarse = pair_dot(jnp.concatenate([coarse[:, 256 * i : 256 * i + 256] for i in range(3)], axis=0), jright_t_ref)
    mass = jac * wmass_ref[...]
    factor = [mass * metric[d] * metric[d] for d in range(3)]
    result = []
    for i in range(3):
        ga, gs, gq = gradient(guess[i], ds, dq)
        stiff = gradient_t(factor[0] * ga, factor[1] * gs, factor[2] * gq, ds, dq)
        result.append(direct[i] - 3.0 * planes(coarse[64 * i : 64 * i + 64]) - viscosity * stiff)
    result.extend([mass, metric[0], metric[1], metric[2]])
    lane = lax.broadcasted_iota(jnp.int32, (NP, LANES), 1)
    index = jnp.zeros((NP, LANES), jnp.int32)
    for e in range(ES):
        index = jnp.where((lane >> 3) == slot_ref[e], e * NP, index)
    index = index + (lane & 7)
    result = [take_lanes(x, index) for x in result]
    for k in range(4):
        joined = join_s(result[k])
        cross_ref[k] = jnp.where(even, joined[0], joined[NP - 1])
        pack_ref[NP * k : NP * k + NP] = joined if k < 3 else result[k]
    for k in range(4, 7):
        pack_ref[NP * k : NP * k + NP] = result[k]


def chip_rows(first, second):
    return jnp.concatenate([first[:-1], (first[-1] + second[0])[None], second[1:]], axis=0)


def own_rows(even, x):
    return jnp.where(even, x[:NP], x[NP - 1 :])


def edge_rows(even, x):
    return jnp.where(even, x[:EDGE], x[ROWS - EDGE :])


def divergence_kernel(own_ref, mate_ref, ds_ref, dq_ref, div_ref, op_ref, level_ref, cross_ref):
    even = parity() == 0
    own, mate = own_ref[...], mate_ref[...]
    packs = [jnp.where(even, own, mate), jnp.where(even, mate, own)]
    parts = [[pack[NP * k : NP * k + NP] for k in range(7)] for pack in packs]
    low, high = packs[0][7 * NP :], packs[1][7 * NP :]
    sides = []
    for k in range(4):
        first, second = parts[0][k], parts[1][k]
        if k == 3:
            first, second = join_s(first), join_s(second)
        whole = chip_rows(first, second)
        sides.append(jnp.concatenate([(whole[0] + low[k])[None], whole[1:-1], (whole[-1] + high[k])[None]], axis=0))
    inv = 1.0 / sides[3]
    accel = [sides[d] * inv for d in range(3)]
    div = []
    levels = []
    for layer in range(2):
        mass = parts[layer][3]
        at = (NP - 1) * layer
        sums = []
        terms = []
        for d in range(3):
            one = mass * parts[layer][4 + d]
            two = one * parts[layer][4 + d]
            op_ref[layer, d] = two
            sums.append(jnp.sum(rows(two), axis=0, keepdims=True))
            terms.append(one * accel[d][at : at + NP])
        op_ref[layer, 3] = mass_shift * mass
        sums.append(jnp.sum(rows(mass), axis=0, keepdims=True))
        sums.append(jnp.zeros((4, LANES), jnp.float32))
        levels.append(jnp.concatenate(sums, axis=0))
        div.append(join_s(gradient_t(terms[0], terms[1], terms[2], ds_ref[...], dq_ref[...])))
    whole = chip_rows(div[0], div[1])
    div_ref[...] = whole
    cross_ref[:EDGE] = edge_rows(even, whole)
    level = jnp.where(even, levels[0], levels[1])
    level_ref[...] = level
    cross_ref[EDGE] = level


def half_window(even, local, received):
    edge = received[:EDGE]
    low = jnp.concatenate([edge[:-1], (edge[-1] + local[0])[None], local[1:EDGE]], axis=0)
    high = jnp.concatenate([local[ROWS - EDGE : -1], (local[-1] + edge[0])[None], edge[1:]], axis=0)
    return jnp.where(even, low, high)


def own_of_half(even, x):
    return jnp.where(even, x[NP : 2 * NP], x[1 : NP + 1])


def inverse_levels(levels, spread_ref, lam_ref):
    result = []
    for level in levels:
        level = full_dot(level, spread_ref[...])
        denom = level[0:1] * lam_ref[0] + level[1:2] * lam_ref[1] + level[2:3] * lam_ref[2] + mass_shift * level[3:4]
        result.append(1.0 / denom)
    return result


def schwarz(half, even, inv_ref, sleft_ref, sright_ref, srback_ref, sback_ref):
    before, after = roll(half, NP, 2), roll(half, -NP, 2)
    columns = []
    for layer in range(2):
        at = (NP - 1) * layer
        columns.append(jnp.concatenate([x[at : at + NP + 2].reshape(80, LANES) for x in (half, before, after)], axis=0))
    spectra = left_dot(sleft_ref, jnp.concatenate(columns, axis=1))
    spectra = jnp.concatenate([spectra[:, LANES * k : LANES * k + LANES] for k in range(2)], axis=0)
    spectra = pair_dot(right_dot(spectra, sright_ref) * inv_ref[...], srback_ref)
    spectra = jnp.concatenate([spectra[MODES * k : MODES * k + MODES] for k in range(2)], axis=1)
    blocks = left_dot(sback_ref, spectra)
    z = []
    for layer in range(2):
        part = blocks[:, LANES * layer : LANES * layer + LANES]
        part = part[:80] + roll(part[80:160], -NP, 1) + roll(part[160:], NP, 1)
        z.append(part.reshape(NP + 2, NP, LANES))
    upper = jnp.concatenate([z[0][8:] + z[1][1:3], z[1][3:]], axis=0)
    lower = jnp.concatenate([z[0][:7], z[0][7:9] + z[1][:2]], axis=0)
    return jnp.where(even, upper, lower)


def join_sides(even, own, mate):
    first, second = jnp.where(even, own, mate), jnp.where(even, mate, own)
    return jnp.concatenate([first[:6], first[6:] + second[:3], second[3:]], axis=0)


def operate(v, op_ref, ds_ref, qright_ref, qright_t_ref):
    ds = ds_ref[...]
    layers = [v[(NP - 1) * k : (NP - 1) * k + NP] for k in range(2)]
    gq = right_dot(jnp.concatenate([rows(x) for x in layers], axis=0), qright_ref)
    hq = [op_ref[k, 2] * planes(gq[64 * k : 64 * k + 64]) for k in range(2)]
    back = right_dot(jnp.concatenate([rows(x) for x in hq], axis=0), qright_t_ref)
    parts = []
    for k, x in enumerate(layers):
        local = d_a(op_ref[k, 0] * d_a(x, False), True) + d_s(op_ref[k, 1] * d_s(x, ds[0]), ds[1])
        parts.append(join_s(local + (op_ref[k, 3] * x + planes(back[64 * k : 64 * k + 64]))))
    return chip_rows(parts[0], parts[1])


def first_smooth_kernel(div_ref, received_ref, level_ref, spread_ref, lam_ref, sleft_ref, sright_ref, srback_ref, sback_ref, half_ref, inv_ref, part_ref):
    even = parity() == 0
    half = half_window(even, div_ref[...], received_ref)
    half_ref[...] = half
    other = received_ref[EDGE]
    own = level_ref[...]
    levels = [jnp.where(even, other, own), jnp.where(even, own, other)]
    for k, inv in enumerate(inverse_levels(levels, spread_ref, lam_ref)):
        inv_ref[MODES * k : MODES * k + MODES] = inv
    part_ref[...] = schwarz(half, even, inv_ref, sleft_ref, sright_ref, srback_ref, sback_ref)


def smooth_kernel(step, before_ref, local_ref, received_ref, inv_ref, sleft_ref, sright_ref, srback_ref, sback_ref, own_image_ref, half_ref, part_ref):
    even = parity() == 0
    image = half_window(even, local_ref[...], received_ref)
    half = before_ref[...] - step * image
    half_ref[...] = half
    part_ref[...] = schwarz(half, even, inv_ref, sleft_ref, sright_ref, srback_ref, sback_ref)
    own_image_ref[...] = own_of_half(even, image)


def operator_kernel(part_ref, mate_ref, op_ref, ds_ref, qright_ref, qright_t_ref, v_ref, local_ref, cross_ref):
    even = parity() == 0
    v = join_sides(even, part_ref[...], mate_ref[...])
    v_ref[...] = v
    local = operate(v, op_ref, ds_ref, qright_ref, qright_t_ref)
    local_ref[...] = local
    cross_ref[...] = edge_rows(even, local)


def last_operator_kernel(part_ref, mate_ref, op_ref, ds_ref, qright_ref, qright_t_ref, ws_ref, div_ref, half_ref, v0_ref, v1_ref, l0_ref, l1_ref, own_ref, face_ref, sums_ref):
    even = parity() == 0
    v2 = join_sides(even, part_ref[...], mate_ref[...])
    l2 = operate(v2, op_ref, ds_ref, qright_ref, qright_t_ref)
    face_ref[...] = jnp.where(even, l2[0], l2[-1])
    v = [v0_ref[...], v1_ref[...], v2]
    images = [l0_ref[...], l1_ref[...], l2]
    residual = div_ref[...] - STEPS[0] * images[0] - STEPS[1] * images[1]
    ws = ws_ref[...]
    pairs = [(v[i], images[j]) for i, j in ((0, 0), (0, 1), (0, 2), (1, 1), (1, 2), (2, 2))]
    pairs.extend((v[i], residual) for i in range(3))
    lane = lax.broadcasted_iota(jnp.int32, (NP, LANES), 1)
    line = jnp.zeros((NP, LANES), jnp.float32)
    for k, (left, right) in enumerate(pairs):
        line = jnp.where(lane == k, jnp.sum(jnp.sum(left * right, axis=0) * ws), line)
    for k in range(sums_ref.shape[0] // NP):
        sums_ref[NP * k : NP * k + NP] = line
    for k, x in enumerate((v[0], v[1], v2, l2)):
        own_ref[k] = own_rows(even, x)
    own_ref[4] = own_of_half(even, half_ref[...])


def to_output(x, order_ref, scratch_ref):
    scratch_ref[...] = rows(x)
    by_s = [scratch_ref[pl.ds(s, NP, stride=NP), :] for s in range(NP - 1)]
    tiles = []
    for tile in range(7):
        index, s = order_ref[0, tile], order_ref[1, tile]
        value = jnp.take_along_axis(by_s[0], index, axis=1)
        for k in range(1, NP - 1):
            value = jnp.where(s == k, jnp.take_along_axis(by_s[k], index, axis=1), value)
        tiles.append(value)
    return jnp.concatenate(tiles, axis=1)


def combine_kernel(sums_ref, face_ref, own_ref, w0_ref, w1_ref, order_ref, p_ref, r_ref, first_ref, second_ref):
    even = parity() == 0
    face = face_ref[...]
    local = own_ref[3]
    first = jnp.where(even, local[0] + face, local[0])
    last = jnp.where(even, local[-1], local[-1] + face)
    w2 = jnp.concatenate([first[None], local[1:-1], last[None]], axis=0)
    line = jnp.sum(sums_ref[...], axis=0, keepdims=True)
    h00, h01, h02, h11, h12, h22, g0, g1, g2 = [line[:, k : k + 1] for k in range(9)]
    m1, m2 = h01 / h00, h02 / h00
    k11, k12, k22 = h11 - m1 * h01, h12 - m1 * h02, h22 - m2 * h02
    f1, f2 = g1 - m1 * g0, g2 - m2 * g0
    n2 = k12 / k11
    c2 = (f2 - n2 * f1) / (k22 - n2 * k12)
    c1 = (f1 - k12 * c2) / k11
    c0 = (g0 - h01 * c1 - h02 * c2) / h00
    pressure = (c0 + STEPS[0])[None] * own_ref[0] + (c1 + STEPS[1])[None] * own_ref[1] + c2[None] * own_ref[2]
    residual = own_ref[4] - (c0[None] * w0_ref[...] + c1[None] * w1_ref[...] + c2[None] * w2)
    p_ref[...] = to_output(pressure, order_ref, first_ref)
    r_ref[...] = to_output(residual, order_ref, second_ref)


def call(kernel, shapes, *args, scratch=()):
    return pl.pallas_call(
        kernel,
        out_shape=[jax.ShapeDtypeStruct(shape, jnp.float32) for shape in shapes],
        in_specs=[pl.BlockSpec(memory_space=pltpu.VMEM)] * len(args),
        out_specs=[pl.BlockSpec(memory_space=pltpu.VMEM)] * len(shapes),
        scratch_shapes=scratch,
        compiler_params=PARAMS,
    )(*args)


def call_forcing(*args):
    shapes = [(7 * NP + 4, NP, LANES), (4, NP, LANES)]
    scratch = [pltpu.SMEM(args[0].shape, jnp.int32)]
    scratch.extend(pltpu.VMEM(x.shape, x.dtype) for x in args[1:])
    scratch.append(pltpu.SemaphoreType.DMA((len(args),)))
    return pl.pallas_call(
        forcing_kernel,
        out_shape=[jax.ShapeDtypeStruct(shape, jnp.float32) for shape in shapes],
        in_specs=[pl.BlockSpec(memory_space=pltpu.HBM)] * len(args),
        out_specs=[pl.BlockSpec(memory_space=pltpu.VMEM)] * len(shapes),
        scratch_shapes=scratch,
        compiler_params=pltpu.CompilerParams(vmem_limit_bytes=FORCING_VMEM),
    )(*args)


FORCING_TABLES = ("w3", "wmass", "ds", "dq", "jright", "jslope", "jright_t", "jleft", "jleft_a", "jleft_s", "jleft_t", "wfine")


def team_groups(count):
    return [[2 * c + side for c in range(count // 2)] for side in range(2)]


def shards(velocity, conv_past, metric, jacobian, element_slot):
    count = lax.axis_size("dom")
    t = {key: jnp.asarray(value) for key, value in TAB.items()}
    field = (NP, NP, LANES)
    chip = (ROWS, NP, LANES)
    half_shape = (2 * NP + 1, NP, LANES)
    edge = (EDGE, NP, LANES)
    pack, cross = call_forcing(
        element_slot, velocity, conv_past, metric, jacobian, *(t[key] for key in FORCING_TABLES)
    )
    own = lax.dynamic_update_slice(pack, swap_cross(cross, count), (7 * NP, 0, 0))
    mate = swap_inner(own, count)
    div, op, level, cross = call(
        divergence_kernel,
        [chip, (2, 4) + field, (NP, LANES), (EDGE + 1, NP, LANES)],
        own, mate, t["ds"], t["dq"],
    )
    solve = (t["sleft"], t["sright"], t["srback"], t["sback"])
    tables = (op, t["ds"], t["qright"], t["qright_t"])
    half, inv, part = call(
        first_smooth_kernel,
        [half_shape, (2 * MODES, ES * (NP + 2)), edge],
        div, swap_cross(cross, count), level, t["spread"], t["lam"], *solve,
    )
    vectors, locals_, images = [], [], []
    for step in STEPS:
        v, local, cross = call(
            operator_kernel, [chip, chip, edge], part, swap_inner(part, count), *tables
        )
        image, half, part = call(
            functools.partial(smooth_kernel, step),
            [field, half_shape, edge],
            half, local, swap_cross(cross, count), inv, *solve,
        )
        vectors.append(v)
        locals_.append(local)
        images.append(image)
    own, face, sums = call(
        last_operator_kernel,
        [(5,) + field, (NP, LANES), (count // 2, LANES)],
        part, swap_inner(part, count), *tables, t["ws"], div, half, *vectors, *locals_,
    )
    sums = lax.all_to_all(sums, "dom", 0, 0, tiled=True, axis_index_groups=team_groups(count))
    face = swap_cross(face, count)
    return tuple(
        call(
            combine_kernel,
            [(NP, 896), (NP, 896)],
            sums, face, own, *images, t["order"],
            scratch=[pltpu.VMEM((NP * NP, LANES), jnp.float32)] * 2,
        )
    )


def solution(mesh):
    return jax.shard_map(
        shards,
        mesh=mesh,
        in_specs=(
            P(None, None, "dom", None),
            P(None, None, "dom", None),
            P(None, "dom", None),
            P("dom", None),
            P("dom"),
        ),
        out_specs=(P("dom", None), P("dom", None)),
        check_vma=False,
    )
```

```python
import functools

import jax
import jax.numpy as jnp
import numpy as np
from jax import lax
from jax.experimental import pallas as pl
from jax.experimental.pallas import tpu as pltpu
from jax.sharding import PartitionSpec as P

NP = 8
NF = 12
ES = 16
LANES = 128
time_step = 0.25
viscosity = 0.05
mass_shift = 0.001
STEPS = (0.45, 0.3)
VMEM = 48 * 1024 * 1024
FORCING_VMEM = 56 * 1024 * 1024
ROWS = 2 * NP - 1
EDGE = NP + 1
MODES = 112


def legendre_pair(points, order):
    before = np.ones(points.shape)
    current = points * 1.0
    for level in range(2, order + 1):
        nextone = ((2 * level - 1) * points * current - (level - 1) * before) / level
        before = current
        current = nextone
    return (current, before)


def jacobi_eigen(matrix):
    size = matrix.shape[0]
    work = matrix * 1.0
    vectors = np.eye(size)
    for sweep in range(30):
        for first in range(size - 1):
            for second in range(first + 1, size):
                off = float(work[first, second])
                if abs(off) > 1e-300:
                    tau = (float(work[second, second]) - float(work[first, first])) / (2.0 * off)
                    if tau >= 0.0:
                        tangent = 1.0 / (tau + (1.0 + tau * tau) ** 0.5)
                    else:
                        tangent = -1.0 / (-tau + (1.0 + tau * tau) ** 0.5)
                    cosine = 1.0 / (1.0 + tangent * tangent) ** 0.5
                    sine = tangent * cosine
                    rotation = np.eye(size)
                    rotation[first, first] = cosine
                    rotation[second, second] = cosine
                    rotation[first, second] = sine
                    rotation[second, first] = -sine
                    work = rotation.T @ work @ rotation
                    vectors = vectors @ rotation
    diagonal_index = np.arange(size)
    return (work[diagonal_index, diagonal_index], vectors)


def base_tables(points_edge, points_fine):
    degree = points_edge - 1
    points = -np.cos(np.pi * np.arange(points_edge) / degree)
    for sweep in range(100):
        top, below = legendre_pair(points, degree)
        points = points - (points * top - below) / (points_edge * top)
    top, below = legendre_pair(points, degree)
    weight_gll = 2.0 / (degree * points_edge * top**2)
    spacing = points[:, None] - points[None, :] + np.eye(points_edge)
    barycentric = 1.0 / np.prod(spacing, axis=1)
    derivative = barycentric[None, :] / barycentric[:, None] / spacing
    derivative = derivative * (1.0 - np.eye(points_edge))
    derivative = derivative - np.eye(points_edge) * derivative.sum(axis=1)[:, None]
    fine_points = np.cos(np.pi * (np.arange(points_fine) + 0.75) / (points_fine + 0.5))
    for sweep in range(100):
        top, below = legendre_pair(fine_points, points_fine)
        slope = points_fine * (fine_points * top - below) / (fine_points * fine_points - 1.0)
        fine_points = fine_points - top / slope
    top, below = legendre_pair(fine_points, points_fine)
    slope = points_fine * (fine_points * top - below) / (fine_points * fine_points - 1.0)
    fine_weight = 2.0 / ((1.0 - fine_points * fine_points) * slope * slope)
    fine_points = fine_points[::-1]
    fine_weight = fine_weight[::-1]
    interpolate = np.ones((points_fine, points_edge))
    for column in range(points_edge):
        for other in range(points_edge):
            if other != column:
                interpolate[:, column] = (
                    interpolate[:, column]
                    * (fine_points - points[other])
                    / (points[column] - points[other])
                )
    stiffness = derivative.T @ (weight_gll[:, None] * derivative)
    extent = 3 * degree + 1
    joined_stiff = np.zeros((extent, extent))
    joined_mass = np.zeros(extent)
    for segment in range(3):
        offset = segment * degree
        joined_stiff[offset : offset + points_edge, offset : offset + points_edge] += stiffness
        joined_mass[offset : offset + points_edge] += weight_gll
    low = degree - 1
    high = 2 * degree + 2
    root_mass = np.sqrt(joined_mass[low:high])
    scaled = joined_stiff[low:high, low:high] / root_mass[:, None] / root_mass[None, :]
    scaled = 0.5 * (scaled + scaled.T)
    eigen_values, eigen_vectors = jacobi_eigen(scaled)
    solve_mat = eigen_vectors / root_mass[:, None]
    breadth = high - low
    return dict(
        derivative=derivative,
        interpolate=interpolate,
        weight=weight_gll,
        fine_weight=fine_weight,
        solve=solve_mat,
        eigen=eigen_values,
    )


def f32(value):
    return np.ascontiguousarray(value, dtype=np.float32)


def halves(value):
    value = np.asarray(value, dtype=np.float32)
    high = value.astype(jnp.bfloat16)
    rest = (value - high.astype(np.float32)).astype(jnp.bfloat16)
    return high, rest


def for_left(value):
    high, rest = halves(value)
    return np.concatenate([high, rest, high], axis=1)


def for_right(value):
    high, rest = halves(value)
    return np.concatenate([high, rest, high], axis=0)


def by_modes_right(value):
    high, rest = halves(by_modes(value, 0))
    parts = (high, rest, high)
    return np.concatenate([x[:LANES] for x in parts] + [x[LANES:] for x in parts])


def pair(value):
    return np.stack(halves(value))


def by_modes(value, axis):
    at = np.arange(ES * (NP + 2))
    order = np.concatenate([at[at % (NP + 2) < NP], at[at % (NP + 2) >= NP]])
    return np.take(value, order, axis=axis)


def make_tables():
    base = base_tables(NP, NF)
    deriv, interp, solve, eigen = base["derivative"], base["interpolate"], base["solve"], base["eigen"]
    w, wf = base["weight"], base["fine_weight"]
    out = {}
    index = np.arange(NP)

    def sublane(matrix):
        rows = [matrix[index, (index + shift) % NP] for shift in range(NP)]
        return f32(np.broadcast_to(np.stack(rows)[:, :, None], (NP, NP, LANES)))

    def lane(matrix):
        rows = []
        for shift in range(-(NP - 1), NP):
            row = np.zeros(NP)
            for q in range(NP):
                if 0 <= q + shift < NP:
                    row[q] = matrix[q, q + shift]
            rows.append(np.tile(row, ES))
        return f32(np.broadcast_to(np.stack(rows)[:, None, :], (2 * NP - 1, NP, LANES)))

    out["ds"] = np.stack([sublane(deriv), sublane(deriv.T)])
    out["dq"] = np.stack([lane(deriv), lane(deriv.T)])
    out["qright"] = for_right(np.kron(np.eye(ES), deriv.T))
    out["qright_t"] = for_right(np.kron(np.eye(ES), deriv))
    out["w3"] = f32(np.einsum("a,s,q->asq", w, w, w).reshape(1, 512))
    out["wmass"] = f32(np.tile(np.einsum("a,s,q->asq", w, w, w), (1, 1, ES)))
    both = interp @ deriv
    pad = np.zeros((16 - NF, NP))
    line = np.concatenate([interp, pad])
    slope = np.concatenate([both, pad])
    out["jright"] = for_right(np.kron(np.eye(ES), line.T))
    out["jslope"] = for_right(np.kron(np.eye(ES), slope.T))
    out["jright_t"] = pair(np.kron(np.eye(ES), line))
    out["jleft"] = for_left(np.kron(interp, interp))
    out["jleft_a"] = for_left(np.kron(both, interp))
    out["jleft_s"] = for_left(np.kron(interp, both))
    out["jleft_t"] = for_left(np.kron(interp, interp).T)
    wide_wf = np.concatenate([wf, np.zeros(16 - NF)])
    out["wfine"] = f32(np.kron(np.kron(wf, wf)[:, None], np.tile(wide_wf, ES)[None, :]))
    at = np.arange(7 * LANES)
    element, within = at // 56, at % 56
    order = np.stack([element * NP + within % NP, within // NP]).reshape(2, 7, 1, LANES)
    out["order"] = np.ascontiguousarray(np.broadcast_to(order, (2, 7, NP, LANES)), dtype=np.int32)
    wide = NP + 2
    left = np.zeros((MODES, 112))
    back = np.zeros((144, MODES))
    at = np.arange(wide)
    for i in range(wide):
        for j in range(wide):
            row = i * wide + j
            inside = np.outer(solve[:, i], solve[1:-1, j]).reshape(80)
            left[row, :80] = inside
            left[row, 80 + at] = solve[:, i] * solve[0, j]
            left[row, 96 + at] = solve[:, i] * solve[wide - 1, j]
            back[:80, row] = inside
            for block, s in enumerate((0, 1, wide - 2, wide - 1)):
                back[80 + 16 * block + at, row] = solve[:, i] * solve[s, j]
    out["sleft"] = for_left(left)
    out["sback"] = for_left(back)
    out["sright"] = for_right(by_modes(np.kron(np.eye(ES), solve[1:-1, :]), 1))
    out["srback"] = by_modes_right(np.kron(np.eye(ES), solve[1:-1, :].T))
    out["spread"] = f32(by_modes(np.kron(np.eye(ES), np.ones((NP, wide))), 1) / 8.0)
    lam_a = np.zeros((MODES, 1))
    lam_s = np.zeros((MODES, 1))
    lam_a[:100, 0] = np.repeat(eigen, wide)
    lam_s[:100, 0] = np.tile(eigen, wide)
    lam_q = by_modes(np.tile(eigen, ES)[None, :], 1)
    full = (MODES, ES * wide)
    out["lam"] = f32(np.stack([np.broadcast_to(lam_a, full), np.broadcast_to(lam_s, full), np.broadcast_to(lam_q, full)]))
    half = np.ones(NP)
    half[0] = half[-1] = 0.5
    out["ws"] = f32(np.broadcast_to(half[:, None], (NP, LANES)))
    return out


TAB = make_tables()
DERIV = [[float(x) for x in row] for row in base_tables(NP, NF)["derivative"].astype(np.float32)]
PARAMS = pltpu.CompilerParams(vmem_limit_bytes=VMEM)


def full_dot(left, right):
    return jnp.dot(left, right, precision=lax.Precision.HIGHEST, preferred_element_type=jnp.float32)


def short_dot(left, right):
    return jnp.dot(left, right, preferred_element_type=jnp.float32)


def split(x):
    high = x.astype(jnp.bfloat16)
    return high, (x - high.astype(jnp.float32)).astype(jnp.bfloat16)


def left_dot(table_ref, x):
    high, rest = split(x)
    return short_dot(table_ref[...], jnp.concatenate([high, high, rest], axis=0))


def right_dot(x, table_ref):
    high, rest = split(x)
    return short_dot(jnp.concatenate([high, high, rest], axis=1), table_ref[...])


def modes_dot(x, table_ref):
    high, rest = split(x)
    parts = (high, high, rest)
    whole = [y[:, :LANES] for y in parts] + [y[:, LANES:] for y in parts]
    return short_dot(jnp.concatenate(whole, axis=1), table_ref[...])


def pair_dot(x, table_ref):
    high, rest = split(x)
    return short_dot(high, table_ref[0]) + (short_dot(high, table_ref[1]) + short_dot(rest, table_ref[0]))


def roll(x, shift, axis):
    return pltpu.roll(x, shift % x.shape[axis], axis)


def d_a(x, transposed):
    rows = []
    for a in range(NP):
        total = None
        for b in range(NP):
            term = (DERIV[b][a] if transposed else DERIV[a][b]) * x[b]
            total = term if total is None else total + term
        rows.append(total)
    return jnp.stack(rows)


def d_s(x, coef):
    total = coef[0][None] * x
    for shift in range(1, NP):
        total = total + coef[shift][None] * roll(x, -shift, 1)
    return total


def d_q(x, coef):
    total = coef[NP - 1][None] * x
    for shift in range(1, NP):
        total = total + coef[NP - 1 + shift][None] * roll(x, -shift, 2)
        total = total + coef[NP - 1 - shift][None] * roll(x, shift, 2)
    return total


def gradient(x, ds, dq):
    return d_a(x, False), d_s(x, ds[0]), d_q(x, dq[0])


def gradient_t(xa, xs, xq, ds, dq):
    return d_a(xa, True) + d_s(xs, ds[1]) + d_q(xq, dq[1])


def join_s(x):
    s = lax.broadcasted_iota(jnp.int32, x.shape, 1)
    from_before = roll(roll(x, NP, 2), 1, 1)
    from_after = roll(roll(x, -NP, 2), -1, 1)
    zero = jnp.zeros_like(x)
    return x + jnp.where(s == 0, from_before, jnp.where(s == NP - 1, from_after, zero))


def parity():
    return lax.rem(lax.axis_index("dom"), 2)


def swap_inner(x, count):
    return lax.ppermute(x, "dom", [(i, i ^ 1) for i in range(count)])


def swap_cross(x, count):
    pairs = [(i, (i + 1) % count if i % 2 else (i - 1) % count) for i in range(count)]
    return lax.ppermute(x, "dom", pairs)


def to_lanes(x):
    shape = (x.shape[0], NP, LANES)
    lane = lax.broadcasted_iota(jnp.int32, shape, 2)
    pieces = []
    for tile in range(4):
        first = x[:, :8, tile * LANES : (tile + 1) * LANES]
        second = x[:, 8:, tile * LANES : (tile + 1) * LANES]
        pieces.append(jnp.where(lane < 64, first, roll(second, 64, 2)))
        pieces.append(jnp.where(lane < 64, roll(first, 64, 2), second))
    y = jnp.stack(pieces, axis=1).reshape(x.shape[0] * NP, NP, LANES)
    sub = lax.broadcasted_iota(jnp.int32, y.shape, 1)
    lane = lax.broadcasted_iota(jnp.int32, y.shape, 2)
    for bit in range(3):
        step = 1 << bit
        in_sub = (sub & step) != 0
        in_lane = (lane & (step * 8)) != 0
        up = roll(roll(y, -step, 1), step * 8, 2)
        down = roll(roll(y, step, 1), -step * 8, 2)
        y = jnp.where(in_sub == in_lane, y, jnp.where(in_lane, up, down))
    return y.reshape(x.shape[0], NP, NP, LANES)


def rows(x):
    return x.reshape(NP * NP, LANES)


def planes(x):
    return x.reshape(NP, NP, LANES)


def take_lanes(x, index):
    flat = x.reshape(-1, LANES)
    tiled = jnp.broadcast_to(index[None], x.shape).reshape(-1, LANES)
    return jnp.take_along_axis(flat, tiled, axis=1).reshape(x.shape)


def forcing_kernel(slot_in, vel_in, past_in, metric_in, jac_in, w3_in, wmass_in, ds_in, dq_in, jright_in, jslope_in, jright_t_in, jleft_in, jleft_a_in, jleft_s_in, jleft_t_in, wfine_in, pack_ref, cross_ref, slot_ref, vel_ref, past_ref, metric_ref, jac_ref, w3_ref, wmass_ref, ds_ref, dq_ref, jright_ref, jslope_ref, jright_t_ref, jleft_ref, jleft_a_ref, jleft_s_ref, jleft_t_ref, wfine_ref, sems):
    sources = (slot_in, vel_in, past_in, metric_in, jac_in, w3_in, wmass_in, ds_in, dq_in, jright_in, jslope_in, jright_t_in, jleft_in, jleft_a_in, jleft_s_in, jleft_t_in, wfine_in)
    targets = (slot_ref, vel_ref, past_ref, metric_ref, jac_ref, w3_ref, wmass_ref, ds_ref, dq_ref, jright_ref, jslope_ref, jright_t_ref, jleft_ref, jleft_a_ref, jleft_s_ref, jleft_t_ref, wfine_ref)
    copies = [pltpu.make_async_copy(x, y, sems.at[k]) for k, (x, y) in enumerate(zip(sources, targets))]
    for copy in copies:
        copy.start()
    for copy in copies[:6]:
        copy.wait()
    even = parity() == 0
    jac = jac_ref[...]
    new, mid, old = vel_ref[0], vel_ref[1], vel_ref[2]
    guess = 3.0 * (new - mid) + old
    direct = (jac * w3_ref[...])[None] * (-10.0 * new + 16.0 * mid - 6.0 * old) + 3.0 * past_ref[0] - past_ref[1]
    lanes = to_lanes(jnp.concatenate([new, guess, direct, metric_ref[...], jac[None]], axis=0))
    new, guess, direct, metric, jac = lanes[0:3], lanes[3:6], lanes[6:9], lanes[9:12], lanes[12]
    for copy in copies[6:]:
        copy.wait()
    ds, dq = ds_ref[...], dq_ref[...]
    moved = [rows(new[i]) for i in range(3)]
    plain = moved + [rows(jac)] + [rows(new[d] * metric[d]) for d in range(3)]
    wide = right_dot(jnp.concatenate(plain, axis=0), jright_ref)
    slope = right_dot(jnp.concatenate(moved, axis=0), jslope_ref)
    scale = left_dot(jleft_ref, wide[192:256]) * wfine_ref[...]
    carry = [left_dot(jleft_ref, wide[256 + 64 * d : 320 + 64 * d]) for d in range(3)]
    products = []
    for i in range(3):
        part = wide[64 * i : 64 * i + 64]
        total = carry[0] * left_dot(jleft_a_ref, part) + carry[1] * left_dot(jleft_s_ref, part)
        total = total + carry[2] * left_dot(jleft_ref, slope[64 * i : 64 * i + 64])
        products.append(scale * total)
    coarse = left_dot(jleft_t_ref, jnp.concatenate(products, axis=1))
    coarse = pair_dot(jnp.concatenate([coarse[:, 256 * i : 256 * i + 256] for i in range(3)], axis=0), jright_t_ref)
    mass = jac * wmass_ref[...]
    factor = [mass * metric[d] * metric[d] for d in range(3)]
    result = []
    for i in range(3):
        ga, gs, gq = gradient(guess[i], ds, dq)
        stiff = gradient_t(factor[0] * ga, factor[1] * gs, factor[2] * gq, ds, dq)
        result.append(direct[i] - 3.0 * planes(coarse[64 * i : 64 * i + 64]) - viscosity * stiff)
    result.extend([mass, metric[0], metric[1], metric[2]])
    lane = lax.broadcasted_iota(jnp.int32, (NP, LANES), 1)
    index = jnp.zeros((NP, LANES), jnp.int32)
    for e in range(ES):
        index = jnp.where((lane >> 3) == slot_ref[e], e * NP, index)
    index = index + (lane & 7)
    result = [take_lanes(x, index) for x in result]
    for k in range(4):
        joined = join_s(result[k])
        cross_ref[k] = jnp.where(even, joined[0], joined[NP - 1])
        pack_ref[NP * k : NP * k + NP] = joined if k < 3 else result[k]
    for k in range(4, 7):
        pack_ref[NP * k : NP * k + NP] = result[k]


def stage_kernel(pack_ref, out_ref, sem):
    copy = pltpu.make_async_copy(pack_ref, out_ref, sem)
    copy.start()
    copy.wait()


def pair_kernel(pack_ref, cross_in, out_ref):
    out_ref[: 7 * NP] = pack_ref[...]
    out_ref[7 * NP :] = cross_in[...]


def chip_rows(first, second):
    return jnp.concatenate([first[:-1], (first[-1] + second[0])[None], second[1:]], axis=0)


def own_rows(even, x):
    return jnp.where(even, x[:NP], x[NP - 1 :])


def edge_rows(even, x):
    return jnp.where(even, x[:EDGE], x[ROWS - EDGE :])


def divergence_kernel(own_ref, mate_ref, ds_ref, qright_t_ref, div_ref, op_ref, level_ref, cross_ref):
    even = parity() == 0
    own, mate = own_ref[...], mate_ref[...]
    packs = [jnp.where(even, own, mate), jnp.where(even, mate, own)]
    parts = [[pack[NP * k : NP * k + NP] for k in range(7)] for pack in packs]
    low, high = packs[0][7 * NP :], packs[1][7 * NP :]
    sides = []
    for k in range(4):
        first, second = parts[0][k], parts[1][k]
        if k == 3:
            first, second = join_s(first), join_s(second)
        whole = chip_rows(first, second)
        sides.append(jnp.concatenate([(whole[0] + low[k])[None], whole[1:-1], (whole[-1] + high[k])[None]], axis=0))
    inv = 1.0 / sides[3]
    accel = [sides[d] * inv for d in range(3)]
    div, last, levels = [], [], []
    for layer in range(2):
        mass = parts[layer][3]
        at = (NP - 1) * layer
        sums = []
        terms = []
        for d in range(3):
            one = mass * parts[layer][4 + d]
            two = one * parts[layer][4 + d]
            op_ref[layer, d] = two
            sums.append(jnp.sum(rows(two), axis=0, keepdims=True))
            terms.append(one * accel[d][at : at + NP])
        op_ref[layer, 3] = mass_shift * mass
        sums.append(jnp.sum(rows(mass), axis=0, keepdims=True))
        sums.append(jnp.zeros((4, LANES), jnp.float32))
        levels.append(jnp.concatenate(sums, axis=0))
        div.append(d_a(terms[0], True) + d_s(terms[1], ds_ref[1]))
        last.append(rows(terms[2]))
    last = right_dot(jnp.concatenate(last, axis=0), qright_t_ref)
    div = [join_s(x + planes(last[64 * k : 64 * k + 64])) for k, x in enumerate(div)]
    whole = chip_rows(div[0], div[1])
    div_ref[...] = whole
    cross_ref[:EDGE] = edge_rows(even, whole)
    level = jnp.where(even, levels[0], levels[1])
    level_ref[...] = level
    cross_ref[EDGE] = level


def half_window(even, local, received):
    edge = received[:EDGE]
    low = jnp.concatenate([edge[:-1], (edge[-1] + local[0])[None], local[1:EDGE]], axis=0)
    high = jnp.concatenate([local[ROWS - EDGE : -1], (local[-1] + edge[0])[None], edge[1:]], axis=0)
    return jnp.where(even, low, high)


def own_of_half(even, x):
    return jnp.where(even, x[NP : 2 * NP], x[1 : NP + 1])


def inverse_levels(levels, spread_ref, lam_ref):
    result = []
    for level in levels:
        level = full_dot(level, spread_ref[...])
        denom = level[0:1] * lam_ref[0] + level[1:2] * lam_ref[1] + level[2:3] * lam_ref[2] + mass_shift * level[3:4]
        result.append(1.0 / denom)
    return result


def schwarz(half, even, inv_ref, sleft_ref, sright_ref, srback_ref, sback_ref, scratch_ref, sum_ref):
    wide = NP + 2
    scratch_ref[...] = half.reshape((2 * NP + 1) * NP, LANES)
    none = jnp.zeros((16 - wide, LANES), jnp.float32)
    columns = []
    for layer in range(2):
        at = (NP - 1) * NP * layer
        before = roll(scratch_ref[pl.ds(at + NP - 2, wide, stride=NP), :], NP, 1)
        after = roll(scratch_ref[pl.ds(at + 1, wide, stride=NP), :], -NP, 1)
        own = half[(NP - 1) * layer : (NP - 1) * layer + wide].reshape(wide * NP, LANES)
        columns.append(jnp.concatenate([own, before, none, after, none], axis=0))
    spectra = left_dot(sleft_ref, jnp.concatenate(columns, axis=1))
    spectra = jnp.concatenate([spectra[:, LANES * k : LANES * k + LANES] for k in range(2)], axis=0)
    spectra = modes_dot(right_dot(spectra, sright_ref) * inv_ref[...], srback_ref)
    spectra = jnp.concatenate([spectra[MODES * k : MODES * k + MODES] for k in range(2)], axis=1)
    blocks = left_dot(sback_ref, spectra)
    z = []
    for layer in range(2):
        part = blocks[:, LANES * layer : LANES * layer + LANES]
        sum_ref[layer] = part[:80]
        for block, (s, shift) in enumerate(((NP - 2, -NP), (NP - 1, -NP), (0, NP), (1, NP))):
            rows_at = pl.ds(s, wide, stride=NP)
            start = 80 + 16 * block
            sum_ref[layer, rows_at, :] = sum_ref[layer, rows_at, :] + roll(part[start : start + wide], shift, 1)
        z.append(sum_ref[layer].reshape(wide, NP, LANES))
    upper = jnp.concatenate([z[0][8:] + z[1][1:3], z[1][3:]], axis=0)
    lower = jnp.concatenate([z[0][:7], z[0][7:9] + z[1][:2]], axis=0)
    return jnp.where(even, upper, lower)


def join_sides(even, own, mate):
    first, second = jnp.where(even, own, mate), jnp.where(even, mate, own)
    return jnp.concatenate([first[:6], first[6:] + second[:3], second[3:]], axis=0)


def operate(v, op_ref, ds_ref, qright_ref, qright_t_ref):
    ds = ds_ref[...]
    layers = [v[(NP - 1) * k : (NP - 1) * k + NP] for k in range(2)]
    gq = right_dot(jnp.concatenate([rows(x) for x in layers], axis=0), qright_ref)
    hq = [op_ref[k, 2] * planes(gq[64 * k : 64 * k + 64]) for k in range(2)]
    back = right_dot(jnp.concatenate([rows(x) for x in hq], axis=0), qright_t_ref)
    parts = []
    for k, x in enumerate(layers):
        local = d_a(op_ref[k, 0] * d_a(x, False), True) + d_s(op_ref[k, 1] * d_s(x, ds[0]), ds[1])
        parts.append(join_s(local + (op_ref[k, 3] * x + planes(back[64 * k : 64 * k + 64]))))
    return chip_rows(parts[0], parts[1])


def first_smooth_kernel(div_ref, received_ref, level_ref, spread_ref, lam_ref, sleft_ref, sright_ref, srback_ref, sback_ref, half_ref, inv_ref, part_ref, scratch_ref, sum_ref):
    even = parity() == 0
    half = half_window(even, div_ref[...], received_ref)
    half_ref[...] = half
    other = received_ref[EDGE]
    own = level_ref[...]
    levels = [jnp.where(even, other, own), jnp.where(even, own, other)]
    for k, inv in enumerate(inverse_levels(levels, spread_ref, lam_ref)):
        inv_ref[MODES * k : MODES * k + MODES] = inv
    part_ref[...] = schwarz(half, even, inv_ref, sleft_ref, sright_ref, srback_ref, sback_ref, scratch_ref, sum_ref)


def smooth_kernel(step, before_ref, local_ref, received_ref, inv_ref, sleft_ref, sright_ref, srback_ref, sback_ref, own_image_ref, half_ref, part_ref, scratch_ref, sum_ref):
    even = parity() == 0
    image = half_window(even, local_ref[...], received_ref)
    half = before_ref[...] - step * image
    half_ref[...] = half
    part_ref[...] = schwarz(half, even, inv_ref, sleft_ref, sright_ref, srback_ref, sback_ref, scratch_ref, sum_ref)
    own_image_ref[...] = own_of_half(even, image)


def operator_kernel(part_ref, mate_ref, op_ref, ds_ref, qright_ref, qright_t_ref, v_ref, local_ref, cross_ref):
    even = parity() == 0
    v = join_sides(even, part_ref[...], mate_ref[...])
    v_ref[...] = v
    local = operate(v, op_ref, ds_ref, qright_ref, qright_t_ref)
    local_ref[...] = local
    cross_ref[...] = edge_rows(even, local)


def fold(parts):
    lane = lax.broadcasted_iota(jnp.int32, (NP, LANES), 1)
    parts = parts + [jnp.zeros((NP, LANES), jnp.float32)] * (ES - len(parts))
    for step in (8, 16, 32, 64):
        chosen = (lane & step) != 0
        parts = [
            jnp.where(chosen, b, a) + roll(jnp.where(chosen, a, b), step, 1)
            for a, b in zip(parts[::2], parts[1::2])
        ]
    return parts[0]


def early_kernel(ws_ref, div_ref, v0_ref, v1_ref, l0_ref, l1_ref, residual_ref, parts_ref):
    ws = ws_ref[...]
    l0, l1 = l0_ref[...], l1_ref[...]
    residual = div_ref[...] - STEPS[0] * l0 - STEPS[1] * l1
    residual_ref[...] = residual
    v0, v1 = v0_ref[...], v1_ref[...]
    for k, (left, right) in enumerate(((v0, l0), (v0, l1), (v1, l1), (v0, residual), (v1, residual))):
        parts_ref[k] = jnp.sum(left * right, axis=0) * ws


def last_operator_kernel(part_ref, mate_ref, op_ref, ds_ref, qright_ref, qright_t_ref, ws_ref, residual_ref, parts_ref, v0_ref, v1_ref, v_ref, local_ref, face_ref, sums_ref):
    even = parity() == 0
    v = join_sides(even, part_ref[...], mate_ref[...])
    v_ref[...] = v
    local = operate(v, op_ref, ds_ref, qright_ref, qright_t_ref)
    local_ref[...] = local
    face_ref[...] = jnp.where(even, local[0], local[-1])
    ws = ws_ref[...]
    new = [jnp.sum(x * y, axis=0) * ws for x, y in ((v0_ref[...], local), (v1_ref[...], local), (v, local), (v, residual_ref[...]))]
    p = [parts_ref[k] for k in range(5)]
    folded = fold([p[0], p[1], new[0], p[2], new[1], new[2], p[3], p[4], new[3]])
    line = jnp.broadcast_to(jnp.sum(folded, axis=0, keepdims=True), (NP, LANES))
    for k in range(sums_ref.shape[0] // NP):
        sums_ref[NP * k : NP * k + NP] = line


def to_output(x, order_ref, scratch_ref, slot):
    scratch_ref[slot] = rows(x)
    by_s = [scratch_ref[slot, pl.ds(s, NP, stride=NP), :] for s in range(NP - 1)]
    tiles = []
    for tile in range(7):
        index, s = order_ref[0, tile], order_ref[1, tile]
        value = jnp.take_along_axis(by_s[0], index, axis=1)
        for k in range(1, NP - 1):
            value = jnp.where(s == k, jnp.take_along_axis(by_s[k], index, axis=1), value)
        tiles.append(value)
    return jnp.concatenate(tiles, axis=1)


def layout_kernel(face_ref, v0_ref, v1_ref, v2_ref, half_ref, w0_ref, w1_ref, local_ref, order_ref, out_ref, scratch_ref):
    even = parity() == 0
    face = face_ref[...]
    local = own_rows(even, local_ref[...])
    first = jnp.where(even, local[0] + face, local[0])
    last = jnp.where(even, local[-1], local[-1] + face)
    w2 = jnp.concatenate([first[None], local[1:-1], last[None]], axis=0)
    fields = [own_rows(even, x[...]) for x in (v0_ref, v1_ref, v2_ref)]
    fields.extend((own_of_half(even, half_ref[...]), w0_ref[...], w1_ref[...], w2))
    for k, x in enumerate(fields):
        out_ref[k] = to_output(x, order_ref, scratch_ref, k)


def combine_kernel(sums_ref, fields_ref, p_ref, r_ref):
    line = jnp.sum(sums_ref[...], axis=0, keepdims=True)
    for step in (4, 2, 1):
        line = line + roll(line, -step, 1)
    shape = (NP, LANES)
    h00, h01, h02, h11, h12, h22, g0, g1, g2 = [jnp.broadcast_to(line[:, NP * k : NP * k + 1], shape) for k in range(9)]
    scale = 1.0 / h00
    m1, m2, m0 = h01 * scale, h02 * scale, g0 * scale
    k11, k12, k22 = h11 - m1 * h01, h12 - m1 * h02, h22 - m2 * h02
    f1, f2 = g1 - m1 * g0, g2 - m2 * g0
    second = 1.0 / k11
    n2 = k12 * second
    c2 = (f2 - n2 * f1) / (k22 - n2 * k12)
    c1 = f1 * second - n2 * c2
    c0 = m0 - m1 * c1 - m2 * c2
    for tile in range(7):
        x = [fields_ref[k, :, LANES * tile : LANES * tile + LANES] for k in range(7)]
        p_ref[:, LANES * tile : LANES * tile + LANES] = (c0 + STEPS[0]) * x[0] + (c1 + STEPS[1]) * x[1] + c2 * x[2]
        r_ref[:, LANES * tile : LANES * tile + LANES] = x[3] - (c0 * x[4] + c1 * x[5] + c2 * x[6])


def call(kernel, shapes, *args, scratch=()):
    return pl.pallas_call(
        kernel,
        out_shape=[jax.ShapeDtypeStruct(shape, jnp.float32) for shape in shapes],
        in_specs=[pl.BlockSpec(memory_space=pltpu.VMEM)] * len(args),
        out_specs=[pl.BlockSpec(memory_space=pltpu.VMEM)] * len(shapes),
        scratch_shapes=scratch,
        compiler_params=PARAMS,
    )(*args)


SMOOTH_SCRATCH = (
    pltpu.VMEM(((2 * NP + 1) * NP, LANES), jnp.float32),
    pltpu.VMEM((2, (NP + 2) * NP, LANES), jnp.float32),
)


def call_forcing(*args):
    shapes = [(7 * NP, NP, LANES), (4, NP, LANES)]
    scratch = [pltpu.SMEM(args[0].shape, jnp.int32)]
    scratch.extend(pltpu.VMEM(x.shape, x.dtype) for x in args[1:])
    scratch.append(pltpu.SemaphoreType.DMA((len(args),)))
    return pl.pallas_call(
        forcing_kernel,
        out_shape=[jax.ShapeDtypeStruct(shape, jnp.float32) for shape in shapes],
        in_specs=[pl.BlockSpec(memory_space=pltpu.HBM)] * len(args),
        out_specs=[pl.BlockSpec(memory_space=pltpu.VMEM)] * len(shapes),
        scratch_shapes=scratch,
        compiler_params=pltpu.CompilerParams(vmem_limit_bytes=FORCING_VMEM),
    )(*args)


FORCING_TABLES = ("w3", "wmass", "ds", "dq", "jright", "jslope", "jright_t", "jleft", "jleft_a", "jleft_s", "jleft_t", "wfine")


def team_groups(count):
    return [[2 * c + side for c in range(count // 2)] for side in range(2)]


def shards(velocity, conv_past, metric, jacobian, element_slot):
    count = lax.axis_size("dom")
    t = {key: jnp.asarray(value) for key, value in TAB.items()}
    field = (NP, NP, LANES)
    chip = (ROWS, NP, LANES)
    half_shape = (2 * NP + 1, NP, LANES)
    edge = (EDGE, NP, LANES)
    pack, cross = call_forcing(
        element_slot, velocity, conv_past, metric, jacobian, *(t[key] for key in FORCING_TABLES)
    )
    cross = swap_cross(cross, count)
    pack = pl.pallas_call(
        stage_kernel,
        out_shape=jax.ShapeDtypeStruct(pack.shape, jnp.float32),
        in_specs=[pl.BlockSpec(memory_space=pltpu.HBM)],
        out_specs=pl.BlockSpec(memory_space=pltpu.VMEM),
        scratch_shapes=[pltpu.SemaphoreType.DMA(())],
        compiler_params=PARAMS,
    )(pack)
    (own,) = call(pair_kernel, [(7 * NP + 4, NP, LANES)], pack, cross)
    mate = swap_inner(own, count)
    div, op, level, cross = call(
        divergence_kernel,
        [chip, (2, 4) + field, (NP, LANES), (EDGE + 1, NP, LANES)],
        own, mate, t["ds"], t["qright_t"],
    )
    solve = (t["sleft"], t["sright"], t["srback"], t["sback"])
    tables = (op, t["ds"], t["qright"], t["qright_t"])
    half, inv, part = call(
        first_smooth_kernel,
        [half_shape, (2 * MODES, ES * (NP + 2)), edge],
        div, swap_cross(cross, count), level, t["spread"], t["lam"], *solve,
        scratch=SMOOTH_SCRATCH,
    )
    vectors, locals_, images = [], [], []
    for step in STEPS:
        v, local, cross = call(
            operator_kernel, [chip, chip, edge], part, swap_inner(part, count), *tables
        )
        image, half, part = call(
            functools.partial(smooth_kernel, step),
            [field, half_shape, edge],
            half, local, swap_cross(cross, count), inv, *solve,
            scratch=SMOOTH_SCRATCH,
        )
        vectors.append(v)
        locals_.append(local)
        images.append(image)
    residual, parts = call(
        early_kernel, [chip, (5, NP, LANES)], t["ws"], div, *vectors, *locals_
    )
    v, local, face, sums = call(
        last_operator_kernel,
        [chip, chip, (NP, LANES), (count // 2, LANES)],
        part, swap_inner(part, count), *tables, t["ws"], residual, parts, *vectors,
    )
    sums = lax.all_to_all(sums, "dom", 0, 0, tiled=True, axis_index_groups=team_groups(count))
    (fields,) = call(
        layout_kernel,
        [(7, NP, 896)],
        swap_cross(face, count), *vectors, v, half, *images, local, t["order"],
        scratch=[pltpu.VMEM((7, NP * NP, LANES), jnp.float32)],
    )
    return tuple(call(combine_kernel, [(NP, 896), (NP, 896)], sums, fields))


def solution(mesh):
    return jax.shard_map(
        shards,
        mesh=mesh,
        in_specs=(
            P(None, None, "dom", None),
            P(None, None, "dom", None),
            P(None, "dom", None),
            P("dom", None),
            P("dom"),
        ),
        out_specs=(P("dom", None), P("dom", None)),
        check_vma=False,
    )
```

```python
import functools

import jax
import jax.numpy as jnp
import numpy as np
from jax import lax
from jax.experimental import pallas as pl
from jax.experimental.pallas import tpu as pltpu
from jax.sharding import PartitionSpec as P

NP = 8
NF = 12
ES = 16
LANES = 128
time_step = 0.25
viscosity = 0.05
mass_shift = 0.001
STEPS = (0.45, 0.3)
VMEM = 48 * 1024 * 1024
FORCING_VMEM = 56 * 1024 * 1024
ROWS = 2 * NP - 1
EDGE = NP + 1
MODES = 112


def legendre_pair(points, order):
    before = np.ones(points.shape)
    current = points * 1.0
    for level in range(2, order + 1):
        nextone = ((2 * level - 1) * points * current - (level - 1) * before) / level
        before = current
        current = nextone
    return (current, before)


def jacobi_eigen(matrix):
    size = matrix.shape[0]
    work = matrix * 1.0
    vectors = np.eye(size)
    for sweep in range(30):
        for first in range(size - 1):
            for second in range(first + 1, size):
                off = float(work[first, second])
                if abs(off) > 1e-300:
                    tau = (float(work[second, second]) - float(work[first, first])) / (2.0 * off)
                    if tau >= 0.0:
                        tangent = 1.0 / (tau + (1.0 + tau * tau) ** 0.5)
                    else:
                        tangent = -1.0 / (-tau + (1.0 + tau * tau) ** 0.5)
                    cosine = 1.0 / (1.0 + tangent * tangent) ** 0.5
                    sine = tangent * cosine
                    rotation = np.eye(size)
                    rotation[first, first] = cosine
                    rotation[second, second] = cosine
                    rotation[first, second] = sine
                    rotation[second, first] = -sine
                    work = rotation.T @ work @ rotation
                    vectors = vectors @ rotation
    diagonal_index = np.arange(size)
    return (work[diagonal_index, diagonal_index], vectors)


def base_tables(points_edge, points_fine):
    degree = points_edge - 1
    points = -np.cos(np.pi * np.arange(points_edge) / degree)
    for sweep in range(100):
        top, below = legendre_pair(points, degree)
        points = points - (points * top - below) / (points_edge * top)
    top, below = legendre_pair(points, degree)
    weight_gll = 2.0 / (degree * points_edge * top**2)
    spacing = points[:, None] - points[None, :] + np.eye(points_edge)
    barycentric = 1.0 / np.prod(spacing, axis=1)
    derivative = barycentric[None, :] / barycentric[:, None] / spacing
    derivative = derivative * (1.0 - np.eye(points_edge))
    derivative = derivative - np.eye(points_edge) * derivative.sum(axis=1)[:, None]
    fine_points = np.cos(np.pi * (np.arange(points_fine) + 0.75) / (points_fine + 0.5))
    for sweep in range(100):
        top, below = legendre_pair(fine_points, points_fine)
        slope = points_fine * (fine_points * top - below) / (fine_points * fine_points - 1.0)
        fine_points = fine_points - top / slope
    top, below = legendre_pair(fine_points, points_fine)
    slope = points_fine * (fine_points * top - below) / (fine_points * fine_points - 1.0)
    fine_weight = 2.0 / ((1.0 - fine_points * fine_points) * slope * slope)
    fine_points = fine_points[::-1]
    fine_weight = fine_weight[::-1]
    interpolate = np.ones((points_fine, points_edge))
    for column in range(points_edge):
        for other in range(points_edge):
            if other != column:
                interpolate[:, column] = (
                    interpolate[:, column]
                    * (fine_points - points[other])
                    / (points[column] - points[other])
                )
    stiffness = derivative.T @ (weight_gll[:, None] * derivative)
    extent = 3 * degree + 1
    joined_stiff = np.zeros((extent, extent))
    joined_mass = np.zeros(extent)
    for segment in range(3):
        offset = segment * degree
        joined_stiff[offset : offset + points_edge, offset : offset + points_edge] += stiffness
        joined_mass[offset : offset + points_edge] += weight_gll
    low = degree - 1
    high = 2 * degree + 2
    root_mass = np.sqrt(joined_mass[low:high])
    scaled = joined_stiff[low:high, low:high] / root_mass[:, None] / root_mass[None, :]
    scaled = 0.5 * (scaled + scaled.T)
    eigen_values, eigen_vectors = jacobi_eigen(scaled)
    solve_mat = eigen_vectors / root_mass[:, None]
    breadth = high - low
    return dict(
        derivative=derivative,
        interpolate=interpolate,
        weight=weight_gll,
        fine_weight=fine_weight,
        solve=solve_mat,
        eigen=eigen_values,
    )


def f32(value):
    return np.ascontiguousarray(value, dtype=np.float32)


def halves(value):
    value = np.asarray(value, dtype=np.float32)
    high = value.astype(jnp.bfloat16)
    rest = (value - high.astype(np.float32)).astype(jnp.bfloat16)
    return high, rest


def for_left(value):
    high, rest = halves(value)
    return np.concatenate([high, rest, high], axis=1)


def for_right(value):
    high, rest = halves(value)
    return np.concatenate([high, rest, high], axis=0)


def by_modes_right(value):
    high, rest = halves(by_modes(value, 0))
    parts = (high, rest, high)
    return np.concatenate([x[:LANES] for x in parts] + [x[LANES:] for x in parts])


def pair(value):
    return np.stack(halves(value))


def by_modes(value, axis):
    at = np.arange(ES * (NP + 2))
    order = np.concatenate([at[at % (NP + 2) < NP], at[at % (NP + 2) >= NP]])
    return np.take(value, order, axis=axis)


def make_tables():
    base = base_tables(NP, NF)
    deriv, interp, solve, eigen = base["derivative"], base["interpolate"], base["solve"], base["eigen"]
    w, wf = base["weight"], base["fine_weight"]
    out = {}
    index = np.arange(NP)

    def sublane(matrix):
        rows = [matrix[index, (index + shift) % NP] for shift in range(NP)]
        return f32(np.broadcast_to(np.stack(rows)[:, :, None], (NP, NP, LANES)))

    def lane(matrix):
        rows = []
        for shift in range(-(NP - 1), NP):
            row = np.zeros(NP)
            for q in range(NP):
                if 0 <= q + shift < NP:
                    row[q] = matrix[q, q + shift]
            rows.append(np.tile(row, ES))
        return f32(np.broadcast_to(np.stack(rows)[:, None, :], (2 * NP - 1, NP, LANES)))

    out["ds"] = np.stack([sublane(deriv), sublane(deriv.T)])
    out["dq"] = np.stack([lane(deriv), lane(deriv.T)])
    out["qright"] = for_right(np.kron(np.eye(ES), deriv.T))
    out["qright_t"] = for_right(np.kron(np.eye(ES), deriv))
    out["w3"] = f32(np.einsum("a,s,q->asq", w, w, w).reshape(1, 512))
    out["wmass"] = f32(np.tile(np.einsum("a,s,q->asq", w, w, w), (1, 1, ES)))
    both = interp @ deriv
    pad = np.zeros((16 - NF, NP))
    line = np.concatenate([interp, pad])
    slope = np.concatenate([both, pad])
    out["jright"] = for_right(np.kron(np.eye(ES), line.T))
    out["jslope"] = for_right(np.kron(np.eye(ES), slope.T))
    out["jright_t"] = pair(np.kron(np.eye(ES), line))
    out["jleft"] = for_left(np.kron(interp, interp))
    out["jleft_a"] = for_left(np.kron(both, interp))
    out["jleft_s"] = for_left(np.kron(interp, both))
    out["jleft_t"] = for_left(np.kron(interp, interp).T)
    wide_wf = np.concatenate([wf, np.zeros(16 - NF)])
    out["wfine"] = f32(np.kron(np.kron(wf, wf)[:, None], np.tile(wide_wf, ES)[None, :]))
    at = np.arange(7 * LANES)
    element, within = at // 56, at % 56
    order = np.stack([element * NP + within % NP, within // NP]).reshape(2, 7, 1, LANES)
    out["order"] = np.ascontiguousarray(np.broadcast_to(order, (2, 7, NP, LANES)), dtype=np.int32)
    wide = NP + 2
    left = np.zeros((MODES, 112))
    back = np.zeros((144, MODES))
    at = np.arange(wide)
    for i in range(wide):
        for j in range(wide):
            row = i * wide + j
            inside = np.outer(solve[:, i], solve[1:-1, j]).reshape(80)
            left[row, :80] = inside
            left[row, 80 + at] = solve[:, i] * solve[0, j]
            left[row, 96 + at] = solve[:, i] * solve[wide - 1, j]
            back[:80, row] = inside
            for block, s in enumerate((0, 1, wide - 2, wide - 1)):
                back[80 + 16 * block + at, row] = solve[:, i] * solve[s, j]
    out["sleft"] = for_left(left)
    out["sback"] = for_left(back)
    out["sright"] = for_right(by_modes(np.kron(np.eye(ES), solve[1:-1, :]), 1))
    out["srback"] = by_modes_right(np.kron(np.eye(ES), solve[1:-1, :].T))
    out["spread"] = f32(by_modes(np.kron(np.eye(ES), np.ones((NP, wide))), 1) / 8.0)
    lam_a = np.zeros((MODES, 1))
    lam_s = np.zeros((MODES, 1))
    lam_a[:100, 0] = np.repeat(eigen, wide)
    lam_s[:100, 0] = np.tile(eigen, wide)
    lam_q = by_modes(np.tile(eigen, ES)[None, :], 1)
    full = (MODES, ES * wide)
    out["lam"] = f32(np.stack([np.broadcast_to(lam_a, full), np.broadcast_to(lam_s, full), np.broadcast_to(lam_q, full)]))
    half = np.ones(NP)
    half[0] = half[-1] = 0.5
    out["ws"] = f32(np.broadcast_to(half[:, None], (NP, LANES)))
    return out


TAB = make_tables()
DERIV = [[float(x) for x in row] for row in base_tables(NP, NF)["derivative"].astype(np.float32)]
PARAMS = pltpu.CompilerParams(vmem_limit_bytes=VMEM)


def full_dot(left, right):
    return jnp.dot(left, right, precision=lax.Precision.HIGHEST, preferred_element_type=jnp.float32)


def short_dot(left, right):
    return jnp.dot(left, right, preferred_element_type=jnp.float32)


def split(x):
    high = x.astype(jnp.bfloat16)
    return high, (x - high.astype(jnp.float32)).astype(jnp.bfloat16)


def left_dot(table_ref, x):
    high, rest = split(x)
    return short_dot(table_ref[...], jnp.concatenate([high, high, rest], axis=0))


def right_dot(x, table_ref):
    high, rest = split(x)
    return short_dot(jnp.concatenate([high, high, rest], axis=1), table_ref[...])


def modes_dot(x, table_ref):
    high, rest = split(x)
    parts = (high, high, rest)
    whole = [y[:, :LANES] for y in parts] + [y[:, LANES:] for y in parts]
    return short_dot(jnp.concatenate(whole, axis=1), table_ref[...])


def pair_dot(x, table_ref):
    high, rest = split(x)
    return short_dot(high, table_ref[0]) + (short_dot(high, table_ref[1]) + short_dot(rest, table_ref[0]))


def roll(x, shift, axis):
    return pltpu.roll(x, shift % x.shape[axis], axis)


def d_a(x, transposed):
    rows = []
    for a in range(NP):
        total = None
        for b in range(NP):
            term = (DERIV[b][a] if transposed else DERIV[a][b]) * x[b]
            total = term if total is None else total + term
        rows.append(total)
    return jnp.stack(rows)


def d_s(x, coef):
    total = coef[0][None] * x
    for shift in range(1, NP):
        total = total + coef[shift][None] * roll(x, -shift, 1)
    return total


def d_q(x, coef):
    total = coef[NP - 1][None] * x
    for shift in range(1, NP):
        total = total + coef[NP - 1 + shift][None] * roll(x, -shift, 2)
        total = total + coef[NP - 1 - shift][None] * roll(x, shift, 2)
    return total


def gradient(x, ds, dq):
    return d_a(x, False), d_s(x, ds[0]), d_q(x, dq[0])


def gradient_t(xa, xs, xq, ds, dq):
    return d_a(xa, True) + d_s(xs, ds[1]) + d_q(xq, dq[1])


def join_s(x):
    s = lax.broadcasted_iota(jnp.int32, x.shape, 1)
    from_before = roll(roll(x, NP, 2), 1, 1)
    from_after = roll(roll(x, -NP, 2), -1, 1)
    zero = jnp.zeros_like(x)
    return x + jnp.where(s == 0, from_before, jnp.where(s == NP - 1, from_after, zero))


def parity():
    return lax.rem(lax.axis_index("dom"), 2)


def swap_inner(x, count):
    return lax.ppermute(x, "dom", [(i, i ^ 1) for i in range(count)])


def swap_cross(x, count):
    pairs = [(i, (i + 1) % count if i % 2 else (i - 1) % count) for i in range(count)]
    return lax.ppermute(x, "dom", pairs)


def to_lanes(x):
    shape = (x.shape[0], NP, LANES)
    lane = lax.broadcasted_iota(jnp.int32, shape, 2)
    pieces = []
    for tile in range(4):
        first = x[:, :8, tile * LANES : (tile + 1) * LANES]
        second = x[:, 8:, tile * LANES : (tile + 1) * LANES]
        pieces.append(jnp.where(lane < 64, first, roll(second, 64, 2)))
        pieces.append(jnp.where(lane < 64, roll(first, 64, 2), second))
    y = jnp.stack(pieces, axis=1).reshape(x.shape[0] * NP, NP, LANES)
    sub = lax.broadcasted_iota(jnp.int32, y.shape, 1)
    lane = lax.broadcasted_iota(jnp.int32, y.shape, 2)
    for bit in range(3):
        step = 1 << bit
        in_sub = (sub & step) != 0
        in_lane = (lane & (step * 8)) != 0
        up = roll(roll(y, -step, 1), step * 8, 2)
        down = roll(roll(y, step, 1), -step * 8, 2)
        y = jnp.where(in_sub == in_lane, y, jnp.where(in_lane, up, down))
    return y.reshape(x.shape[0], NP, NP, LANES)


def rows(x):
    return x.reshape(NP * NP, LANES)


def planes(x):
    return x.reshape(NP, NP, LANES)


def take_lanes(x, index):
    flat = x.reshape(-1, LANES)
    tiled = jnp.broadcast_to(index[None], x.shape).reshape(-1, LANES)
    return jnp.take_along_axis(flat, tiled, axis=1).reshape(x.shape)


def forcing_kernel(slot_in, vel_in, past_in, metric_in, jac_in, w3_in, wmass_in, ds_in, dq_in, jright_in, jslope_in, jright_t_in, jleft_in, jleft_a_in, jleft_s_in, jleft_t_in, wfine_in, pack_ref, cross_ref, slot_ref, vel_ref, past_ref, metric_ref, jac_ref, w3_ref, wmass_ref, ds_ref, dq_ref, jright_ref, jslope_ref, jright_t_ref, jleft_ref, jleft_a_ref, jleft_s_ref, jleft_t_ref, wfine_ref, sems):
    sources = (slot_in, vel_in, past_in, metric_in, jac_in, w3_in, wmass_in, ds_in, dq_in, jright_in, jslope_in, jright_t_in, jleft_in, jleft_a_in, jleft_s_in, jleft_t_in, wfine_in)
    targets = (slot_ref, vel_ref, past_ref, metric_ref, jac_ref, w3_ref, wmass_ref, ds_ref, dq_ref, jright_ref, jslope_ref, jright_t_ref, jleft_ref, jleft_a_ref, jleft_s_ref, jleft_t_ref, wfine_ref)
    copies = [pltpu.make_async_copy(x, y, sems.at[k]) for k, (x, y) in enumerate(zip(sources, targets))]
    for copy in copies:
        copy.start()
    for copy in copies[:6]:
        copy.wait()
    even = parity() == 0
    jac = jac_ref[...]
    new, mid, old = vel_ref[0], vel_ref[1], vel_ref[2]
    guess = 3.0 * (new - mid) + old
    direct = (jac * w3_ref[...])[None] * (-10.0 * new + 16.0 * mid - 6.0 * old) + 3.0 * past_ref[0] - past_ref[1]
    lanes = to_lanes(jnp.concatenate([new, guess, direct, metric_ref[...], jac[None]], axis=0))
    new, guess, direct, metric, jac = lanes[0:3], lanes[3:6], lanes[6:9], lanes[9:12], lanes[12]
    for copy in copies[6:]:
        copy.wait()
    ds, dq = ds_ref[...], dq_ref[...]
    moved = [rows(new[i]) for i in range(3)]
    plain = moved + [rows(jac)] + [rows(new[d] * metric[d]) for d in range(3)]
    wide = right_dot(jnp.concatenate(plain, axis=0), jright_ref)
    slope = right_dot(jnp.concatenate(moved, axis=0), jslope_ref)
    scale = left_dot(jleft_ref, wide[192:256]) * wfine_ref[...]
    carry = [left_dot(jleft_ref, wide[256 + 64 * d : 320 + 64 * d]) for d in range(3)]
    products = []
    for i in range(3):
        part = wide[64 * i : 64 * i + 64]
        total = carry[0] * left_dot(jleft_a_ref, part) + carry[1] * left_dot(jleft_s_ref, part)
        total = total + carry[2] * left_dot(jleft_ref, slope[64 * i : 64 * i + 64])
        products.append(scale * total)
    coarse = left_dot(jleft_t_ref, jnp.concatenate(products, axis=1))
    coarse = pair_dot(jnp.concatenate([coarse[:, 256 * i : 256 * i + 256] for i in range(3)], axis=0), jright_t_ref)
    mass = jac * wmass_ref[...]
    factor = [mass * metric[d] * metric[d] for d in range(3)]
    result = []
    for i in range(3):
        ga, gs, gq = gradient(guess[i], ds, dq)
        stiff = gradient_t(factor[0] * ga, factor[1] * gs, factor[2] * gq, ds, dq)
        result.append(direct[i] - 3.0 * planes(coarse[64 * i : 64 * i + 64]) - viscosity * stiff)
    result.extend([mass, metric[0], metric[1], metric[2]])
    lane = lax.broadcasted_iota(jnp.int32, (NP, LANES), 1)
    index = jnp.zeros((NP, LANES), jnp.int32)
    for e in range(ES):
        index = jnp.where((lane >> 3) == slot_ref[e], e * NP, index)
    index = index + (lane & 7)
    result = [take_lanes(x, index) for x in result]
    for k in range(4):
        joined = join_s(result[k])
        cross_ref[k] = jnp.where(even, joined[0], joined[NP - 1])
        pack_ref[NP * k : NP * k + NP] = joined if k < 3 else result[k]
    for k in range(4, 7):
        pack_ref[NP * k : NP * k + NP] = result[k]


def stage_kernel(pack_ref, out_ref, sem):
    copy = pltpu.make_async_copy(pack_ref, out_ref, sem)
    copy.start()
    copy.wait()


def pair_kernel(pack_ref, cross_in, out_ref):
    out_ref[: 7 * NP] = pack_ref[...]
    out_ref[7 * NP :] = cross_in[...]


def chip_rows(first, second):
    return jnp.concatenate([first[:-1], (first[-1] + second[0])[None], second[1:]], axis=0)


def own_rows(even, x):
    return jnp.where(even, x[:NP], x[NP - 1 :])


def edge_rows(even, x):
    return jnp.where(even, x[:EDGE], x[ROWS - EDGE :])


def divergence_kernel(own_ref, mate_ref, ds_ref, qright_t_ref, div_ref, op_ref, level_ref, cross_ref):
    even = parity() == 0
    own, mate = own_ref[...], mate_ref[...]
    packs = [jnp.where(even, own, mate), jnp.where(even, mate, own)]
    parts = [[pack[NP * k : NP * k + NP] for k in range(7)] for pack in packs]
    low, high = packs[0][7 * NP :], packs[1][7 * NP :]
    sides = []
    for k in range(4):
        first, second = parts[0][k], parts[1][k]
        if k == 3:
            first, second = join_s(first), join_s(second)
        whole = chip_rows(first, second)
        sides.append(jnp.concatenate([(whole[0] + low[k])[None], whole[1:-1], (whole[-1] + high[k])[None]], axis=0))
    inv = 1.0 / sides[3]
    accel = [sides[d] * inv for d in range(3)]
    div, last, levels = [], [], []
    for layer in range(2):
        mass = parts[layer][3]
        at = (NP - 1) * layer
        sums = []
        terms = []
        for d in range(3):
            one = mass * parts[layer][4 + d]
            two = one * parts[layer][4 + d]
            op_ref[layer, d] = two
            sums.append(jnp.sum(rows(two), axis=0, keepdims=True))
            terms.append(one * accel[d][at : at + NP])
        op_ref[layer, 3] = mass_shift * mass
        sums.append(jnp.sum(rows(mass), axis=0, keepdims=True))
        sums.append(jnp.zeros((4, LANES), jnp.float32))
        levels.append(jnp.concatenate(sums, axis=0))
        div.append(d_a(terms[0], True) + d_s(terms[1], ds_ref[1]))
        last.append(rows(terms[2]))
    last = right_dot(jnp.concatenate(last, axis=0), qright_t_ref)
    div = [join_s(x + planes(last[64 * k : 64 * k + 64])) for k, x in enumerate(div)]
    whole = chip_rows(div[0], div[1])
    div_ref[...] = whole
    cross_ref[:EDGE] = edge_rows(even, whole)
    level = jnp.where(even, levels[0], levels[1])
    level_ref[...] = level
    cross_ref[EDGE] = level


def half_window(even, local, received):
    edge = received[:EDGE]
    low = jnp.concatenate([edge[:-1], (edge[-1] + local[0])[None], local[1:EDGE]], axis=0)
    high = jnp.concatenate([local[ROWS - EDGE : -1], (local[-1] + edge[0])[None], edge[1:]], axis=0)
    return jnp.where(even, low, high)


def own_of_half(even, x):
    return jnp.where(even, x[NP : 2 * NP], x[1 : NP + 1])


def inverse_levels(levels, spread_ref, lam_ref):
    result = []
    for level in levels:
        level = full_dot(level, spread_ref[...])
        denom = level[0:1] * lam_ref[0] + level[1:2] * lam_ref[1] + level[2:3] * lam_ref[2] + mass_shift * level[3:4]
        result.append(1.0 / denom)
    return result


def schwarz(half, even, inv_ref, sleft_ref, sright_ref, srback_ref, sback_ref, scratch_ref, sum_ref):
    wide = NP + 2
    scratch_ref[...] = half.reshape((2 * NP + 1) * NP, LANES)
    none = jnp.zeros((16 - wide, LANES), jnp.float32)
    columns = []
    for layer in range(2):
        at = (NP - 1) * NP * layer
        before = roll(scratch_ref[pl.ds(at + NP - 2, wide, stride=NP), :], NP, 1)
        after = roll(scratch_ref[pl.ds(at + 1, wide, stride=NP), :], -NP, 1)
        own = half[(NP - 1) * layer : (NP - 1) * layer + wide].reshape(wide * NP, LANES)
        columns.append(jnp.concatenate([own, before, none, after, none], axis=0))
    spectra = [left_dot(sleft_ref, x) for x in columns]
    spectra = [right_dot(x, sright_ref) for x in spectra]
    spectra = [x * inv_ref[MODES * k : MODES * k + MODES] for k, x in enumerate(spectra)]
    spectra = [modes_dot(x, srback_ref) for x in spectra]
    blocks = [left_dot(sback_ref, x) for x in spectra]
    z = []
    for layer in range(2):
        part = blocks[layer]
        sum_ref[layer] = part[:80]
        for block, (s, shift) in enumerate(((NP - 2, -NP), (NP - 1, -NP), (0, NP), (1, NP))):
            rows_at = pl.ds(s, wide, stride=NP)
            start = 80 + 16 * block
            sum_ref[layer, rows_at, :] = sum_ref[layer, rows_at, :] + roll(part[start : start + wide], shift, 1)
        z.append(sum_ref[layer].reshape(wide, NP, LANES))
    upper = jnp.concatenate([z[0][8:] + z[1][1:3], z[1][3:]], axis=0)
    lower = jnp.concatenate([z[0][:7], z[0][7:9] + z[1][:2]], axis=0)
    return jnp.where(even, upper, lower)


def join_sides(even, own, mate):
    first, second = jnp.where(even, own, mate), jnp.where(even, mate, own)
    return jnp.concatenate([first[:6], first[6:] + second[:3], second[3:]], axis=0)


def operate(v, op_ref, ds_ref, qright_ref, qright_t_ref):
    ds = ds_ref[...]
    layers = [v[(NP - 1) * k : (NP - 1) * k + NP] for k in range(2)]
    gq = right_dot(jnp.concatenate([rows(x) for x in layers], axis=0), qright_ref)
    hq = [op_ref[k, 2] * planes(gq[64 * k : 64 * k + 64]) for k in range(2)]
    back = right_dot(jnp.concatenate([rows(x) for x in hq], axis=0), qright_t_ref)
    parts = []
    for k, x in enumerate(layers):
        local = d_a(op_ref[k, 0] * d_a(x, False), True) + d_s(op_ref[k, 1] * d_s(x, ds[0]), ds[1])
        parts.append(join_s(local + (op_ref[k, 3] * x + planes(back[64 * k : 64 * k + 64]))))
    return chip_rows(parts[0], parts[1])


def first_smooth_kernel(div_ref, received_ref, level_ref, spread_ref, lam_ref, sleft_ref, sright_ref, srback_ref, sback_ref, half_ref, inv_ref, part_ref, scratch_ref, sum_ref):
    even = parity() == 0
    half = half_window(even, div_ref[...], received_ref)
    half_ref[...] = half
    other = received_ref[EDGE]
    own = level_ref[...]
    levels = [jnp.where(even, other, own), jnp.where(even, own, other)]
    for k, inv in enumerate(inverse_levels(levels, spread_ref, lam_ref)):
        inv_ref[MODES * k : MODES * k + MODES] = inv
    part_ref[...] = schwarz(half, even, inv_ref, sleft_ref, sright_ref, srback_ref, sback_ref, scratch_ref, sum_ref)


def smooth_kernel(step, before_ref, local_ref, received_ref, inv_ref, sleft_ref, sright_ref, srback_ref, sback_ref, own_image_ref, half_ref, part_ref, scratch_ref, sum_ref):
    even = parity() == 0
    image = half_window(even, local_ref[...], received_ref)
    half = before_ref[...] - step * image
    half_ref[...] = half
    part_ref[...] = schwarz(half, even, inv_ref, sleft_ref, sright_ref, srback_ref, sback_ref, scratch_ref, sum_ref)
    own_image_ref[...] = own_of_half(even, image)


def operator_kernel(part_ref, mate_ref, op_ref, ds_ref, qright_ref, qright_t_ref, v_ref, local_ref, cross_ref):
    even = parity() == 0
    v = join_sides(even, part_ref[...], mate_ref[...])
    v_ref[...] = v
    local = operate(v, op_ref, ds_ref, qright_ref, qright_t_ref)
    local_ref[...] = local
    cross_ref[...] = edge_rows(even, local)


def fold(parts):
    lane = lax.broadcasted_iota(jnp.int32, (NP, LANES), 1)
    parts = parts + [jnp.zeros((NP, LANES), jnp.float32)] * (ES - len(parts))
    for step in (8, 16, 32, 64):
        chosen = (lane & step) != 0
        parts = [
            jnp.where(chosen, b, a) + roll(jnp.where(chosen, a, b), step, 1)
            for a, b in zip(parts[::2], parts[1::2])
        ]
    return parts[0]


def early_kernel(ws_ref, div_ref, v0_ref, v1_ref, l0_ref, l1_ref, residual_ref, parts_ref):
    ws = ws_ref[...]
    l0, l1 = l0_ref[...], l1_ref[...]
    residual = div_ref[...] - STEPS[0] * l0 - STEPS[1] * l1
    residual_ref[...] = residual
    v0, v1 = v0_ref[...], v1_ref[...]
    for k, (left, right) in enumerate(((v0, l0), (v0, l1), (v1, l1), (v0, residual), (v1, residual))):
        parts_ref[k] = jnp.sum(left * right, axis=0) * ws


def last_sums_kernel(part_ref, mate_ref, op_ref, ds_ref, qright_ref, parts_ref, l0_ref, l1_ref, residual_ref, ws_ref, v_ref, sums_ref):
    even = parity() == 0
    v = join_sides(even, part_ref[...], mate_ref[...])
    v_ref[...] = v
    layers = [v[(NP - 1) * k : (NP - 1) * k + NP] for k in range(2)]
    gq = right_dot(jnp.concatenate([rows(x) for x in layers], axis=0), qright_ref)
    energy = None
    for k, x in enumerate(layers):
        ga, gs, gq_k = d_a(x, False), d_s(x, ds_ref[0]), planes(gq[64 * k : 64 * k + 64])
        part = op_ref[k, 0] * ga * ga + op_ref[k, 1] * gs * gs + op_ref[k, 2] * gq_k * gq_k + op_ref[k, 3] * x * x
        part = jnp.sum(part, axis=0)
        energy = part if energy is None else energy + part
    ws = ws_ref[...]
    new = [jnp.sum(x[...] * v, axis=0) * ws for x in (l0_ref, l1_ref, residual_ref)]
    p = [parts_ref[k] for k in range(5)]
    folded = fold([p[0], p[1], new[0], p[2], new[1], energy, p[3], p[4], new[2]])
    line = jnp.broadcast_to(jnp.sum(folded, axis=0, keepdims=True), (NP, LANES))
    for k in range(sums_ref.shape[0] // NP):
        sums_ref[NP * k : NP * k + NP] = line


def last_operator_kernel(v_ref, op_ref, ds_ref, qright_ref, qright_t_ref, local_ref, face_ref):
    even = parity() == 0
    local = operate(v_ref[...], op_ref, ds_ref, qright_ref, qright_t_ref)
    local_ref[...] = local
    face_ref[...] = jnp.where(even, local[0], local[-1])


def to_output(x, order_ref, scratch_ref, slot):
    scratch_ref[slot] = rows(x)
    by_s = [scratch_ref[slot, pl.ds(s, NP, stride=NP), :] for s in range(NP - 1)]
    tiles = []
    for tile in range(7):
        index, s = order_ref[0, tile], order_ref[1, tile]
        value = jnp.take_along_axis(by_s[0], index, axis=1)
        for k in range(1, NP - 1):
            value = jnp.where(s == k, jnp.take_along_axis(by_s[k], index, axis=1), value)
        tiles.append(value)
    return jnp.concatenate(tiles, axis=1)


def layout_kernel(face_ref, v0_ref, v1_ref, v2_ref, half_ref, w0_ref, w1_ref, local_ref, order_ref, out_ref, scratch_ref):
    even = parity() == 0
    face = face_ref[...]
    local = own_rows(even, local_ref[...])
    first = jnp.where(even, local[0] + face, local[0])
    last = jnp.where(even, local[-1], local[-1] + face)
    w2 = jnp.concatenate([first[None], local[1:-1], last[None]], axis=0)
    fields = [own_rows(even, x[...]) for x in (v0_ref, v1_ref, v2_ref)]
    fields.extend((own_of_half(even, half_ref[...]), w0_ref[...], w1_ref[...], w2))
    for k, x in enumerate(fields):
        out_ref[k] = to_output(x, order_ref, scratch_ref, k)


def combine_kernel(sums_ref, fields_ref, p_ref, r_ref):
    line = jnp.sum(sums_ref[...], axis=0, keepdims=True)
    for step in (4, 2, 1):
        line = line + roll(line, -step, 1)
    shape = (NP, LANES)
    h00, h01, h02, h11, h12, h22, g0, g1, g2 = [jnp.broadcast_to(line[:, NP * k : NP * k + 1], shape) for k in range(9)]
    scale = 1.0 / h00
    m1, m2, m0 = h01 * scale, h02 * scale, g0 * scale
    k11, k12, k22 = h11 - m1 * h01, h12 - m1 * h02, h22 - m2 * h02
    f1, f2 = g1 - m1 * g0, g2 - m2 * g0
    second = 1.0 / k11
    n2 = k12 * second
    c2 = (f2 - n2 * f1) / (k22 - n2 * k12)
    c1 = f1 * second - n2 * c2
    c0 = m0 - m1 * c1 - m2 * c2
    for tile in range(7):
        x = [fields_ref[k, :, LANES * tile : LANES * tile + LANES] for k in range(7)]
        p_ref[:, LANES * tile : LANES * tile + LANES] = (c0 + STEPS[0]) * x[0] + (c1 + STEPS[1]) * x[1] + c2 * x[2]
        r_ref[:, LANES * tile : LANES * tile + LANES] = x[3] - (c0 * x[4] + c1 * x[5] + c2 * x[6])


def call(kernel, shapes, *args, scratch=()):
    return pl.pallas_call(
        kernel,
        out_shape=[jax.ShapeDtypeStruct(shape, jnp.float32) for shape in shapes],
        in_specs=[pl.BlockSpec(memory_space=pltpu.VMEM)] * len(args),
        out_specs=[pl.BlockSpec(memory_space=pltpu.VMEM)] * len(shapes),
        scratch_shapes=scratch,
        compiler_params=PARAMS,
    )(*args)


SMOOTH_SCRATCH = (
    pltpu.VMEM(((2 * NP + 1) * NP, LANES), jnp.float32),
    pltpu.VMEM((2, (NP + 2) * NP, LANES), jnp.float32),
)


def call_forcing(*args):
    shapes = [(7 * NP, NP, LANES), (4, NP, LANES)]
    scratch = [pltpu.SMEM(args[0].shape, jnp.int32)]
    scratch.extend(pltpu.VMEM(x.shape, x.dtype) for x in args[1:])
    scratch.append(pltpu.SemaphoreType.DMA((len(args),)))
    return pl.pallas_call(
        forcing_kernel,
        out_shape=[jax.ShapeDtypeStruct(shape, jnp.float32) for shape in shapes],
        in_specs=[pl.BlockSpec(memory_space=pltpu.HBM)] * len(args),
        out_specs=[pl.BlockSpec(memory_space=pltpu.VMEM)] * len(shapes),
        scratch_shapes=scratch,
        compiler_params=pltpu.CompilerParams(vmem_limit_bytes=FORCING_VMEM),
    )(*args)


FORCING_TABLES = ("w3", "wmass", "ds", "dq", "jright", "jslope", "jright_t", "jleft", "jleft_a", "jleft_s", "jleft_t", "wfine")


def team_groups(count):
    return [[2 * c + side for c in range(count // 2)] for side in range(2)]


def shards(velocity, conv_past, metric, jacobian, element_slot):
    count = lax.axis_size("dom")
    t = {key: jnp.asarray(value) for key, value in TAB.items()}
    field = (NP, NP, LANES)
    chip = (ROWS, NP, LANES)
    half_shape = (2 * NP + 1, NP, LANES)
    edge = (EDGE, NP, LANES)
    pack, cross = call_forcing(
        element_slot, velocity, conv_past, metric, jacobian, *(t[key] for key in FORCING_TABLES)
    )
    cross = swap_cross(cross, count)
    pack = pl.pallas_call(
        stage_kernel,
        out_shape=jax.ShapeDtypeStruct(pack.shape, jnp.float32),
        in_specs=[pl.BlockSpec(memory_space=pltpu.HBM)],
        out_specs=pl.BlockSpec(memory_space=pltpu.VMEM),
        scratch_shapes=[pltpu.SemaphoreType.DMA(())],
        compiler_params=PARAMS,
    )(pack)
    (own,) = call(pair_kernel, [(7 * NP + 4, NP, LANES)], pack, cross)
    mate = swap_inner(own, count)
    div, op, level, cross = call(
        divergence_kernel,
        [chip, (2, 4) + field, (NP, LANES), (EDGE + 1, NP, LANES)],
        own, mate, t["ds"], t["qright_t"],
    )
    solve = (t["sleft"], t["sright"], t["srback"], t["sback"])
    tables = (op, t["ds"], t["qright"], t["qright_t"])
    half, inv, part = call(
        first_smooth_kernel,
        [half_shape, (2 * MODES, ES * (NP + 2)), edge],
        div, swap_cross(cross, count), level, t["spread"], t["lam"], *solve,
        scratch=SMOOTH_SCRATCH,
    )
    vectors, locals_, images = [], [], []
    for step in STEPS:
        v, local, cross = call(
            operator_kernel, [chip, chip, edge], part, swap_inner(part, count), *tables
        )
        image, half, part = call(
            functools.partial(smooth_kernel, step),
            [field, half_shape, edge],
            half, local, swap_cross(cross, count), inv, *solve,
            scratch=SMOOTH_SCRATCH,
        )
        vectors.append(v)
        locals_.append(local)
        images.append(image)
    residual, parts = call(
        early_kernel, [chip, (5, NP, LANES)], t["ws"], div, *vectors, *locals_
    )
    v, sums = call(
        last_sums_kernel,
        [chip, (count // 2, LANES)],
        part, swap_inner(part, count), op, t["ds"], t["qright"], parts, *locals_, residual, t["ws"],
    )
    sums = lax.all_to_all(sums, "dom", 0, 0, tiled=True, axis_index_groups=team_groups(count))
    local, face = call(last_operator_kernel, [chip, (NP, LANES)], v, *tables)
    (fields,) = call(
        layout_kernel,
        [(7, NP, 896)],
        swap_cross(face, count), *vectors, v, half, *images, local, t["order"],
        scratch=[pltpu.VMEM((7, NP * NP, LANES), jnp.float32)],
    )
    return tuple(call(combine_kernel, [(NP, 896), (NP, 896)], sums, fields))


def solution(mesh):
    return jax.shard_map(
        shards,
        mesh=mesh,
        in_specs=(
            P(None, None, "dom", None),
            P(None, None, "dom", None),
            P(None, "dom", None),
            P("dom", None),
            P("dom"),
        ),
        out_specs=(P("dom", None), P("dom", None)),
        check_vma=False,
    )
```

```python
import functools

import jax
import jax.numpy as jnp
import numpy as np
from jax import lax
from jax.experimental import pallas as pl
from jax.experimental.pallas import tpu as pltpu
from jax.sharding import PartitionSpec as P

NP = 8
NF = 12
ES = 16
LANES = 128
time_step = 0.25
viscosity = 0.05
mass_shift = 0.001
STEPS = (0.45, 0.3)
VMEM = 48 * 1024 * 1024
FORCING_VMEM = 56 * 1024 * 1024
ROWS = 2 * NP - 1
EDGE = NP + 1
MODES = 112


def legendre_pair(points, order):
    before = np.ones(points.shape)
    current = points * 1.0
    for level in range(2, order + 1):
        nextone = ((2 * level - 1) * points * current - (level - 1) * before) / level
        before = current
        current = nextone
    return (current, before)


def jacobi_eigen(matrix):
    size = matrix.shape[0]
    work = matrix * 1.0
    vectors = np.eye(size)
    for sweep in range(30):
        for first in range(size - 1):
            for second in range(first + 1, size):
                off = float(work[first, second])
                if abs(off) > 1e-300:
                    tau = (float(work[second, second]) - float(work[first, first])) / (2.0 * off)
                    if tau >= 0.0:
                        tangent = 1.0 / (tau + (1.0 + tau * tau) ** 0.5)
                    else:
                        tangent = -1.0 / (-tau + (1.0 + tau * tau) ** 0.5)
                    cosine = 1.0 / (1.0 + tangent * tangent) ** 0.5
                    sine = tangent * cosine
                    rotation = np.eye(size)
                    rotation[first, first] = cosine
                    rotation[second, second] = cosine
                    rotation[first, second] = sine
                    rotation[second, first] = -sine
                    work = rotation.T @ work @ rotation
                    vectors = vectors @ rotation
    diagonal_index = np.arange(size)
    return (work[diagonal_index, diagonal_index], vectors)


def base_tables(points_edge, points_fine):
    degree = points_edge - 1
    points = -np.cos(np.pi * np.arange(points_edge) / degree)
    for sweep in range(100):
        top, below = legendre_pair(points, degree)
        points = points - (points * top - below) / (points_edge * top)
    top, below = legendre_pair(points, degree)
    weight_gll = 2.0 / (degree * points_edge * top**2)
    spacing = points[:, None] - points[None, :] + np.eye(points_edge)
    barycentric = 1.0 / np.prod(spacing, axis=1)
    derivative = barycentric[None, :] / barycentric[:, None] / spacing
    derivative = derivative * (1.0 - np.eye(points_edge))
    derivative = derivative - np.eye(points_edge) * derivative.sum(axis=1)[:, None]
    fine_points = np.cos(np.pi * (np.arange(points_fine) + 0.75) / (points_fine + 0.5))
    for sweep in range(100):
        top, below = legendre_pair(fine_points, points_fine)
        slope = points_fine * (fine_points * top - below) / (fine_points * fine_points - 1.0)
        fine_points = fine_points - top / slope
    top, below = legendre_pair(fine_points, points_fine)
    slope = points_fine * (fine_points * top - below) / (fine_points * fine_points - 1.0)
    fine_weight = 2.0 / ((1.0 - fine_points * fine_points) * slope * slope)
    fine_points = fine_points[::-1]
    fine_weight = fine_weight[::-1]
    interpolate = np.ones((points_fine, points_edge))
    for column in range(points_edge):
        for other in range(points_edge):
            if other != column:
                interpolate[:, column] = (
                    interpolate[:, column]
                    * (fine_points - points[other])
                    / (points[column] - points[other])
                )
    stiffness = derivative.T @ (weight_gll[:, None] * derivative)
    extent = 3 * degree + 1
    joined_stiff = np.zeros((extent, extent))
    joined_mass = np.zeros(extent)
    for segment in range(3):
        offset = segment * degree
        joined_stiff[offset : offset + points_edge, offset : offset + points_edge] += stiffness
        joined_mass[offset : offset + points_edge] += weight_gll
    low = degree - 1
    high = 2 * degree + 2
    root_mass = np.sqrt(joined_mass[low:high])
    scaled = joined_stiff[low:high, low:high] / root_mass[:, None] / root_mass[None, :]
    scaled = 0.5 * (scaled + scaled.T)
    eigen_values, eigen_vectors = jacobi_eigen(scaled)
    solve_mat = eigen_vectors / root_mass[:, None]
    breadth = high - low
    return dict(
        derivative=derivative,
        interpolate=interpolate,
        weight=weight_gll,
        fine_weight=fine_weight,
        solve=solve_mat,
        eigen=eigen_values,
    )


def f32(value):
    return np.ascontiguousarray(value, dtype=np.float32)


def halves(value):
    value = np.asarray(value, dtype=np.float32)
    high = value.astype(jnp.bfloat16)
    rest = (value - high.astype(np.float32)).astype(jnp.bfloat16)
    return high, rest


def for_left(value):
    high, rest = halves(value)
    return np.concatenate([high, rest, high], axis=1)


def for_right(value):
    high, rest = halves(value)
    return np.concatenate([high, rest, high], axis=0)


def by_modes_right(value):
    a, b, c = thirds(by_modes(value, 0))
    parts = (c, b, a, b, a, a)
    return np.concatenate([x[:LANES] for x in parts] + [x[LANES:] for x in parts])


def thirds(value):
    value = np.asarray(value, dtype=np.float32)
    pieces = []
    for k in range(3):
        pieces.append(value.astype(jnp.bfloat16))
        value = value - pieces[-1].astype(np.float32)
    return pieces


def for_right_full(value):
    a, b, c = thirds(value)
    return np.concatenate([c, b, a, b, a, a], axis=0)


def for_left_full(value):
    a, b, c = thirds(value)
    return np.concatenate([c, b, a, b, a, a], axis=1)


def pair(value):
    return np.stack(halves(value))


def by_modes(value, axis):
    at = np.arange(ES * (NP + 2))
    order = np.concatenate([at[at % (NP + 2) < NP], at[at % (NP + 2) >= NP]])
    return np.take(value, order, axis=axis)


def make_tables():
    base = base_tables(NP, NF)
    deriv, interp, solve, eigen = base["derivative"], base["interpolate"], base["solve"], base["eigen"]
    w, wf = base["weight"], base["fine_weight"]
    out = {}
    index = np.arange(NP)

    def sublane(matrix):
        rows = [matrix[index, (index + shift) % NP] for shift in range(NP)]
        return f32(np.broadcast_to(np.stack(rows)[:, :, None], (NP, NP, LANES)))

    def lane(matrix):
        rows = []
        for shift in range(-(NP - 1), NP):
            row = np.zeros(NP)
            for q in range(NP):
                if 0 <= q + shift < NP:
                    row[q] = matrix[q, q + shift]
            rows.append(np.tile(row, ES))
        return f32(np.broadcast_to(np.stack(rows)[:, None, :], (2 * NP - 1, NP, LANES)))

    out["ds"] = np.stack([sublane(deriv), sublane(deriv.T)])
    out["dq"] = np.stack([lane(deriv), lane(deriv.T)])
    out["qright"] = for_right_full(np.kron(np.eye(ES), deriv.T))
    out["qright_t"] = for_right_full(np.kron(np.eye(ES), deriv))
    out["w3"] = f32(np.einsum("a,s,q->asq", w, w, w).reshape(1, 512))
    out["wmass"] = f32(np.tile(np.einsum("a,s,q->asq", w, w, w), (1, 1, ES)))
    both = interp @ deriv
    pad = np.zeros((16 - NF, NP))
    line = np.concatenate([interp, pad])
    slope = np.concatenate([both, pad])
    out["jright"] = for_right_full(np.kron(np.eye(ES), line.T))
    out["jslope"] = for_right_full(np.kron(np.eye(ES), slope.T))
    out["jright_t"] = for_right_full(np.kron(np.eye(ES), line))
    out["jleft"] = for_left_full(np.kron(interp, interp))
    out["jleft_a"] = for_left_full(np.kron(both, interp))
    out["jleft_s"] = for_left_full(np.kron(interp, both))
    out["jleft_t"] = for_left_full(np.kron(interp, interp).T)
    wide_wf = np.concatenate([wf, np.zeros(16 - NF)])
    out["wfine"] = f32(np.kron(np.kron(wf, wf)[:, None], np.tile(wide_wf, ES)[None, :]))
    at = np.arange(7 * LANES)
    element, within = at // 56, at % 56
    order = np.stack([element * NP + within % NP, within // NP]).reshape(2, 7, 1, LANES)
    out["order"] = np.ascontiguousarray(np.broadcast_to(order, (2, 7, NP, LANES)), dtype=np.int32)
    wide = NP + 2
    left = np.zeros((MODES, 112))
    back = np.zeros((144, MODES))
    at = np.arange(wide)
    for i in range(wide):
        for j in range(wide):
            row = i * wide + j
            inside = np.outer(solve[:, i], solve[1:-1, j]).reshape(80)
            left[row, :80] = inside
            left[row, 80 + at] = solve[:, i] * solve[0, j]
            left[row, 96 + at] = solve[:, i] * solve[wide - 1, j]
            back[:80, row] = inside
            for block, s in enumerate((0, 1, wide - 2, wide - 1)):
                back[80 + 16 * block + at, row] = solve[:, i] * solve[s, j]
    out["sleft"] = for_left_full(left)
    out["sback"] = for_left_full(back)
    out["sright"] = for_right_full(by_modes(np.kron(np.eye(ES), solve[1:-1, :]), 1))
    out["srback"] = by_modes_right(np.kron(np.eye(ES), solve[1:-1, :].T))
    out["spread"] = f32(by_modes(np.kron(np.eye(ES), np.ones((NP, wide))), 1) / 8.0)
    lam_a = np.zeros((MODES, 1))
    lam_s = np.zeros((MODES, 1))
    lam_a[:100, 0] = np.repeat(eigen, wide)
    lam_s[:100, 0] = np.tile(eigen, wide)
    lam_q = by_modes(np.tile(eigen, ES)[None, :], 1)
    full = (MODES, ES * wide)
    out["lam"] = f32(np.stack([np.broadcast_to(lam_a, full), np.broadcast_to(lam_s, full), np.broadcast_to(lam_q, full)]))
    half = np.ones(NP)
    half[0] = half[-1] = 0.5
    out["ws"] = f32(np.broadcast_to(half[:, None], (NP, LANES)))
    return out


TAB = make_tables()
DERIV = [[float(x) for x in row] for row in base_tables(NP, NF)["derivative"].astype(np.float32)]
PARAMS = pltpu.CompilerParams(vmem_limit_bytes=VMEM)


def full_dot(left, right):
    return jnp.dot(left, right, precision=lax.Precision.HIGHEST, preferred_element_type=jnp.float32)


def short_dot(left, right):
    return jnp.dot(left, right, preferred_element_type=jnp.float32)


def split_once(x):
    high = x.astype(jnp.bfloat16)
    return high, x - high.astype(jnp.float32)


def split(x):
    high = x.astype(jnp.bfloat16)
    return high, (x - high.astype(jnp.float32)).astype(jnp.bfloat16)


def left_dot(table_ref, x):
    high, rest = split(x)
    return short_dot(table_ref[...], jnp.concatenate([high, high, rest], axis=0))


def right_dot(x, table_ref):
    high, rest = split(x)
    return short_dot(jnp.concatenate([high, high, rest], axis=1), table_ref[...])


def full_pieces(x):
    a, rest = split_once(x)
    b, rest = split_once(rest)
    c = rest.astype(jnp.bfloat16)
    return [a, b, c, a, b, a]


def full_right_dot(x, table_ref):
    return short_dot(jnp.concatenate(full_pieces(x), axis=1), table_ref[...])


def full_left_dot(table_ref, x):
    return short_dot(table_ref[...], jnp.concatenate(full_pieces(x), axis=0))


def modes_dot(x, table_ref):
    parts = full_pieces(x)
    whole = [y[:, :LANES] for y in parts] + [y[:, LANES:] for y in parts]
    return short_dot(jnp.concatenate(whole, axis=1), table_ref[...])


def pair_dot(x, table_ref):
    high, rest = split(x)
    return short_dot(high, table_ref[0]) + (short_dot(high, table_ref[1]) + short_dot(rest, table_ref[0]))


def roll(x, shift, axis):
    return pltpu.roll(x, shift % x.shape[axis], axis)


def d_a(x, transposed):
    rows = []
    for a in range(NP):
        total = None
        for b in range(NP):
            term = (DERIV[b][a] if transposed else DERIV[a][b]) * x[b]
            total = term if total is None else total + term
        rows.append(total)
    return jnp.stack(rows)


def d_s(x, coef):
    total = coef[0][None] * x
    for shift in range(1, NP):
        total = total + coef[shift][None] * roll(x, -shift, 1)
    return total


def d_q(x, coef):
    total = coef[NP - 1][None] * x
    for shift in range(1, NP):
        total = total + coef[NP - 1 + shift][None] * roll(x, -shift, 2)
        total = total + coef[NP - 1 - shift][None] * roll(x, shift, 2)
    return total


def gradient(x, ds, dq):
    return d_a(x, False), d_s(x, ds[0]), d_q(x, dq[0])


def gradient_t(xa, xs, xq, ds, dq):
    return d_a(xa, True) + d_s(xs, ds[1]) + d_q(xq, dq[1])


def join_s(x):
    s = lax.broadcasted_iota(jnp.int32, x.shape, 1)
    from_before = roll(roll(x, NP, 2), 1, 1)
    from_after = roll(roll(x, -NP, 2), -1, 1)
    zero = jnp.zeros_like(x)
    return x + jnp.where(s == 0, from_before, jnp.where(s == NP - 1, from_after, zero))


def parity():
    return lax.rem(lax.axis_index("dom"), 2)


def swap_inner(x, count):
    return lax.ppermute(x, "dom", [(i, i ^ 1) for i in range(count)])


def swap_cross(x, count):
    pairs = [(i, (i + 1) % count if i % 2 else (i - 1) % count) for i in range(count)]
    return lax.ppermute(x, "dom", pairs)


def to_lanes(x):
    shape = (x.shape[0], NP, LANES)
    lane = lax.broadcasted_iota(jnp.int32, shape, 2)
    pieces = []
    for tile in range(4):
        first = x[:, :8, tile * LANES : (tile + 1) * LANES]
        second = x[:, 8:, tile * LANES : (tile + 1) * LANES]
        pieces.append(jnp.where(lane < 64, first, roll(second, 64, 2)))
        pieces.append(jnp.where(lane < 64, roll(first, 64, 2), second))
    y = jnp.stack(pieces, axis=1).reshape(x.shape[0] * NP, NP, LANES)
    sub = lax.broadcasted_iota(jnp.int32, y.shape, 1)
    lane = lax.broadcasted_iota(jnp.int32, y.shape, 2)
    for bit in range(3):
        step = 1 << bit
        in_sub = (sub & step) != 0
        in_lane = (lane & (step * 8)) != 0
        up = roll(roll(y, -step, 1), step * 8, 2)
        down = roll(roll(y, step, 1), -step * 8, 2)
        y = jnp.where(in_sub == in_lane, y, jnp.where(in_lane, up, down))
    return y.reshape(x.shape[0], NP, NP, LANES)


def rows(x):
    return x.reshape(NP * NP, LANES)


def planes(x):
    return x.reshape(NP, NP, LANES)


def take_lanes(x, index):
    flat = x.reshape(-1, LANES)
    tiled = jnp.broadcast_to(index[None], x.shape).reshape(-1, LANES)
    return jnp.take_along_axis(flat, tiled, axis=1).reshape(x.shape)


def forcing_kernel(slot_in, vel_in, past_in, metric_in, jac_in, w3_in, wmass_in, ds_in, dq_in, jright_in, jslope_in, jright_t_in, jleft_in, jleft_a_in, jleft_s_in, jleft_t_in, wfine_in, pack_ref, cross_ref, slot_ref, vel_ref, past_ref, metric_ref, jac_ref, w3_ref, wmass_ref, ds_ref, dq_ref, jright_ref, jslope_ref, jright_t_ref, jleft_ref, jleft_a_ref, jleft_s_ref, jleft_t_ref, wfine_ref, sems):
    sources = (slot_in, vel_in, past_in, metric_in, jac_in, w3_in, wmass_in, ds_in, dq_in, jright_in, jslope_in, jright_t_in, jleft_in, jleft_a_in, jleft_s_in, jleft_t_in, wfine_in)
    targets = (slot_ref, vel_ref, past_ref, metric_ref, jac_ref, w3_ref, wmass_ref, ds_ref, dq_ref, jright_ref, jslope_ref, jright_t_ref, jleft_ref, jleft_a_ref, jleft_s_ref, jleft_t_ref, wfine_ref)
    copies = [pltpu.make_async_copy(x, y, sems.at[k]) for k, (x, y) in enumerate(zip(sources, targets))]
    for copy in copies:
        copy.start()
    for copy in copies[:6]:
        copy.wait()
    even = parity() == 0
    jac = jac_ref[...]
    new, mid, old = vel_ref[0], vel_ref[1], vel_ref[2]
    guess = 3.0 * (new - mid) + old
    direct = (jac * w3_ref[...])[None] * (-10.0 * new + 16.0 * mid - 6.0 * old) + 3.0 * past_ref[0] - past_ref[1]
    lanes = to_lanes(jnp.concatenate([new, guess, direct, metric_ref[...], jac[None]], axis=0))
    new, guess, direct, metric, jac = lanes[0:3], lanes[3:6], lanes[6:9], lanes[9:12], lanes[12]
    for copy in copies[6:]:
        copy.wait()
    ds, dq = ds_ref[...], dq_ref[...]
    moved = [rows(new[i]) for i in range(3)]
    plain = moved + [rows(jac)] + [rows(new[d] * metric[d]) for d in range(3)]
    wide = full_right_dot(jnp.concatenate(plain, axis=0), jright_ref)
    slope = full_right_dot(jnp.concatenate(moved, axis=0), jslope_ref)
    scale = full_left_dot(jleft_ref, wide[192:256]) * wfine_ref[...]
    carry = [full_left_dot(jleft_ref, wide[256 + 64 * d : 320 + 64 * d]) for d in range(3)]
    products = []
    for i in range(3):
        part = wide[64 * i : 64 * i + 64]
        total = carry[0] * full_left_dot(jleft_a_ref, part) + carry[1] * full_left_dot(jleft_s_ref, part)
        total = total + carry[2] * full_left_dot(jleft_ref, slope[64 * i : 64 * i + 64])
        products.append(scale * total)
    coarse = full_left_dot(jleft_t_ref, jnp.concatenate(products, axis=1))
    coarse = full_right_dot(jnp.concatenate([coarse[:, 256 * i : 256 * i + 256] for i in range(3)], axis=0), jright_t_ref)
    mass = jac * wmass_ref[...]
    factor = [mass * metric[d] * metric[d] for d in range(3)]
    result = []
    for i in range(3):
        ga, gs, gq = gradient(guess[i], ds, dq)
        stiff = gradient_t(factor[0] * ga, factor[1] * gs, factor[2] * gq, ds, dq)
        result.append(direct[i] - 3.0 * planes(coarse[64 * i : 64 * i + 64]) - viscosity * stiff)
    result.extend([mass, metric[0], metric[1], metric[2]])
    lane = lax.broadcasted_iota(jnp.int32, (NP, LANES), 1)
    index = jnp.zeros((NP, LANES), jnp.int32)
    for e in range(ES):
        index = jnp.where((lane >> 3) == slot_ref[e], e * NP, index)
    index = index + (lane & 7)
    result = [take_lanes(x, index) for x in result]
    for k in range(4):
        joined = join_s(result[k])
        cross_ref[k] = jnp.where(even, joined[0], joined[NP - 1])
        pack_ref[NP * k : NP * k + NP] = joined if k < 3 else result[k]
    for k in range(4, 7):
        pack_ref[NP * k : NP * k + NP] = result[k]


def stage_kernel(pack_ref, out_ref, sem):
    copy = pltpu.make_async_copy(pack_ref, out_ref, sem)
    copy.start()
    copy.wait()


def pair_kernel(pack_ref, cross_in, out_ref):
    out_ref[: 7 * NP] = pack_ref[...]
    out_ref[7 * NP :] = cross_in[...]


def chip_rows(first, second):
    return jnp.concatenate([first[:-1], (first[-1] + second[0])[None], second[1:]], axis=0)


def own_rows(even, x):
    return jnp.where(even, x[:NP], x[NP - 1 :])


def edge_rows(even, x):
    return jnp.where(even, x[:EDGE], x[ROWS - EDGE :])


def divergence_kernel(own_ref, mate_ref, ds_ref, qright_t_ref, div_ref, op_ref, level_ref, cross_ref):
    even = parity() == 0
    own, mate = own_ref[...], mate_ref[...]
    packs = [jnp.where(even, own, mate), jnp.where(even, mate, own)]
    parts = [[pack[NP * k : NP * k + NP] for k in range(7)] for pack in packs]
    low, high = packs[0][7 * NP :], packs[1][7 * NP :]
    sides = []
    for k in range(4):
        first, second = parts[0][k], parts[1][k]
        if k == 3:
            first, second = join_s(first), join_s(second)
        whole = chip_rows(first, second)
        sides.append(jnp.concatenate([(whole[0] + low[k])[None], whole[1:-1], (whole[-1] + high[k])[None]], axis=0))
    inv = 1.0 / sides[3]
    accel = [sides[d] * inv for d in range(3)]
    div, last, levels = [], [], []
    for layer in range(2):
        mass = parts[layer][3]
        at = (NP - 1) * layer
        sums = []
        terms = []
        for d in range(3):
            one = mass * parts[layer][4 + d]
            two = one * parts[layer][4 + d]
            op_ref[layer, d] = two
            sums.append(jnp.sum(rows(two), axis=0, keepdims=True))
            terms.append(one * accel[d][at : at + NP])
        op_ref[layer, 3] = mass_shift * mass
        sums.append(jnp.sum(rows(mass), axis=0, keepdims=True))
        sums.append(jnp.zeros((4, LANES), jnp.float32))
        levels.append(jnp.concatenate(sums, axis=0))
        div.append(d_a(terms[0], True) + d_s(terms[1], ds_ref[1]))
        last.append(rows(terms[2]))
    last = full_right_dot(jnp.concatenate(last, axis=0), qright_t_ref)
    div = [join_s(x + planes(last[64 * k : 64 * k + 64])) for k, x in enumerate(div)]
    whole = chip_rows(div[0], div[1])
    div_ref[...] = whole
    cross_ref[:EDGE] = edge_rows(even, whole)
    level = jnp.where(even, levels[0], levels[1])
    level_ref[...] = level
    cross_ref[EDGE] = level


def half_window(even, local, received):
    edge = received[:EDGE]
    low = jnp.concatenate([edge[:-1], (edge[-1] + local[0])[None], local[1:EDGE]], axis=0)
    high = jnp.concatenate([local[ROWS - EDGE : -1], (local[-1] + edge[0])[None], edge[1:]], axis=0)
    return jnp.where(even, low, high)


def own_of_half(even, x):
    return jnp.where(even, x[NP : 2 * NP], x[1 : NP + 1])


def inverse_levels(levels, spread_ref, lam_ref):
    result = []
    for level in levels:
        level = full_dot(level, spread_ref[...])
        denom = level[0:1] * lam_ref[0] + level[1:2] * lam_ref[1] + level[2:3] * lam_ref[2] + mass_shift * level[3:4]
        result.append(1.0 / denom)
    return result


def schwarz(half, even, inv_ref, sleft_ref, sright_ref, srback_ref, sback_ref, scratch_ref, sum_ref):
    wide = NP + 2
    scratch_ref[...] = half.reshape((2 * NP + 1) * NP, LANES)
    none = jnp.zeros((16 - wide, LANES), jnp.float32)
    columns = []
    for layer in range(2):
        at = (NP - 1) * NP * layer
        before = roll(scratch_ref[pl.ds(at + NP - 2, wide, stride=NP), :], NP, 1)
        after = roll(scratch_ref[pl.ds(at + 1, wide, stride=NP), :], -NP, 1)
        own = half[(NP - 1) * layer : (NP - 1) * layer + wide].reshape(wide * NP, LANES)
        columns.append(jnp.concatenate([own, before, none, after, none], axis=0))
    spectra = [full_left_dot(sleft_ref, x) for x in columns]
    spectra = [full_right_dot(x, sright_ref) for x in spectra]
    spectra = [x * inv_ref[MODES * k : MODES * k + MODES] for k, x in enumerate(spectra)]
    spectra = [modes_dot(x, srback_ref) for x in spectra]
    blocks = [full_left_dot(sback_ref, x) for x in spectra]
    z = []
    for layer in range(2):
        part = blocks[layer]
        sum_ref[layer] = part[:80]
        for block, (s, shift) in enumerate(((NP - 2, -NP), (NP - 1, -NP), (0, NP), (1, NP))):
            rows_at = pl.ds(s, wide, stride=NP)
            start = 80 + 16 * block
            sum_ref[layer, rows_at, :] = sum_ref[layer, rows_at, :] + roll(part[start : start + wide], shift, 1)
        z.append(sum_ref[layer].reshape(wide, NP, LANES))
    upper = jnp.concatenate([z[0][8:] + z[1][1:3], z[1][3:]], axis=0)
    lower = jnp.concatenate([z[0][:7], z[0][7:9] + z[1][:2]], axis=0)
    return jnp.where(even, upper, lower)


def join_sides(even, own, mate):
    first, second = jnp.where(even, own, mate), jnp.where(even, mate, own)
    return jnp.concatenate([first[:6], first[6:] + second[:3], second[3:]], axis=0)


def operate(v, op_ref, ds_ref, qright_ref, qright_t_ref):
    ds = ds_ref[...]
    layers = [v[(NP - 1) * k : (NP - 1) * k + NP] for k in range(2)]
    gq = full_right_dot(jnp.concatenate([rows(x) for x in layers], axis=0), qright_ref)
    hq = [op_ref[k, 2] * planes(gq[64 * k : 64 * k + 64]) for k in range(2)]
    back = full_right_dot(jnp.concatenate([rows(x) for x in hq], axis=0), qright_t_ref)
    parts = []
    for k, x in enumerate(layers):
        local = d_a(op_ref[k, 0] * d_a(x, False), True) + d_s(op_ref[k, 1] * d_s(x, ds[0]), ds[1])
        parts.append(join_s(local + (op_ref[k, 3] * x + planes(back[64 * k : 64 * k + 64]))))
    return chip_rows(parts[0], parts[1])


def first_smooth_kernel(div_ref, received_ref, level_ref, spread_ref, lam_ref, sleft_ref, sright_ref, srback_ref, sback_ref, half_ref, inv_ref, part_ref, scratch_ref, sum_ref):
    even = parity() == 0
    half = half_window(even, div_ref[...], received_ref)
    half_ref[...] = half
    other = received_ref[EDGE]
    own = level_ref[...]
    levels = [jnp.where(even, other, own), jnp.where(even, own, other)]
    for k, inv in enumerate(inverse_levels(levels, spread_ref, lam_ref)):
        inv_ref[MODES * k : MODES * k + MODES] = inv
    part_ref[...] = schwarz(half, even, inv_ref, sleft_ref, sright_ref, srback_ref, sback_ref, scratch_ref, sum_ref)


def smooth_kernel(step, before_ref, local_ref, received_ref, inv_ref, sleft_ref, sright_ref, srback_ref, sback_ref, own_image_ref, half_ref, part_ref, scratch_ref, sum_ref):
    even = parity() == 0
    image = half_window(even, local_ref[...], received_ref)
    half = before_ref[...] - step * image
    half_ref[...] = half
    part_ref[...] = schwarz(half, even, inv_ref, sleft_ref, sright_ref, srback_ref, sback_ref, scratch_ref, sum_ref)
    own_image_ref[...] = own_of_half(even, image)


def operator_kernel(part_ref, mate_ref, op_ref, ds_ref, qright_ref, qright_t_ref, v_ref, local_ref, cross_ref):
    even = parity() == 0
    v = join_sides(even, part_ref[...], mate_ref[...])
    v_ref[...] = v
    local = operate(v, op_ref, ds_ref, qright_ref, qright_t_ref)
    local_ref[...] = local
    cross_ref[...] = edge_rows(even, local)


def fold(parts):
    lane = lax.broadcasted_iota(jnp.int32, (NP, LANES), 1)
    parts = parts + [jnp.zeros((NP, LANES), jnp.float32)] * (ES - len(parts))
    for step in (8, 16, 32, 64):
        chosen = (lane & step) != 0
        parts = [
            jnp.where(chosen, b, a) + roll(jnp.where(chosen, a, b), step, 1)
            for a, b in zip(parts[::2], parts[1::2])
        ]
    return parts[0]


def early_kernel(ws_ref, div_ref, v0_ref, v1_ref, l0_ref, l1_ref, residual_ref, parts_ref):
    ws = ws_ref[...]
    l0, l1 = l0_ref[...], l1_ref[...]
    residual = div_ref[...] - STEPS[0] * l0 - STEPS[1] * l1
    residual_ref[...] = residual
    v0, v1 = v0_ref[...], v1_ref[...]
    for k, (left, right) in enumerate(((v0, l0), (v0, l1), (v1, l1), (v0, residual), (v1, residual))):
        parts_ref[k] = jnp.sum(left * right, axis=0) * ws


def last_sums_kernel(part_ref, mate_ref, op_ref, ds_ref, qright_ref, parts_ref, l0_ref, l1_ref, residual_ref, ws_ref, v_ref, sums_ref):
    even = parity() == 0
    v = join_sides(even, part_ref[...], mate_ref[...])
    v_ref[...] = v
    layers = [v[(NP - 1) * k : (NP - 1) * k + NP] for k in range(2)]
    gq = full_right_dot(jnp.concatenate([rows(x) for x in layers], axis=0), qright_ref)
    energy = None
    for k, x in enumerate(layers):
        ga, gs, gq_k = d_a(x, False), d_s(x, ds_ref[0]), planes(gq[64 * k : 64 * k + 64])
        part = op_ref[k, 0] * ga * ga + op_ref[k, 1] * gs * gs + op_ref[k, 2] * gq_k * gq_k + op_ref[k, 3] * x * x
        part = jnp.sum(part, axis=0)
        energy = part if energy is None else energy + part
    ws = ws_ref[...]
    new = [jnp.sum(x[...] * v, axis=0) * ws for x in (l0_ref, l1_ref, residual_ref)]
    p = [parts_ref[k] for k in range(5)]
    folded = fold([p[0], p[1], new[0], p[2], new[1], energy, p[3], p[4], new[2]])
    line = jnp.broadcast_to(jnp.sum(folded, axis=0, keepdims=True), (NP, LANES))
    for k in range(sums_ref.shape[0] // NP):
        sums_ref[NP * k : NP * k + NP] = line


def last_operator_kernel(v_ref, op_ref, ds_ref, qright_ref, qright_t_ref, local_ref, face_ref):
    even = parity() == 0
    local = operate(v_ref[...], op_ref, ds_ref, qright_ref, qright_t_ref)
    local_ref[...] = local
    face_ref[...] = jnp.where(even, local[0], local[-1])


def to_output(x, order_ref, scratch_ref, slot):
    scratch_ref[slot] = rows(x)
    by_s = [scratch_ref[slot, pl.ds(s, NP, stride=NP), :] for s in range(NP - 1)]
    tiles = []
    for tile in range(7):
        index, s = order_ref[0, tile], order_ref[1, tile]
        value = jnp.take_along_axis(by_s[0], index, axis=1)
        for k in range(1, NP - 1):
            value = jnp.where(s == k, jnp.take_along_axis(by_s[k], index, axis=1), value)
        tiles.append(value)
    return jnp.concatenate(tiles, axis=1)


def layout_kernel(face_ref, v0_ref, v1_ref, v2_ref, half_ref, w0_ref, w1_ref, local_ref, order_ref, out_ref, scratch_ref):
    even = parity() == 0
    face = face_ref[...]
    local = own_rows(even, local_ref[...])
    first = jnp.where(even, local[0] + face, local[0])
    last = jnp.where(even, local[-1], local[-1] + face)
    w2 = jnp.concatenate([first[None], local[1:-1], last[None]], axis=0)
    fields = [own_rows(even, x[...]) for x in (v0_ref, v1_ref, v2_ref)]
    fields.extend((own_of_half(even, half_ref[...]), w0_ref[...], w1_ref[...], w2))
    for k, x in enumerate(fields):
        out_ref[k] = to_output(x, order_ref, scratch_ref, k)


def combine_kernel(sums_ref, fields_ref, p_ref, r_ref):
    line = jnp.sum(sums_ref[...], axis=0, keepdims=True)
    for step in (4, 2, 1):
        line = line + roll(line, -step, 1)
    shape = (NP, LANES)
    h00, h01, h02, h11, h12, h22, g0, g1, g2 = [jnp.broadcast_to(line[:, NP * k : NP * k + 1], shape) for k in range(9)]
    scale = 1.0 / h00
    m1, m2, m0 = h01 * scale, h02 * scale, g0 * scale
    k11, k12, k22 = h11 - m1 * h01, h12 - m1 * h02, h22 - m2 * h02
    f1, f2 = g1 - m1 * g0, g2 - m2 * g0
    second = 1.0 / k11
    n2 = k12 * second
    c2 = (f2 - n2 * f1) / (k22 - n2 * k12)
    c1 = f1 * second - n2 * c2
    c0 = m0 - m1 * c1 - m2 * c2
    for tile in range(7):
        x = [fields_ref[k, :, LANES * tile : LANES * tile + LANES] for k in range(7)]
        p_ref[:, LANES * tile : LANES * tile + LANES] = (c0 + STEPS[0]) * x[0] + (c1 + STEPS[1]) * x[1] + c2 * x[2]
        r_ref[:, LANES * tile : LANES * tile + LANES] = x[3] - (c0 * x[4] + c1 * x[5] + c2 * x[6])


def call(kernel, shapes, *args, scratch=()):
    return pl.pallas_call(
        kernel,
        out_shape=[jax.ShapeDtypeStruct(shape, jnp.float32) for shape in shapes],
        in_specs=[pl.BlockSpec(memory_space=pltpu.VMEM)] * len(args),
        out_specs=[pl.BlockSpec(memory_space=pltpu.VMEM)] * len(shapes),
        scratch_shapes=scratch,
        compiler_params=PARAMS,
    )(*args)


SMOOTH_SCRATCH = (
    pltpu.VMEM(((2 * NP + 1) * NP, LANES), jnp.float32),
    pltpu.VMEM((2, (NP + 2) * NP, LANES), jnp.float32),
)


def call_forcing(*args):
    shapes = [(7 * NP, NP, LANES), (4, NP, LANES)]
    scratch = [pltpu.SMEM(args[0].shape, jnp.int32)]
    scratch.extend(pltpu.VMEM(x.shape, x.dtype) for x in args[1:])
    scratch.append(pltpu.SemaphoreType.DMA((len(args),)))
    return pl.pallas_call(
        forcing_kernel,
        out_shape=[jax.ShapeDtypeStruct(shape, jnp.float32) for shape in shapes],
        in_specs=[pl.BlockSpec(memory_space=pltpu.HBM)] * len(args),
        out_specs=[pl.BlockSpec(memory_space=pltpu.VMEM)] * len(shapes),
        scratch_shapes=scratch,
        compiler_params=pltpu.CompilerParams(vmem_limit_bytes=FORCING_VMEM),
    )(*args)


FORCING_TABLES = ("w3", "wmass", "ds", "dq", "jright", "jslope", "jright_t", "jleft", "jleft_a", "jleft_s", "jleft_t", "wfine")


def team_groups(count):
    return [[2 * c + side for c in range(count // 2)] for side in range(2)]


def shards(velocity, conv_past, metric, jacobian, element_slot):
    count = lax.axis_size("dom")
    t = {key: jnp.asarray(value) for key, value in TAB.items()}
    field = (NP, NP, LANES)
    chip = (ROWS, NP, LANES)
    half_shape = (2 * NP + 1, NP, LANES)
    edge = (EDGE, NP, LANES)
    pack, cross = call_forcing(
        element_slot, velocity, conv_past, metric, jacobian, *(t[key] for key in FORCING_TABLES)
    )
    cross = swap_cross(cross, count)
    pack = pl.pallas_call(
        stage_kernel,
        out_shape=jax.ShapeDtypeStruct(pack.shape, jnp.float32),
        in_specs=[pl.BlockSpec(memory_space=pltpu.HBM)],
        out_specs=pl.BlockSpec(memory_space=pltpu.VMEM),
        scratch_shapes=[pltpu.SemaphoreType.DMA(())],
        compiler_params=PARAMS,
    )(pack)
    (own,) = call(pair_kernel, [(7 * NP + 4, NP, LANES)], pack, cross)
    mate = swap_inner(own, count)
    div, op, level, cross = call(
        divergence_kernel,
        [chip, (2, 4) + field, (NP, LANES), (EDGE + 1, NP, LANES)],
        own, mate, t["ds"], t["qright_t"],
    )
    solve = (t["sleft"], t["sright"], t["srback"], t["sback"])
    tables = (op, t["ds"], t["qright"], t["qright_t"])
    half, inv, part = call(
        first_smooth_kernel,
        [half_shape, (2 * MODES, ES * (NP + 2)), edge],
        div, swap_cross(cross, count), level, t["spread"], t["lam"], *solve,
        scratch=SMOOTH_SCRATCH,
    )
    vectors, locals_, images = [], [], []
    for step in STEPS:
        v, local, cross = call(
            operator_kernel, [chip, chip, edge], part, swap_inner(part, count), *tables
        )
        image, half, part = call(
            functools.partial(smooth_kernel, step),
            [field, half_shape, edge],
            half, local, swap_cross(cross, count), inv, *solve,
            scratch=SMOOTH_SCRATCH,
        )
        vectors.append(v)
        locals_.append(local)
        images.append(image)
    residual, parts = call(
        early_kernel, [chip, (5, NP, LANES)], t["ws"], div, *vectors, *locals_
    )
    v, sums = call(
        last_sums_kernel,
        [chip, (count // 2, LANES)],
        part, swap_inner(part, count), op, t["ds"], t["qright"], parts, *locals_, residual, t["ws"],
    )
    sums = lax.all_to_all(sums, "dom", 0, 0, tiled=True, axis_index_groups=team_groups(count))
    local, face = call(last_operator_kernel, [chip, (NP, LANES)], v, *tables)
    (fields,) = call(
        layout_kernel,
        [(7, NP, 896)],
        swap_cross(face, count), *vectors, v, half, *images, local, t["order"],
        scratch=[pltpu.VMEM((7, NP * NP, LANES), jnp.float32)],
    )
    return tuple(call(combine_kernel, [(NP, 896), (NP, 896)], sums, fields))


def solution(mesh):
    return jax.shard_map(
        shards,
        mesh=mesh,
        in_specs=(
            P(None, None, "dom", None),
            P(None, None, "dom", None),
            P(None, "dom", None),
            P("dom", None),
            P("dom"),
        ),
        out_specs=(P("dom", None), P("dom", None)),
        check_vma=False,
    )
```

```python
import functools

import jax
import jax.numpy as jnp
import numpy as np
from jax import lax
from jax.experimental import pallas as pl
from jax.experimental.pallas import tpu as pltpu
from jax.sharding import PartitionSpec as P

NP = 8
NF = 12
ES = 16
LANES = 128
time_step = 0.25
viscosity = 0.05
mass_shift = 0.001
STEPS = (0.45, 0.3)
VMEM = 48 * 1024 * 1024
FORCING_VMEM = 56 * 1024 * 1024
ROWS = 2 * NP - 1
EDGE = NP + 1
MODES = 112


def legendre_pair(points, order):
    before = np.ones(points.shape)
    current = points * 1.0
    for level in range(2, order + 1):
        nextone = ((2 * level - 1) * points * current - (level - 1) * before) / level
        before = current
        current = nextone
    return (current, before)


def jacobi_eigen(matrix):
    size = matrix.shape[0]
    work = matrix * 1.0
    vectors = np.eye(size)
    for sweep in range(30):
        for first in range(size - 1):
            for second in range(first + 1, size):
                off = float(work[first, second])
                if abs(off) > 1e-300:
                    tau = (float(work[second, second]) - float(work[first, first])) / (2.0 * off)
                    if tau >= 0.0:
                        tangent = 1.0 / (tau + (1.0 + tau * tau) ** 0.5)
                    else:
                        tangent = -1.0 / (-tau + (1.0 + tau * tau) ** 0.5)
                    cosine = 1.0 / (1.0 + tangent * tangent) ** 0.5
                    sine = tangent * cosine
                    rotation = np.eye(size)
                    rotation[first, first] = cosine
                    rotation[second, second] = cosine
                    rotation[first, second] = sine
                    rotation[second, first] = -sine
                    work = rotation.T @ work @ rotation
                    vectors = vectors @ rotation
    diagonal_index = np.arange(size)
    return (work[diagonal_index, diagonal_index], vectors)


def base_tables(points_edge, points_fine):
    degree = points_edge - 1
    points = -np.cos(np.pi * np.arange(points_edge) / degree)
    for sweep in range(100):
        top, below = legendre_pair(points, degree)
        points = points - (points * top - below) / (points_edge * top)
    top, below = legendre_pair(points, degree)
    weight_gll = 2.0 / (degree * points_edge * top**2)
    spacing = points[:, None] - points[None, :] + np.eye(points_edge)
    barycentric = 1.0 / np.prod(spacing, axis=1)
    derivative = barycentric[None, :] / barycentric[:, None] / spacing
    derivative = derivative * (1.0 - np.eye(points_edge))
    derivative = derivative - np.eye(points_edge) * derivative.sum(axis=1)[:, None]
    fine_points = np.cos(np.pi * (np.arange(points_fine) + 0.75) / (points_fine + 0.5))
    for sweep in range(100):
        top, below = legendre_pair(fine_points, points_fine)
        slope = points_fine * (fine_points * top - below) / (fine_points * fine_points - 1.0)
        fine_points = fine_points - top / slope
    top, below = legendre_pair(fine_points, points_fine)
    slope = points_fine * (fine_points * top - below) / (fine_points * fine_points - 1.0)
    fine_weight = 2.0 / ((1.0 - fine_points * fine_points) * slope * slope)
    fine_points = fine_points[::-1]
    fine_weight = fine_weight[::-1]
    interpolate = np.ones((points_fine, points_edge))
    for column in range(points_edge):
        for other in range(points_edge):
            if other != column:
                interpolate[:, column] = (
                    interpolate[:, column]
                    * (fine_points - points[other])
                    / (points[column] - points[other])
                )
    stiffness = derivative.T @ (weight_gll[:, None] * derivative)
    extent = 3 * degree + 1
    joined_stiff = np.zeros((extent, extent))
    joined_mass = np.zeros(extent)
    for segment in range(3):
        offset = segment * degree
        joined_stiff[offset : offset + points_edge, offset : offset + points_edge] += stiffness
        joined_mass[offset : offset + points_edge] += weight_gll
    low = degree - 1
    high = 2 * degree + 2
    root_mass = np.sqrt(joined_mass[low:high])
    scaled = joined_stiff[low:high, low:high] / root_mass[:, None] / root_mass[None, :]
    scaled = 0.5 * (scaled + scaled.T)
    eigen_values, eigen_vectors = jacobi_eigen(scaled)
    solve_mat = eigen_vectors / root_mass[:, None]
    breadth = high - low
    return dict(
        derivative=derivative,
        interpolate=interpolate,
        weight=weight_gll,
        fine_weight=fine_weight,
        solve=solve_mat,
        eigen=eigen_values,
    )


def f32(value):
    return np.ascontiguousarray(value, dtype=np.float32)


def halves(value):
    value = np.asarray(value, dtype=np.float32)
    high = value.astype(jnp.bfloat16)
    rest = (value - high.astype(np.float32)).astype(jnp.bfloat16)
    return high, rest


def for_left(value):
    high, rest = halves(value)
    return np.concatenate([high, rest, high], axis=1)


def for_right(value):
    high, rest = halves(value)
    return np.concatenate([high, rest, high], axis=0)


def by_modes_right(value):
    high, rest = halves(by_modes(value, 0))
    parts = (high, rest, high)
    return np.concatenate([x[:LANES] for x in parts] + [x[LANES:] for x in parts])


def pair(value):
    return np.stack(halves(value))


def by_modes(value, axis):
    at = np.arange(ES * (NP + 2))
    order = np.concatenate([at[at % (NP + 2) < NP], at[at % (NP + 2) >= NP]])
    return np.take(value, order, axis=axis)


def make_tables():
    base = base_tables(NP, NF)
    deriv, interp, solve, eigen = base["derivative"], base["interpolate"], base["solve"], base["eigen"]
    w, wf = base["weight"], base["fine_weight"]
    out = {}
    index = np.arange(NP)

    def sublane(matrix):
        rows = [matrix[index, (index + shift) % NP] for shift in range(NP)]
        return f32(np.broadcast_to(np.stack(rows)[:, :, None], (NP, NP, LANES)))

    def lane(matrix):
        rows = [np.tile(matrix[index, (index + shift) % NP], ES) for shift in range(NP)]
        return f32(np.broadcast_to(np.stack(rows)[:, None, :], (NP, NP, LANES)))

    out["ds"] = np.stack([sublane(deriv), sublane(deriv.T)])
    out["dq"] = np.stack([lane(deriv), lane(deriv.T)])
    out["qright"] = for_right(np.kron(np.eye(ES), deriv.T))
    out["qright_t"] = for_right(np.kron(np.eye(ES), deriv))
    out["w3"] = f32(np.einsum("a,s,q->asq", w, w, w).reshape(1, 512))
    out["wmass"] = f32(np.tile(np.einsum("a,s,q->asq", w, w, w), (1, 1, ES)))
    both = interp @ deriv
    pad = np.zeros((16 - NF, NP))
    line = np.concatenate([interp, pad])
    slope = np.concatenate([both, pad])
    out["jright"] = for_right(np.kron(np.eye(ES), line.T))
    out["jslope"] = for_right(np.kron(np.eye(ES), slope.T))
    out["jright_t"] = pair(np.kron(np.eye(ES), line))
    out["jleft"] = for_left(np.kron(interp, interp))
    out["jleft_a"] = for_left(np.kron(both, interp))
    out["jleft_s"] = for_left(np.kron(interp, both))
    out["jleft_t"] = for_left(np.kron(interp, interp).T)
    wide_wf = np.concatenate([wf, np.zeros(16 - NF)])
    out["wfine"] = f32(np.kron(np.kron(wf, wf)[:, None], np.tile(wide_wf, ES)[None, :]))
    at = np.arange(7 * LANES)
    element, within = at // 56, at % 56
    order = np.stack([element * NP + within % NP, within // NP]).reshape(2, 7, 1, LANES)
    out["order"] = np.ascontiguousarray(np.broadcast_to(order, (2, 7, NP, LANES)), dtype=np.int32)
    wide = NP + 2
    left = np.zeros((MODES, 112))
    back = np.zeros((144, MODES))
    at = np.arange(wide)
    for i in range(wide):
        for j in range(wide):
            row = i * wide + j
            inside = np.outer(solve[:, i], solve[1:-1, j]).reshape(80)
            left[row, :80] = inside
            left[row, 80 + at] = solve[:, i] * solve[0, j]
            left[row, 96 + at] = solve[:, i] * solve[wide - 1, j]
            back[:80, row] = inside
            for block, s in enumerate((0, 1, wide - 2, wide - 1)):
                back[80 + 16 * block + at, row] = solve[:, i] * solve[s, j]
    out["sleft"] = for_left(left)
    out["sback"] = for_left(back)
    out["sright"] = for_right(by_modes(np.kron(np.eye(ES), solve[1:-1, :]), 1))
    out["srback"] = by_modes_right(np.kron(np.eye(ES), solve[1:-1, :].T))
    out["spread"] = f32(by_modes(np.kron(np.eye(ES), np.ones((NP, wide))), 1) / 8.0)
    lam_a = np.zeros((MODES, 1))
    lam_s = np.zeros((MODES, 1))
    lam_a[:100, 0] = np.repeat(eigen, wide)
    lam_s[:100, 0] = np.tile(eigen, wide)
    lam_q = by_modes(np.tile(eigen, ES)[None, :], 1)
    full = (MODES, ES * wide)
    out["lam"] = f32(np.stack([np.broadcast_to(lam_a, full), np.broadcast_to(lam_s, full), np.broadcast_to(lam_q, full)]))
    half = np.ones(NP)
    half[0] = half[-1] = 0.5
    out["ws"] = f32(np.broadcast_to(half[:, None], (NP, LANES)))
    return out


TAB = make_tables()
DERIV = [[float(x) for x in row] for row in base_tables(NP, NF)["derivative"].astype(np.float32)]
PARAMS = pltpu.CompilerParams(vmem_limit_bytes=VMEM)


def full_dot(left, right):
    return jnp.dot(left, right, precision=lax.Precision.HIGHEST, preferred_element_type=jnp.float32)


def short_dot(left, right):
    return jnp.dot(left, right, preferred_element_type=jnp.float32)


def split(x):
    high = x.astype(jnp.bfloat16)
    return high, (x - high.astype(jnp.float32)).astype(jnp.bfloat16)


def left_dot(table_ref, x):
    high, rest = split(x)
    return short_dot(table_ref[...], jnp.concatenate([high, high, rest], axis=0))


def right_dot(x, table_ref):
    high, rest = split(x)
    return short_dot(jnp.concatenate([high, high, rest], axis=1), table_ref[...])


def modes_dot(x, table_ref):
    high, rest = split(x)
    parts = (high, high, rest)
    whole = [y[:, :LANES] for y in parts] + [y[:, LANES:] for y in parts]
    return short_dot(jnp.concatenate(whole, axis=1), table_ref[...])


def pair_dot(x, table_ref):
    high, rest = split(x)
    return short_dot(high, table_ref[0]) + (short_dot(high, table_ref[1]) + short_dot(rest, table_ref[0]))


def roll(x, shift, axis):
    return pltpu.roll(x, shift % x.shape[axis], axis)


def d_a(x, transposed):
    rows = []
    for a in range(NP):
        total = None
        for b in range(NP):
            term = (DERIV[b][a] if transposed else DERIV[a][b]) * x[b]
            total = term if total is None else total + term
        rows.append(total)
    return jnp.stack(rows)


def d_s(x, coef):
    total = coef[0][None] * x
    for shift in range(1, NP):
        total = total + coef[shift][None] * roll(x, -shift, 1)
    return total


def d_q(x, coef):
    flat = x.reshape(-1, LANES)
    lane = lax.broadcasted_iota(jnp.int32, flat.shape, 1)
    total = coef[0][None] * x
    for shift in range(1, NP):
        index = (lane & (LANES - NP)) | ((lane + shift) & (NP - 1))
        total = total + coef[shift][None] * jnp.take_along_axis(flat, index, axis=1).reshape(x.shape)
    return total


def gradient(x, ds, dq):
    return d_a(x, False), d_s(x, ds[0]), d_q(x, dq[0])


def gradient_t(xa, xs, xq, ds, dq):
    return d_a(xa, True) + d_s(xs, ds[1]) + d_q(xq, dq[1])


def join_s(x):
    s = lax.broadcasted_iota(jnp.int32, x.shape, 1)
    from_before = roll(roll(x, NP, 2), 1, 1)
    from_after = roll(roll(x, -NP, 2), -1, 1)
    zero = jnp.zeros_like(x)
    return x + jnp.where(s == 0, from_before, jnp.where(s == NP - 1, from_after, zero))


def parity():
    return lax.rem(lax.axis_index("dom"), 2)


def swap_inner(x, count):
    return lax.ppermute(x, "dom", [(i, i ^ 1) for i in range(count)])


def swap_cross(x, count):
    pairs = [(i, (i + 1) % count if i % 2 else (i - 1) % count) for i in range(count)]
    return lax.ppermute(x, "dom", pairs)


def to_lanes(x):
    shape = (x.shape[0], NP, LANES)
    lane = lax.broadcasted_iota(jnp.int32, shape, 2)
    pieces = []
    for tile in range(4):
        first = x[:, :8, tile * LANES : (tile + 1) * LANES]
        second = x[:, 8:, tile * LANES : (tile + 1) * LANES]
        pieces.append(jnp.where(lane < 64, first, roll(second, 64, 2)))
        pieces.append(jnp.where(lane < 64, roll(first, 64, 2), second))
    y = jnp.stack(pieces, axis=1).reshape(x.shape[0] * NP, NP, LANES)
    sub = lax.broadcasted_iota(jnp.int32, y.shape, 1)
    lane = lax.broadcasted_iota(jnp.int32, y.shape, 2)
    for bit in range(3):
        step = 1 << bit
        in_sub = (sub & step) != 0
        in_lane = (lane & (step * 8)) != 0
        flat = y.reshape(-1, LANES)
        swapped = jnp.take_along_axis(flat, lane.reshape(-1, LANES) ^ (step * 8), axis=1).reshape(y.shape)
        if step == 4:
            moved = roll(swapped, step, 1)
        else:
            moved = jnp.where(in_sub, roll(swapped, step, 1), roll(swapped, -step, 1))
        y = jnp.where(in_sub == in_lane, y, moved)
    return y.reshape(x.shape[0], NP, NP, LANES)


def rows(x):
    return x.reshape(NP * NP, LANES)


def planes(x):
    return x.reshape(NP, NP, LANES)


def take_lanes(x, index):
    flat = x.reshape(-1, LANES)
    tiled = jnp.broadcast_to(index[None], x.shape).reshape(-1, LANES)
    return jnp.take_along_axis(flat, tiled, axis=1).reshape(x.shape)


def forcing_kernel(slot_in, vel_in, past_in, metric_in, jac_in, w3_in, wmass_in, ds_in, dq_in, jright_in, jslope_in, jright_t_in, jleft_in, jleft_a_in, jleft_s_in, jleft_t_in, wfine_in, pack_ref, cross_ref, slot_ref, vel_ref, past_ref, metric_ref, jac_ref, w3_ref, wmass_ref, ds_ref, dq_ref, jright_ref, jslope_ref, jright_t_ref, jleft_ref, jleft_a_ref, jleft_s_ref, jleft_t_ref, wfine_ref, sems):
    sources = (slot_in, vel_in, past_in, metric_in, jac_in, w3_in, wmass_in, ds_in, dq_in, jright_in, jslope_in, jright_t_in, jleft_in, jleft_a_in, jleft_s_in, jleft_t_in, wfine_in)
    targets = (slot_ref, vel_ref, past_ref, metric_ref, jac_ref, w3_ref, wmass_ref, ds_ref, dq_ref, jright_ref, jslope_ref, jright_t_ref, jleft_ref, jleft_a_ref, jleft_s_ref, jleft_t_ref, wfine_ref)
    copies = [pltpu.make_async_copy(x, y, sems.at[k]) for k, (x, y) in enumerate(zip(sources, targets))]
    for copy in copies:
        copy.start()
    for copy in copies[:6]:
        copy.wait()
    even = parity() == 0
    jac = jac_ref[...]
    new, mid, old = vel_ref[0], vel_ref[1], vel_ref[2]
    guess = 3.0 * (new - mid) + old
    direct = (jac * w3_ref[...])[None] * (-10.0 * new + 16.0 * mid - 6.0 * old) + 3.0 * past_ref[0] - past_ref[1]
    lanes = to_lanes(jnp.concatenate([new, guess, direct, metric_ref[...], jac[None]], axis=0))
    new, guess, direct, metric, jac = lanes[0:3], lanes[3:6], lanes[6:9], lanes[9:12], lanes[12]
    for copy in copies[6:]:
        copy.wait()
    ds, dq = ds_ref[...], dq_ref[...]
    moved = [rows(new[i]) for i in range(3)]
    plain = moved + [rows(jac)] + [rows(new[d] * metric[d]) for d in range(3)]
    wide = right_dot(jnp.concatenate(plain, axis=0), jright_ref)
    slope = right_dot(jnp.concatenate(moved, axis=0), jslope_ref)
    scale = left_dot(jleft_ref, wide[192:256]) * wfine_ref[...]
    carry = [left_dot(jleft_ref, wide[256 + 64 * d : 320 + 64 * d]) for d in range(3)]
    products = []
    for i in range(3):
        part = wide[64 * i : 64 * i + 64]
        total = carry[0] * left_dot(jleft_a_ref, part) + carry[1] * left_dot(jleft_s_ref, part)
        total = total + carry[2] * left_dot(jleft_ref, slope[64 * i : 64 * i + 64])
        products.append(scale * total)
    coarse = left_dot(jleft_t_ref, jnp.concatenate(products, axis=1))
    coarse = pair_dot(jnp.concatenate([coarse[:, 256 * i : 256 * i + 256] for i in range(3)], axis=0), jright_t_ref)
    mass = jac * wmass_ref[...]
    factor = [mass * metric[d] * metric[d] for d in range(3)]
    result = []
    for i in range(3):
        ga, gs, gq = gradient(guess[i], ds, dq)
        stiff = gradient_t(factor[0] * ga, factor[1] * gs, factor[2] * gq, ds, dq)
        result.append(direct[i] - 3.0 * planes(coarse[64 * i : 64 * i + 64]) - viscosity * stiff)
    result.extend([mass, metric[0], metric[1], metric[2]])
    lane = lax.broadcasted_iota(jnp.int32, (NP, LANES), 1)
    index = jnp.zeros((NP, LANES), jnp.int32)
    for e in range(ES):
        index = jnp.where((lane >> 3) == slot_ref[e], e * NP, index)
    index = index + (lane & 7)
    result = [take_lanes(x, index) for x in result]
    for k in range(4):
        joined = join_s(result[k])
        cross_ref[k] = jnp.where(even, joined[0], joined[NP - 1])
        pack_ref[NP * k : NP * k + NP] = joined if k < 3 else result[k]
    for k in range(4, 7):
        pack_ref[NP * k : NP * k + NP] = result[k]


def stage_kernel(pack_ref, out_ref, sem):
    copy = pltpu.make_async_copy(pack_ref, out_ref, sem)
    copy.start()
    copy.wait()


def pair_kernel(pack_ref, cross_in, out_ref):
    out_ref[: 7 * NP] = pack_ref[...]
    out_ref[7 * NP :] = cross_in[...]


def chip_rows(first, second):
    return jnp.concatenate([first[:-1], (first[-1] + second[0])[None], second[1:]], axis=0)


def own_rows(even, x):
    return jnp.where(even, x[:NP], x[NP - 1 :])


def edge_rows(even, x):
    return jnp.where(even, x[:EDGE], x[ROWS - EDGE :])


def divergence_kernel(own_ref, mate_ref, ds_ref, qright_t_ref, div_ref, op_ref, level_ref, cross_ref):
    even = parity() == 0
    own, mate = own_ref[...], mate_ref[...]
    packs = [jnp.where(even, own, mate), jnp.where(even, mate, own)]
    parts = [[pack[NP * k : NP * k + NP] for k in range(7)] for pack in packs]
    low, high = packs[0][7 * NP :], packs[1][7 * NP :]
    sides = []
    for k in range(4):
        first, second = parts[0][k], parts[1][k]
        if k == 3:
            first, second = join_s(first), join_s(second)
        whole = chip_rows(first, second)
        sides.append(jnp.concatenate([(whole[0] + low[k])[None], whole[1:-1], (whole[-1] + high[k])[None]], axis=0))
    inv = 1.0 / sides[3]
    accel = [sides[d] * inv for d in range(3)]
    div, last, levels = [], [], []
    for layer in range(2):
        mass = parts[layer][3]
        at = (NP - 1) * layer
        sums = []
        terms = []
        for d in range(3):
            one = mass * parts[layer][4 + d]
            two = one * parts[layer][4 + d]
            op_ref[layer, d] = two
            sums.append(jnp.sum(rows(two), axis=0, keepdims=True))
            terms.append(one * accel[d][at : at + NP])
        op_ref[layer, 3] = mass_shift * mass
        sums.append(jnp.sum(rows(mass), axis=0, keepdims=True))
        sums.append(jnp.zeros((4, LANES), jnp.float32))
        levels.append(jnp.concatenate(sums, axis=0))
        div.append(d_a(terms[0], True) + d_s(terms[1], ds_ref[1]))
        last.append(rows(terms[2]))
    last = right_dot(jnp.concatenate(last, axis=0), qright_t_ref)
    div = [join_s(x + planes(last[64 * k : 64 * k + 64])) for k, x in enumerate(div)]
    whole = chip_rows(div[0], div[1])
    div_ref[...] = whole
    cross_ref[:EDGE] = edge_rows(even, whole)
    level = jnp.where(even, levels[0], levels[1])
    level_ref[...] = level
    cross_ref[EDGE] = level


def half_window(even, local, received):
    edge = received[:EDGE]
    low = jnp.concatenate([edge[:-1], (edge[-1] + local[0])[None], local[1:EDGE]], axis=0)
    high = jnp.concatenate([local[ROWS - EDGE : -1], (local[-1] + edge[0])[None], edge[1:]], axis=0)
    return jnp.where(even, low, high)


def own_of_half(even, x):
    return jnp.where(even, x[NP : 2 * NP], x[1 : NP + 1])


def inverse_levels(levels, spread_ref, lam_ref):
    result = []
    for level in levels:
        level = full_dot(level, spread_ref[...])
        denom = level[0:1] * lam_ref[0] + level[1:2] * lam_ref[1] + level[2:3] * lam_ref[2] + mass_shift * level[3:4]
        result.append(1.0 / denom)
    return result


def schwarz(half, even, inv_ref, sleft_ref, sright_ref, srback_ref, sback_ref, scratch_ref, sum_ref):
    wide = NP + 2
    scratch_ref[...] = half.reshape((2 * NP + 1) * NP, LANES)
    none = jnp.zeros((16 - wide, LANES), jnp.float32)
    columns = []
    for layer in range(2):
        at = (NP - 1) * NP * layer
        before = roll(scratch_ref[pl.ds(at + NP - 2, wide, stride=NP), :], NP, 1)
        after = roll(scratch_ref[pl.ds(at + 1, wide, stride=NP), :], -NP, 1)
        own = half[(NP - 1) * layer : (NP - 1) * layer + wide].reshape(wide * NP, LANES)
        columns.append(jnp.concatenate([own, before, none, after, none], axis=0))
    spectra = [left_dot(sleft_ref, x) for x in columns]
    spectra = [right_dot(x, sright_ref) for x in spectra]
    spectra = [x * inv_ref[MODES * k : MODES * k + MODES] for k, x in enumerate(spectra)]
    spectra = [modes_dot(x, srback_ref) for x in spectra]
    blocks = [left_dot(sback_ref, x) for x in spectra]
    z = []
    for layer in range(2):
        part = blocks[layer]
        sum_ref[layer] = part[:80]
        for block, (s, shift) in enumerate(((NP - 2, -NP), (NP - 1, -NP), (0, NP), (1, NP))):
            rows_at = pl.ds(s, wide, stride=NP)
            start = 80 + 16 * block
            sum_ref[layer, rows_at, :] = sum_ref[layer, rows_at, :] + roll(part[start : start + wide], shift, 1)
        z.append(sum_ref[layer].reshape(wide, NP, LANES))
    upper = jnp.concatenate([z[0][8:] + z[1][1:3], z[1][3:]], axis=0)
    lower = jnp.concatenate([z[0][:7], z[0][7:9] + z[1][:2]], axis=0)
    return jnp.where(even, upper, lower)


def join_sides(even, own, mate):
    first, second = jnp.where(even, own, mate), jnp.where(even, mate, own)
    return jnp.concatenate([first[:6], first[6:] + second[:3], second[3:]], axis=0)


def operate(v, op_ref, ds_ref, qright_ref, qright_t_ref):
    ds = ds_ref[...]
    layers = [v[(NP - 1) * k : (NP - 1) * k + NP] for k in range(2)]
    gq = right_dot(jnp.concatenate([rows(x) for x in layers], axis=0), qright_ref)
    hq = [op_ref[k, 2] * planes(gq[64 * k : 64 * k + 64]) for k in range(2)]
    back = right_dot(jnp.concatenate([rows(x) for x in hq], axis=0), qright_t_ref)
    parts = []
    for k, x in enumerate(layers):
        local = d_a(op_ref[k, 0] * d_a(x, False), True) + d_s(op_ref[k, 1] * d_s(x, ds[0]), ds[1])
        parts.append(join_s(local + (op_ref[k, 3] * x + planes(back[64 * k : 64 * k + 64]))))
    return chip_rows(parts[0], parts[1])


def first_smooth_kernel(div_ref, received_ref, level_ref, spread_ref, lam_ref, sleft_ref, sright_ref, srback_ref, sback_ref, half_ref, inv_ref, part_ref, scratch_ref, sum_ref):
    even = parity() == 0
    half = half_window(even, div_ref[...], received_ref)
    half_ref[...] = half
    other = received_ref[EDGE]
    own = level_ref[...]
    levels = [jnp.where(even, other, own), jnp.where(even, own, other)]
    for k, inv in enumerate(inverse_levels(levels, spread_ref, lam_ref)):
        inv_ref[MODES * k : MODES * k + MODES] = inv
    part_ref[...] = schwarz(half, even, inv_ref, sleft_ref, sright_ref, srback_ref, sback_ref, scratch_ref, sum_ref)


def smooth_kernel(step, before_ref, local_ref, received_ref, inv_ref, sleft_ref, sright_ref, srback_ref, sback_ref, own_image_ref, half_ref, part_ref, scratch_ref, sum_ref):
    even = parity() == 0
    image = half_window(even, local_ref[...], received_ref)
    half = before_ref[...] - step * image
    half_ref[...] = half
    part_ref[...] = schwarz(half, even, inv_ref, sleft_ref, sright_ref, srback_ref, sback_ref, scratch_ref, sum_ref)
    own_image_ref[...] = own_of_half(even, image)


def operator_kernel(part_ref, mate_ref, op_ref, ds_ref, qright_ref, qright_t_ref, v_ref, local_ref, cross_ref):
    even = parity() == 0
    v = join_sides(even, part_ref[...], mate_ref[...])
    v_ref[...] = v
    local = operate(v, op_ref, ds_ref, qright_ref, qright_t_ref)
    local_ref[...] = local
    cross_ref[...] = edge_rows(even, local)


def fold(parts):
    lane = lax.broadcasted_iota(jnp.int32, (NP, LANES), 1)
    parts = parts + [jnp.zeros((NP, LANES), jnp.float32)] * (ES - len(parts))
    for step in (8, 16, 32, 64):
        chosen = (lane & step) != 0
        parts = [
            jnp.where(chosen, b, a) + roll(jnp.where(chosen, a, b), step, 1)
            for a, b in zip(parts[::2], parts[1::2])
        ]
    return parts[0]


def early_kernel(ws_ref, div_ref, v0_ref, v1_ref, l0_ref, l1_ref, residual_ref, parts_ref):
    ws = ws_ref[...]
    l0, l1 = l0_ref[...], l1_ref[...]
    residual = div_ref[...] - STEPS[0] * l0 - STEPS[1] * l1
    residual_ref[...] = residual
    v0, v1 = v0_ref[...], v1_ref[...]
    for k, (left, right) in enumerate(((v0, l0), (v0, l1), (v1, l1), (v0, residual), (v1, residual))):
        parts_ref[k] = jnp.sum(left * right, axis=0) * ws


def last_sums_kernel(part_ref, mate_ref, op_ref, ds_ref, qright_ref, parts_ref, l0_ref, l1_ref, residual_ref, ws_ref, v_ref, sums_ref):
    even = parity() == 0
    v = join_sides(even, part_ref[...], mate_ref[...])
    v_ref[...] = v
    layers = [v[(NP - 1) * k : (NP - 1) * k + NP] for k in range(2)]
    gq = right_dot(jnp.concatenate([rows(x) for x in layers], axis=0), qright_ref)
    energy = None
    for k, x in enumerate(layers):
        ga, gs, gq_k = d_a(x, False), d_s(x, ds_ref[0]), planes(gq[64 * k : 64 * k + 64])
        part = op_ref[k, 0] * ga * ga + op_ref[k, 1] * gs * gs + op_ref[k, 2] * gq_k * gq_k + op_ref[k, 3] * x * x
        part = jnp.sum(part, axis=0)
        energy = part if energy is None else energy + part
    ws = ws_ref[...]
    new = [jnp.sum(x[...] * v, axis=0) * ws for x in (l0_ref, l1_ref, residual_ref)]
    p = [parts_ref[k] for k in range(5)]
    folded = fold([p[0], p[1], new[0], p[2], new[1], energy, p[3], p[4], new[2]])
    line = jnp.broadcast_to(jnp.sum(folded, axis=0, keepdims=True), (NP, LANES))
    for k in range(sums_ref.shape[0] // NP):
        sums_ref[NP * k : NP * k + NP] = line


def last_operator_kernel(v_ref, op_ref, ds_ref, qright_ref, qright_t_ref, local_ref, face_ref):
    even = parity() == 0
    local = operate(v_ref[...], op_ref, ds_ref, qright_ref, qright_t_ref)
    local_ref[...] = local
    face_ref[...] = jnp.where(even, local[0], local[-1])


def to_output(x, order_ref, scratch_ref, slot):
    scratch_ref[slot] = rows(x)
    by_s = [scratch_ref[slot, pl.ds(s, NP, stride=NP), :] for s in range(NP - 1)]
    tiles = []
    for tile in range(7):
        index, s = order_ref[0, tile], order_ref[1, tile]
        value = jnp.take_along_axis(by_s[0], index, axis=1)
        for k in range(1, NP - 1):
            value = jnp.where(s == k, jnp.take_along_axis(by_s[k], index, axis=1), value)
        tiles.append(value)
    return jnp.concatenate(tiles, axis=1)


def layout_kernel(face_ref, v0_ref, v1_ref, v2_ref, half_ref, w0_ref, w1_ref, local_ref, order_ref, out_ref, scratch_ref):
    even = parity() == 0
    face = face_ref[...]
    local = own_rows(even, local_ref[...])
    first = jnp.where(even, local[0] + face, local[0])
    last = jnp.where(even, local[-1], local[-1] + face)
    w2 = jnp.concatenate([first[None], local[1:-1], last[None]], axis=0)
    fields = [own_rows(even, x[...]) for x in (v0_ref, v1_ref, v2_ref)]
    fields.extend((own_of_half(even, half_ref[...]), w0_ref[...], w1_ref[...], w2))
    for k, x in enumerate(fields):
        out_ref[k] = to_output(x, order_ref, scratch_ref, k)


def combine_kernel(sums_ref, fields_ref, p_ref, r_ref):
    line = jnp.sum(sums_ref[...], axis=0, keepdims=True)
    for step in (4, 2, 1):
        line = line + roll(line, -step, 1)
    shape = (NP, LANES)
    h00, h01, h02, h11, h12, h22, g0, g1, g2 = [jnp.broadcast_to(line[:, NP * k : NP * k + 1], shape) for k in range(9)]
    scale = 1.0 / h00
    m1, m2, m0 = h01 * scale, h02 * scale, g0 * scale
    k11, k12, k22 = h11 - m1 * h01, h12 - m1 * h02, h22 - m2 * h02
    f1, f2 = g1 - m1 * g0, g2 - m2 * g0
    second = 1.0 / k11
    n2 = k12 * second
    c2 = (f2 - n2 * f1) / (k22 - n2 * k12)
    c1 = f1 * second - n2 * c2
    c0 = m0 - m1 * c1 - m2 * c2
    for tile in range(7):
        x = [fields_ref[k, :, LANES * tile : LANES * tile + LANES] for k in range(7)]
        p_ref[:, LANES * tile : LANES * tile + LANES] = (c0 + STEPS[0]) * x[0] + (c1 + STEPS[1]) * x[1] + c2 * x[2]
        r_ref[:, LANES * tile : LANES * tile + LANES] = x[3] - (c0 * x[4] + c1 * x[5] + c2 * x[6])


def call(kernel, shapes, *args, scratch=()):
    return pl.pallas_call(
        kernel,
        out_shape=[jax.ShapeDtypeStruct(shape, jnp.float32) for shape in shapes],
        in_specs=[pl.BlockSpec(memory_space=pltpu.VMEM)] * len(args),
        out_specs=[pl.BlockSpec(memory_space=pltpu.VMEM)] * len(shapes),
        scratch_shapes=scratch,
        compiler_params=PARAMS,
    )(*args)


SMOOTH_SCRATCH = (
    pltpu.VMEM(((2 * NP + 1) * NP, LANES), jnp.float32),
    pltpu.VMEM((2, (NP + 2) * NP, LANES), jnp.float32),
)


def call_forcing(*args):
    shapes = [(7 * NP, NP, LANES), (4, NP, LANES)]
    scratch = [pltpu.SMEM(args[0].shape, jnp.int32)]
    scratch.extend(pltpu.VMEM(x.shape, x.dtype) for x in args[1:])
    scratch.append(pltpu.SemaphoreType.DMA((len(args),)))
    return pl.pallas_call(
        forcing_kernel,
        out_shape=[jax.ShapeDtypeStruct(shape, jnp.float32) for shape in shapes],
        in_specs=[pl.BlockSpec(memory_space=pltpu.HBM)] * len(args),
        out_specs=[pl.BlockSpec(memory_space=pltpu.VMEM)] * len(shapes),
        scratch_shapes=scratch,
        compiler_params=pltpu.CompilerParams(vmem_limit_bytes=FORCING_VMEM),
    )(*args)


FORCING_TABLES = ("w3", "wmass", "ds", "dq", "jright", "jslope", "jright_t", "jleft", "jleft_a", "jleft_s", "jleft_t", "wfine")


def team_groups(count):
    return [[2 * c + side for c in range(count // 2)] for side in range(2)]


def shards(velocity, conv_past, metric, jacobian, element_slot):
    count = lax.axis_size("dom")
    t = {key: jnp.asarray(value) for key, value in TAB.items()}
    field = (NP, NP, LANES)
    chip = (ROWS, NP, LANES)
    half_shape = (2 * NP + 1, NP, LANES)
    edge = (EDGE, NP, LANES)
    pack, cross = call_forcing(
        element_slot, velocity, conv_past, metric, jacobian, *(t[key] for key in FORCING_TABLES)
    )
    cross = swap_cross(cross, count)
    pack = pl.pallas_call(
        stage_kernel,
        out_shape=jax.ShapeDtypeStruct(pack.shape, jnp.float32),
        in_specs=[pl.BlockSpec(memory_space=pltpu.HBM)],
        out_specs=pl.BlockSpec(memory_space=pltpu.VMEM),
        scratch_shapes=[pltpu.SemaphoreType.DMA(())],
        compiler_params=PARAMS,
    )(pack)
    (own,) = call(pair_kernel, [(7 * NP + 4, NP, LANES)], pack, cross)
    mate = swap_inner(own, count)
    div, op, level, cross = call(
        divergence_kernel,
        [chip, (2, 4) + field, (NP, LANES), (EDGE + 1, NP, LANES)],
        own, mate, t["ds"], t["qright_t"],
    )
    solve = (t["sleft"], t["sright"], t["srback"], t["sback"])
    tables = (op, t["ds"], t["qright"], t["qright_t"])
    half, inv, part = call(
        first_smooth_kernel,
        [half_shape, (2 * MODES, ES * (NP + 2)), edge],
        div, swap_cross(cross, count), level, t["spread"], t["lam"], *solve,
        scratch=SMOOTH_SCRATCH,
    )
    vectors, locals_, images = [], [], []
    for step in STEPS:
        v, local, cross = call(
            operator_kernel, [chip, chip, edge], part, swap_inner(part, count), *tables
        )
        image, half, part = call(
            functools.partial(smooth_kernel, step),
            [field, half_shape, edge],
            half, local, swap_cross(cross, count), inv, *solve,
            scratch=SMOOTH_SCRATCH,
        )
        vectors.append(v)
        locals_.append(local)
        images.append(image)
    residual, parts = call(
        early_kernel, [chip, (5, NP, LANES)], t["ws"], div, *vectors, *locals_
    )
    v, sums = call(
        last_sums_kernel,
        [chip, (count // 2, LANES)],
        part, swap_inner(part, count), op, t["ds"], t["qright"], parts, *locals_, residual, t["ws"],
    )
    sums = lax.all_to_all(sums, "dom", 0, 0, tiled=True, axis_index_groups=team_groups(count))
    local, face = call(last_operator_kernel, [chip, (NP, LANES)], v, *tables)
    (fields,) = call(
        layout_kernel,
        [(7, NP, 896)],
        swap_cross(face, count), *vectors, v, half, *images, local, t["order"],
        scratch=[pltpu.VMEM((7, NP * NP, LANES), jnp.float32)],
    )
    return tuple(call(combine_kernel, [(NP, 896), (NP, 896)], sums, fields))


def solution(mesh):
    return jax.shard_map(
        shards,
        mesh=mesh,
        in_specs=(
            P(None, None, "dom", None),
            P(None, None, "dom", None),
            P(None, "dom", None),
            P("dom", None),
            P("dom"),
        ),
        out_specs=(P("dom", None), P("dom", None)),
        check_vma=False,
    )
```

```python
import functools

import jax
import jax.numpy as jnp
import numpy as np
from jax import lax
from jax.experimental import pallas as pl
from jax.experimental.pallas import tpu as pltpu
from jax.sharding import PartitionSpec as P

NP = 8
NF = 12
ES = 16
LANES = 128
time_step = 0.25
viscosity = 0.05
mass_shift = 0.001
STEPS = (0.45, 0.3)
VMEM = 48 * 1024 * 1024
FORCING_VMEM = 56 * 1024 * 1024
ROWS = 2 * NP - 1
EDGE = NP + 1
MODES = 112


def legendre_pair(points, order):
    before = np.ones(points.shape)
    current = points * 1.0
    for level in range(2, order + 1):
        nextone = ((2 * level - 1) * points * current - (level - 1) * before) / level
        before = current
        current = nextone
    return (current, before)


def jacobi_eigen(matrix):
    size = matrix.shape[0]
    work = matrix * 1.0
    vectors = np.eye(size)
    for sweep in range(30):
        for first in range(size - 1):
            for second in range(first + 1, size):
                off = float(work[first, second])
                if abs(off) > 1e-300:
                    tau = (float(work[second, second]) - float(work[first, first])) / (2.0 * off)
                    if tau >= 0.0:
                        tangent = 1.0 / (tau + (1.0 + tau * tau) ** 0.5)
                    else:
                        tangent = -1.0 / (-tau + (1.0 + tau * tau) ** 0.5)
                    cosine = 1.0 / (1.0 + tangent * tangent) ** 0.5
                    sine = tangent * cosine
                    rotation = np.eye(size)
                    rotation[first, first] = cosine
                    rotation[second, second] = cosine
                    rotation[first, second] = sine
                    rotation[second, first] = -sine
                    work = rotation.T @ work @ rotation
                    vectors = vectors @ rotation
    diagonal_index = np.arange(size)
    return (work[diagonal_index, diagonal_index], vectors)


def base_tables(points_edge, points_fine):
    degree = points_edge - 1
    points = -np.cos(np.pi * np.arange(points_edge) / degree)
    for sweep in range(100):
        top, below = legendre_pair(points, degree)
        points = points - (points * top - below) / (points_edge * top)
    top, below = legendre_pair(points, degree)
    weight_gll = 2.0 / (degree * points_edge * top**2)
    spacing = points[:, None] - points[None, :] + np.eye(points_edge)
    barycentric = 1.0 / np.prod(spacing, axis=1)
    derivative = barycentric[None, :] / barycentric[:, None] / spacing
    derivative = derivative * (1.0 - np.eye(points_edge))
    derivative = derivative - np.eye(points_edge) * derivative.sum(axis=1)[:, None]
    fine_points = np.cos(np.pi * (np.arange(points_fine) + 0.75) / (points_fine + 0.5))
    for sweep in range(100):
        top, below = legendre_pair(fine_points, points_fine)
        slope = points_fine * (fine_points * top - below) / (fine_points * fine_points - 1.0)
        fine_points = fine_points - top / slope
    top, below = legendre_pair(fine_points, points_fine)
    slope = points_fine * (fine_points * top - below) / (fine_points * fine_points - 1.0)
    fine_weight = 2.0 / ((1.0 - fine_points * fine_points) * slope * slope)
    fine_points = fine_points[::-1]
    fine_weight = fine_weight[::-1]
    interpolate = np.ones((points_fine, points_edge))
    for column in range(points_edge):
        for other in range(points_edge):
            if other != column:
                interpolate[:, column] = (
                    interpolate[:, column]
                    * (fine_points - points[other])
                    / (points[column] - points[other])
                )
    stiffness = derivative.T @ (weight_gll[:, None] * derivative)
    extent = 3 * degree + 1
    joined_stiff = np.zeros((extent, extent))
    joined_mass = np.zeros(extent)
    for segment in range(3):
        offset = segment * degree
        joined_stiff[offset : offset + points_edge, offset : offset + points_edge] += stiffness
        joined_mass[offset : offset + points_edge] += weight_gll
    low = degree - 1
    high = 2 * degree + 2
    root_mass = np.sqrt(joined_mass[low:high])
    scaled = joined_stiff[low:high, low:high] / root_mass[:, None] / root_mass[None, :]
    scaled = 0.5 * (scaled + scaled.T)
    eigen_values, eigen_vectors = jacobi_eigen(scaled)
    solve_mat = eigen_vectors / root_mass[:, None]
    breadth = high - low
    return dict(
        derivative=derivative,
        interpolate=interpolate,
        weight=weight_gll,
        fine_weight=fine_weight,
        solve=solve_mat,
        eigen=eigen_values,
    )


def f32(value):
    return np.ascontiguousarray(value, dtype=np.float32)


def halves(value):
    value = np.asarray(value, dtype=np.float32)
    high = value.astype(jnp.bfloat16)
    rest = (value - high.astype(np.float32)).astype(jnp.bfloat16)
    return high, rest


def for_left(value):
    high, rest = halves(value)
    return np.concatenate([high, rest, high], axis=1)


def for_right(value):
    high, rest = halves(value)
    return np.concatenate([high, rest, high], axis=0)


def by_modes_right(value):
    a, b, c = thirds(by_modes(value, 0))
    parts = (c, b, a, b, a, a)
    return np.concatenate([x[:LANES] for x in parts] + [x[LANES:] for x in parts])


def thirds(value):
    value = np.asarray(value, dtype=np.float32)
    pieces = []
    for k in range(3):
        pieces.append(value.astype(jnp.bfloat16))
        value = value - pieces[-1].astype(np.float32)
    return pieces


def for_right_full(value):
    a, b, c = thirds(value)
    return np.concatenate([c, b, a, b, a, a], axis=0)


def for_left_full(value):
    a, b, c = thirds(value)
    return np.concatenate([c, b, a, b, a, a], axis=1)


def pair(value):
    return np.stack(halves(value))


def by_modes(value, axis):
    at = np.arange(ES * (NP + 2))
    order = np.concatenate([at[at % (NP + 2) < NP], at[at % (NP + 2) >= NP]])
    return np.take(value, order, axis=axis)


def make_tables():
    base = base_tables(NP, NF)
    deriv, interp, solve, eigen = base["derivative"], base["interpolate"], base["solve"], base["eigen"]
    w, wf = base["weight"], base["fine_weight"]
    out = {}
    index = np.arange(NP)

    def sublane(matrix):
        rows = [matrix[index, (index + shift) % NP] for shift in range(NP)]
        return f32(np.broadcast_to(np.stack(rows)[:, :, None], (NP, NP, LANES)))

    def lane(matrix):
        rows = [np.tile(matrix[index, (index + shift) % NP], ES) for shift in range(NP)]
        return f32(np.broadcast_to(np.stack(rows)[:, None, :], (NP, NP, LANES)))

    out["ds"] = np.stack([sublane(deriv), sublane(deriv.T)])
    out["dq"] = np.stack([lane(deriv), lane(deriv.T)])
    out["qright"] = for_right_full(np.kron(np.eye(ES), deriv.T))
    out["qright_t"] = for_right_full(np.kron(np.eye(ES), deriv))
    out["w3"] = f32(np.einsum("a,s,q->asq", w, w, w).reshape(1, 512))
    out["wmass"] = f32(np.tile(np.einsum("a,s,q->asq", w, w, w), (1, 1, ES)))
    both = interp @ deriv
    pad = np.zeros((16 - NF, NP))
    line = np.concatenate([interp, pad])
    slope = np.concatenate([both, pad])
    out["jright"] = for_right_full(np.kron(np.eye(ES), line.T))
    out["jslope"] = for_right_full(np.kron(np.eye(ES), slope.T))
    out["jright_t"] = for_right_full(np.kron(np.eye(ES), line))
    out["jleft"] = for_left_full(np.kron(interp, interp))
    out["jleft_a"] = for_left_full(np.kron(both, interp))
    out["jleft_s"] = for_left_full(np.kron(interp, both))
    out["jleft_t"] = for_left_full(np.kron(interp, interp).T)
    wide_wf = np.concatenate([wf, np.zeros(16 - NF)])
    out["wfine"] = f32(np.kron(np.kron(wf, wf)[:, None], np.tile(wide_wf, ES)[None, :]))
    at = np.arange(7 * LANES)
    element, within = at // 56, at % 56
    order = np.stack([element * NP + within % NP, within // NP]).reshape(2, 7, 1, LANES)
    out["order"] = np.ascontiguousarray(np.broadcast_to(order, (2, 7, NP, LANES)), dtype=np.int32)
    wide = NP + 2
    left = np.zeros((MODES, 112))
    back = np.zeros((144, MODES))
    at = np.arange(wide)
    for i in range(wide):
        for j in range(wide):
            row = i * wide + j
            inside = np.outer(solve[:, i], solve[1:-1, j]).reshape(80)
            left[row, :80] = inside
            left[row, 80 + at] = solve[:, i] * solve[0, j]
            left[row, 96 + at] = solve[:, i] * solve[wide - 1, j]
            back[:80, row] = inside
            for block, s in enumerate((0, 1, wide - 2, wide - 1)):
                back[80 + 16 * block + at, row] = solve[:, i] * solve[s, j]
    out["sleft"] = for_left_full(left)
    out["sback"] = for_left_full(back)
    out["sright"] = for_right_full(by_modes(np.kron(np.eye(ES), solve[1:-1, :]), 1))
    out["srback"] = by_modes_right(np.kron(np.eye(ES), solve[1:-1, :].T))
    out["spread"] = f32(by_modes(np.kron(np.eye(ES), np.ones((NP, wide))), 1) / 8.0)
    lam_a = np.zeros((MODES, 1))
    lam_s = np.zeros((MODES, 1))
    lam_a[:100, 0] = np.repeat(eigen, wide)
    lam_s[:100, 0] = np.tile(eigen, wide)
    lam_q = by_modes(np.tile(eigen, ES)[None, :], 1)
    full = (MODES, ES * wide)
    out["lam"] = f32(np.stack([np.broadcast_to(lam_a, full), np.broadcast_to(lam_s, full), np.broadcast_to(lam_q, full)]))
    half = np.ones(NP)
    half[0] = half[-1] = 0.5
    out["ws"] = f32(np.broadcast_to(half[:, None], (NP, LANES)))
    return out


TAB = make_tables()
DERIV = [[float(x) for x in row] for row in base_tables(NP, NF)["derivative"].astype(np.float32)]
PARAMS = pltpu.CompilerParams(vmem_limit_bytes=VMEM)


def full_dot(left, right):
    return jnp.dot(left, right, precision=lax.Precision.HIGHEST, preferred_element_type=jnp.float32)


def short_dot(left, right):
    return jnp.dot(left, right, preferred_element_type=jnp.float32)


def split_once(x):
    high = x.astype(jnp.bfloat16)
    return high, x - high.astype(jnp.float32)


def split(x):
    high = x.astype(jnp.bfloat16)
    return high, (x - high.astype(jnp.float32)).astype(jnp.bfloat16)


def left_dot(table_ref, x):
    high, rest = split(x)
    return short_dot(table_ref[...], jnp.concatenate([high, high, rest], axis=0))


def right_dot(x, table_ref):
    high, rest = split(x)
    return short_dot(jnp.concatenate([high, high, rest], axis=1), table_ref[...])


def full_pieces(x):
    a, rest = split_once(x)
    b, rest = split_once(rest)
    c = rest.astype(jnp.bfloat16)
    return [a, b, c, a, b, a]


def full_right_dot(x, table_ref):
    return short_dot(jnp.concatenate(full_pieces(x), axis=1), table_ref[...])


def full_left_dot(table_ref, x):
    return short_dot(table_ref[...], jnp.concatenate(full_pieces(x), axis=0))


def modes_dot(x, table_ref):
    parts = full_pieces(x)
    whole = [y[:, :LANES] for y in parts] + [y[:, LANES:] for y in parts]
    return short_dot(jnp.concatenate(whole, axis=1), table_ref[...])


def pair_dot(x, table_ref):
    high, rest = split(x)
    return short_dot(high, table_ref[0]) + (short_dot(high, table_ref[1]) + short_dot(rest, table_ref[0]))


def roll(x, shift, axis):
    return pltpu.roll(x, shift % x.shape[axis], axis)


def d_a(x, transposed):
    rows = []
    for a in range(NP):
        total = None
        for b in range(NP):
            term = (DERIV[b][a] if transposed else DERIV[a][b]) * x[b]
            total = term if total is None else total + term
        rows.append(total)
    return jnp.stack(rows)


def d_s(x, coef):
    total = coef[0][None] * x
    for shift in range(1, NP):
        total = total + coef[shift][None] * roll(x, -shift, 1)
    return total


def d_q(x, coef):
    flat = x.reshape(-1, LANES)
    lane = lax.broadcasted_iota(jnp.int32, flat.shape, 1)
    total = coef[0][None] * x
    for shift in range(1, NP):
        index = (lane & (LANES - NP)) | ((lane + shift) & (NP - 1))
        total = total + coef[shift][None] * jnp.take_along_axis(flat, index, axis=1).reshape(x.shape)
    return total


def gradient(x, ds, dq):
    return d_a(x, False), d_s(x, ds[0]), d_q(x, dq[0])


def gradient_t(xa, xs, xq, ds, dq):
    return d_a(xa, True) + d_s(xs, ds[1]) + d_q(xq, dq[1])


def join_s(x):
    s = lax.broadcasted_iota(jnp.int32, x.shape, 1)
    from_before = roll(roll(x, NP, 2), 1, 1)
    from_after = roll(roll(x, -NP, 2), -1, 1)
    zero = jnp.zeros_like(x)
    return x + jnp.where(s == 0, from_before, jnp.where(s == NP - 1, from_after, zero))


def parity():
    return lax.rem(lax.axis_index("dom"), 2)


def swap_inner(x, count):
    return lax.ppermute(x, "dom", [(i, i ^ 1) for i in range(count)])


def swap_cross(x, count):
    pairs = [(i, (i + 1) % count if i % 2 else (i - 1) % count) for i in range(count)]
    return lax.ppermute(x, "dom", pairs)


def to_lanes(x):
    shape = (x.shape[0], NP, LANES)
    lane = lax.broadcasted_iota(jnp.int32, shape, 2)
    pieces = []
    for tile in range(4):
        first = x[:, :8, tile * LANES : (tile + 1) * LANES]
        second = x[:, 8:, tile * LANES : (tile + 1) * LANES]
        pieces.append(jnp.where(lane < 64, first, roll(second, 64, 2)))
        pieces.append(jnp.where(lane < 64, roll(first, 64, 2), second))
    y = jnp.stack(pieces, axis=1).reshape(x.shape[0] * NP, NP, LANES)
    sub = lax.broadcasted_iota(jnp.int32, y.shape, 1)
    lane = lax.broadcasted_iota(jnp.int32, y.shape, 2)
    for bit in range(3):
        step = 1 << bit
        in_sub = (sub & step) != 0
        in_lane = (lane & (step * 8)) != 0
        flat = y.reshape(-1, LANES)
        swapped = jnp.take_along_axis(flat, lane.reshape(-1, LANES) ^ (step * 8), axis=1).reshape(y.shape)
        if step == 4:
            moved = roll(swapped, step, 1)
        else:
            moved = jnp.where(in_sub, roll(swapped, step, 1), roll(swapped, -step, 1))
        y = jnp.where(in_sub == in_lane, y, moved)
    return y.reshape(x.shape[0], NP, NP, LANES)


def rows(x):
    return x.reshape(NP * NP, LANES)


def planes(x):
    return x.reshape(NP, NP, LANES)


def take_lanes(x, index):
    flat = x.reshape(-1, LANES)
    tiled = jnp.broadcast_to(index[None], x.shape).reshape(-1, LANES)
    return jnp.take_along_axis(flat, tiled, axis=1).reshape(x.shape)


def forcing_kernel(slot_in, vel_in, past_in, metric_in, jac_in, w3_in, wmass_in, ds_in, dq_in, jright_in, jslope_in, jright_t_in, jleft_in, jleft_a_in, jleft_s_in, jleft_t_in, wfine_in, pack_ref, cross_ref, slot_ref, vel_ref, past_ref, metric_ref, jac_ref, w3_ref, wmass_ref, ds_ref, dq_ref, jright_ref, jslope_ref, jright_t_ref, jleft_ref, jleft_a_ref, jleft_s_ref, jleft_t_ref, wfine_ref, sems):
    sources = (slot_in, vel_in, past_in, metric_in, jac_in, w3_in, wmass_in, ds_in, dq_in, jright_in, jslope_in, jright_t_in, jleft_in, jleft_a_in, jleft_s_in, jleft_t_in, wfine_in)
    targets = (slot_ref, vel_ref, past_ref, metric_ref, jac_ref, w3_ref, wmass_ref, ds_ref, dq_ref, jright_ref, jslope_ref, jright_t_ref, jleft_ref, jleft_a_ref, jleft_s_ref, jleft_t_ref, wfine_ref)
    copies = [pltpu.make_async_copy(x, y, sems.at[k]) for k, (x, y) in enumerate(zip(sources, targets))]
    for copy in copies:
        copy.start()
    for copy in copies[:6]:
        copy.wait()
    even = parity() == 0
    jac = jac_ref[...]
    new, mid, old = vel_ref[0], vel_ref[1], vel_ref[2]
    guess = 3.0 * (new - mid) + old
    direct = (jac * w3_ref[...])[None] * (-10.0 * new + 16.0 * mid - 6.0 * old) + 3.0 * past_ref[0] - past_ref[1]
    lanes = to_lanes(jnp.concatenate([new, guess, direct, metric_ref[...], jac[None]], axis=0))
    new, guess, direct, metric, jac = lanes[0:3], lanes[3:6], lanes[6:9], lanes[9:12], lanes[12]
    for copy in copies[6:]:
        copy.wait()
    ds, dq = ds_ref[...], dq_ref[...]
    moved = [rows(new[i]) for i in range(3)]
    plain = moved + [rows(jac)] + [rows(new[d] * metric[d]) for d in range(3)]
    wide = full_right_dot(jnp.concatenate(plain, axis=0), jright_ref)
    slope = full_right_dot(jnp.concatenate(moved, axis=0), jslope_ref)
    scale = full_left_dot(jleft_ref, wide[192:256]) * wfine_ref[...]
    carry = [full_left_dot(jleft_ref, wide[256 + 64 * d : 320 + 64 * d]) for d in range(3)]
    products = []
    for i in range(3):
        part = wide[64 * i : 64 * i + 64]
        total = carry[0] * full_left_dot(jleft_a_ref, part) + carry[1] * full_left_dot(jleft_s_ref, part)
        total = total + carry[2] * full_left_dot(jleft_ref, slope[64 * i : 64 * i + 64])
        products.append(scale * total)
    coarse = full_left_dot(jleft_t_ref, jnp.concatenate(products, axis=1))
    coarse = full_right_dot(jnp.concatenate([coarse[:, 256 * i : 256 * i + 256] for i in range(3)], axis=0), jright_t_ref)
    mass = jac * wmass_ref[...]
    factor = [mass * metric[d] * metric[d] for d in range(3)]
    result = []
    for i in range(3):
        ga, gs, gq = gradient(guess[i], ds, dq)
        stiff = gradient_t(factor[0] * ga, factor[1] * gs, factor[2] * gq, ds, dq)
        result.append(direct[i] - 3.0 * planes(coarse[64 * i : 64 * i + 64]) - viscosity * stiff)
    result.extend([mass, metric[0], metric[1], metric[2]])
    lane = lax.broadcasted_iota(jnp.int32, (NP, LANES), 1)
    index = jnp.zeros((NP, LANES), jnp.int32)
    for e in range(ES):
        index = jnp.where((lane >> 3) == slot_ref[e], e * NP, index)
    index = index + (lane & 7)
    result = [take_lanes(x, index) for x in result]
    for k in range(4):
        joined = join_s(result[k])
        cross_ref[k] = jnp.where(even, joined[0], joined[NP - 1])
        pack_ref[NP * k : NP * k + NP] = joined if k < 3 else result[k]
    for k in range(4, 7):
        pack_ref[NP * k : NP * k + NP] = result[k]


def stage_kernel(pack_ref, out_ref, sem):
    copy = pltpu.make_async_copy(pack_ref, out_ref, sem)
    copy.start()
    copy.wait()


def pair_kernel(pack_ref, cross_in, out_ref):
    out_ref[: 7 * NP] = pack_ref[...]
    out_ref[7 * NP :] = cross_in[...]


def chip_rows(first, second):
    return jnp.concatenate([first[:-1], (first[-1] + second[0])[None], second[1:]], axis=0)


def own_rows(even, x):
    return jnp.where(even, x[:NP], x[NP - 1 :])


def edge_rows(even, x):
    return jnp.where(even, x[:EDGE], x[ROWS - EDGE :])


def divergence_kernel(own_ref, mate_ref, ds_ref, qright_t_ref, div_ref, op_ref, level_ref, cross_ref):
    even = parity() == 0
    own, mate = own_ref[...], mate_ref[...]
    packs = [jnp.where(even, own, mate), jnp.where(even, mate, own)]
    parts = [[pack[NP * k : NP * k + NP] for k in range(7)] for pack in packs]
    low, high = packs[0][7 * NP :], packs[1][7 * NP :]
    sides = []
    for k in range(4):
        first, second = parts[0][k], parts[1][k]
        if k == 3:
            first, second = join_s(first), join_s(second)
        whole = chip_rows(first, second)
        sides.append(jnp.concatenate([(whole[0] + low[k])[None], whole[1:-1], (whole[-1] + high[k])[None]], axis=0))
    inv = 1.0 / sides[3]
    accel = [sides[d] * inv for d in range(3)]
    div, last, levels = [], [], []
    for layer in range(2):
        mass = parts[layer][3]
        at = (NP - 1) * layer
        sums = []
        terms = []
        for d in range(3):
            one = mass * parts[layer][4 + d]
            two = one * parts[layer][4 + d]
            op_ref[layer, d] = two
            sums.append(jnp.sum(rows(two), axis=0, keepdims=True))
            terms.append(one * accel[d][at : at + NP])
        op_ref[layer, 3] = mass_shift * mass
        sums.append(jnp.sum(rows(mass), axis=0, keepdims=True))
        sums.append(jnp.zeros((4, LANES), jnp.float32))
        levels.append(jnp.concatenate(sums, axis=0))
        div.append(d_a(terms[0], True) + d_s(terms[1], ds_ref[1]))
        last.append(rows(terms[2]))
    last = full_right_dot(jnp.concatenate(last, axis=0), qright_t_ref)
    div = [join_s(x + planes(last[64 * k : 64 * k + 64])) for k, x in enumerate(div)]
    whole = chip_rows(div[0], div[1])
    div_ref[...] = whole
    cross_ref[:EDGE] = edge_rows(even, whole)
    level = jnp.where(even, levels[0], levels[1])
    level_ref[...] = level
    cross_ref[EDGE] = level


def half_window(even, local, received):
    edge = received[:EDGE]
    low = jnp.concatenate([edge[:-1], (edge[-1] + local[0])[None], local[1:EDGE]], axis=0)
    high = jnp.concatenate([local[ROWS - EDGE : -1], (local[-1] + edge[0])[None], edge[1:]], axis=0)
    return jnp.where(even, low, high)


def own_of_half(even, x):
    return jnp.where(even, x[NP : 2 * NP], x[1 : NP + 1])


def inverse_levels(levels, spread_ref, lam_ref):
    result = []
    for level in levels:
        level = full_dot(level, spread_ref[...])
        denom = level[0:1] * lam_ref[0] + level[1:2] * lam_ref[1] + level[2:3] * lam_ref[2] + mass_shift * level[3:4]
        result.append(1.0 / denom)
    return result


def schwarz(half, even, inv_ref, sleft_ref, sright_ref, srback_ref, sback_ref, scratch_ref, sum_ref):
    wide = NP + 2
    scratch_ref[...] = half.reshape((2 * NP + 1) * NP, LANES)
    none = jnp.zeros((16 - wide, LANES), jnp.float32)
    columns = []
    for layer in range(2):
        at = (NP - 1) * NP * layer
        before = roll(scratch_ref[pl.ds(at + NP - 2, wide, stride=NP), :], NP, 1)
        after = roll(scratch_ref[pl.ds(at + 1, wide, stride=NP), :], -NP, 1)
        own = half[(NP - 1) * layer : (NP - 1) * layer + wide].reshape(wide * NP, LANES)
        columns.append(jnp.concatenate([own, before, none, after, none], axis=0))
    spectra = [full_left_dot(sleft_ref, x) for x in columns]
    spectra = [full_right_dot(x, sright_ref) for x in spectra]
    spectra = [x * inv_ref[MODES * k : MODES * k + MODES] for k, x in enumerate(spectra)]
    spectra = [modes_dot(x, srback_ref) for x in spectra]
    blocks = [full_left_dot(sback_ref, x) for x in spectra]
    z = []
    for layer in range(2):
        part = blocks[layer]
        sum_ref[layer] = part[:80]
        for block, (s, shift) in enumerate(((NP - 2, -NP), (NP - 1, -NP), (0, NP), (1, NP))):
            rows_at = pl.ds(s, wide, stride=NP)
            start = 80 + 16 * block
            sum_ref[layer, rows_at, :] = sum_ref[layer, rows_at, :] + roll(part[start : start + wide], shift, 1)
        z.append(sum_ref[layer].reshape(wide, NP, LANES))
    upper = jnp.concatenate([z[0][8:] + z[1][1:3], z[1][3:]], axis=0)
    lower = jnp.concatenate([z[0][:7], z[0][7:9] + z[1][:2]], axis=0)
    return jnp.where(even, upper, lower)


def join_sides(even, own, mate):
    first, second = jnp.where(even, own, mate), jnp.where(even, mate, own)
    return jnp.concatenate([first[:6], first[6:] + second[:3], second[3:]], axis=0)


def operate(v, op_ref, ds_ref, qright_ref, qright_t_ref):
    ds = ds_ref[...]
    layers = [v[(NP - 1) * k : (NP - 1) * k + NP] for k in range(2)]
    gq = full_right_dot(jnp.concatenate([rows(x) for x in layers], axis=0), qright_ref)
    hq = [op_ref[k, 2] * planes(gq[64 * k : 64 * k + 64]) for k in range(2)]
    back = full_right_dot(jnp.concatenate([rows(x) for x in hq], axis=0), qright_t_ref)
    parts = []
    for k, x in enumerate(layers):
        local = d_a(op_ref[k, 0] * d_a(x, False), True) + d_s(op_ref[k, 1] * d_s(x, ds[0]), ds[1])
        parts.append(join_s(local + (op_ref[k, 3] * x + planes(back[64 * k : 64 * k + 64]))))
    return chip_rows(parts[0], parts[1])


def first_smooth_kernel(div_ref, received_ref, level_ref, spread_ref, lam_ref, sleft_ref, sright_ref, srback_ref, sback_ref, half_ref, inv_ref, part_ref, scratch_ref, sum_ref):
    even = parity() == 0
    half = half_window(even, div_ref[...], received_ref)
    half_ref[...] = half
    other = received_ref[EDGE]
    own = level_ref[...]
    levels = [jnp.where(even, other, own), jnp.where(even, own, other)]
    for k, inv in enumerate(inverse_levels(levels, spread_ref, lam_ref)):
        inv_ref[MODES * k : MODES * k + MODES] = inv
    part_ref[...] = schwarz(half, even, inv_ref, sleft_ref, sright_ref, srback_ref, sback_ref, scratch_ref, sum_ref)


def smooth_kernel(step, before_ref, local_ref, received_ref, inv_ref, sleft_ref, sright_ref, srback_ref, sback_ref, own_image_ref, half_ref, part_ref, scratch_ref, sum_ref):
    even = parity() == 0
    image = half_window(even, local_ref[...], received_ref)
    half = before_ref[...] - step * image
    half_ref[...] = half
    part_ref[...] = schwarz(half, even, inv_ref, sleft_ref, sright_ref, srback_ref, sback_ref, scratch_ref, sum_ref)
    own_image_ref[...] = own_of_half(even, image)


def operator_kernel(part_ref, mate_ref, op_ref, ds_ref, qright_ref, qright_t_ref, v_ref, local_ref, cross_ref):
    even = parity() == 0
    v = join_sides(even, part_ref[...], mate_ref[...])
    v_ref[...] = v
    local = operate(v, op_ref, ds_ref, qright_ref, qright_t_ref)
    local_ref[...] = local
    cross_ref[...] = edge_rows(even, local)


def fold(parts):
    lane = lax.broadcasted_iota(jnp.int32, (NP, LANES), 1)
    parts = parts + [jnp.zeros((NP, LANES), jnp.float32)] * (ES - len(parts))
    for step in (8, 16, 32, 64):
        chosen = (lane & step) != 0
        parts = [
            jnp.where(chosen, b, a) + roll(jnp.where(chosen, a, b), step, 1)
            for a, b in zip(parts[::2], parts[1::2])
        ]
    return parts[0]


def early_kernel(ws_ref, div_ref, v0_ref, v1_ref, l0_ref, l1_ref, residual_ref, parts_ref):
    ws = ws_ref[...]
    l0, l1 = l0_ref[...], l1_ref[...]
    residual = div_ref[...] - STEPS[0] * l0 - STEPS[1] * l1
    residual_ref[...] = residual
    v0, v1 = v0_ref[...], v1_ref[...]
    for k, (left, right) in enumerate(((v0, l0), (v0, l1), (v1, l1), (v0, residual), (v1, residual))):
        parts_ref[k] = jnp.sum(left * right, axis=0) * ws


def last_sums_kernel(part_ref, mate_ref, op_ref, ds_ref, qright_ref, parts_ref, l0_ref, l1_ref, residual_ref, ws_ref, v_ref, sums_ref):
    even = parity() == 0
    v = join_sides(even, part_ref[...], mate_ref[...])
    v_ref[...] = v
    layers = [v[(NP - 1) * k : (NP - 1) * k + NP] for k in range(2)]
    gq = full_right_dot(jnp.concatenate([rows(x) for x in layers], axis=0), qright_ref)
    energy = None
    for k, x in enumerate(layers):
        ga, gs, gq_k = d_a(x, False), d_s(x, ds_ref[0]), planes(gq[64 * k : 64 * k + 64])
        part = op_ref[k, 0] * ga * ga + op_ref[k, 1] * gs * gs + op_ref[k, 2] * gq_k * gq_k + op_ref[k, 3] * x * x
        part = jnp.sum(part, axis=0)
        energy = part if energy is None else energy + part
    ws = ws_ref[...]
    new = [jnp.sum(x[...] * v, axis=0) * ws for x in (l0_ref, l1_ref, residual_ref)]
    p = [parts_ref[k] for k in range(5)]
    folded = fold([p[0], p[1], new[0], p[2], new[1], energy, p[3], p[4], new[2]])
    line = jnp.broadcast_to(jnp.sum(folded, axis=0, keepdims=True), (NP, LANES))
    for k in range(sums_ref.shape[0] // NP):
        sums_ref[NP * k : NP * k + NP] = line


def last_operator_kernel(v_ref, op_ref, ds_ref, qright_ref, qright_t_ref, local_ref, face_ref):
    even = parity() == 0
    local = operate(v_ref[...], op_ref, ds_ref, qright_ref, qright_t_ref)
    local_ref[...] = local
    face_ref[...] = jnp.where(even, local[0], local[-1])


def to_output(x, order_ref, scratch_ref, slot):
    scratch_ref[slot] = rows(x)
    by_s = [scratch_ref[slot, pl.ds(s, NP, stride=NP), :] for s in range(NP - 1)]
    tiles = []
    for tile in range(7):
        index, s = order_ref[0, tile], order_ref[1, tile]
        value = jnp.take_along_axis(by_s[0], index, axis=1)
        for k in range(1, NP - 1):
            value = jnp.where(s == k, jnp.take_along_axis(by_s[k], index, axis=1), value)
        tiles.append(value)
    return jnp.concatenate(tiles, axis=1)


def layout_kernel(face_ref, v0_ref, v1_ref, v2_ref, half_ref, w0_ref, w1_ref, local_ref, order_ref, out_ref, scratch_ref):
    even = parity() == 0
    face = face_ref[...]
    local = own_rows(even, local_ref[...])
    first = jnp.where(even, local[0] + face, local[0])
    last = jnp.where(even, local[-1], local[-1] + face)
    w2 = jnp.concatenate([first[None], local[1:-1], last[None]], axis=0)
    fields = [own_rows(even, x[...]) for x in (v0_ref, v1_ref, v2_ref)]
    fields.extend((own_of_half(even, half_ref[...]), w0_ref[...], w1_ref[...], w2))
    for k, x in enumerate(fields):
        out_ref[k] = to_output(x, order_ref, scratch_ref, k)


def combine_kernel(sums_ref, fields_ref, p_ref, r_ref):
    line = jnp.sum(sums_ref[...], axis=0, keepdims=True)
    for step in (4, 2, 1):
        line = line + roll(line, -step, 1)
    shape = (NP, LANES)
    h00, h01, h02, h11, h12, h22, g0, g1, g2 = [jnp.broadcast_to(line[:, NP * k : NP * k + 1], shape) for k in range(9)]
    scale = 1.0 / h00
    m1, m2, m0 = h01 * scale, h02 * scale, g0 * scale
    k11, k12, k22 = h11 - m1 * h01, h12 - m1 * h02, h22 - m2 * h02
    f1, f2 = g1 - m1 * g0, g2 - m2 * g0
    second = 1.0 / k11
    n2 = k12 * second
    c2 = (f2 - n2 * f1) / (k22 - n2 * k12)
    c1 = f1 * second - n2 * c2
    c0 = m0 - m1 * c1 - m2 * c2
    for tile in range(7):
        x = [fields_ref[k, :, LANES * tile : LANES * tile + LANES] for k in range(7)]
        p_ref[:, LANES * tile : LANES * tile + LANES] = (c0 + STEPS[0]) * x[0] + (c1 + STEPS[1]) * x[1] + c2 * x[2]
        r_ref[:, LANES * tile : LANES * tile + LANES] = x[3] - (c0 * x[4] + c1 * x[5] + c2 * x[6])


def call(kernel, shapes, *args, scratch=()):
    return pl.pallas_call(
        kernel,
        out_shape=[jax.ShapeDtypeStruct(shape, jnp.float32) for shape in shapes],
        in_specs=[pl.BlockSpec(memory_space=pltpu.VMEM)] * len(args),
        out_specs=[pl.BlockSpec(memory_space=pltpu.VMEM)] * len(shapes),
        scratch_shapes=scratch,
        compiler_params=PARAMS,
    )(*args)


SMOOTH_SCRATCH = (
    pltpu.VMEM(((2 * NP + 1) * NP, LANES), jnp.float32),
    pltpu.VMEM((2, (NP + 2) * NP, LANES), jnp.float32),
)


def call_forcing(*args):
    shapes = [(7 * NP, NP, LANES), (4, NP, LANES)]
    scratch = [pltpu.SMEM(args[0].shape, jnp.int32)]
    scratch.extend(pltpu.VMEM(x.shape, x.dtype) for x in args[1:])
    scratch.append(pltpu.SemaphoreType.DMA((len(args),)))
    return pl.pallas_call(
        forcing_kernel,
        out_shape=[jax.ShapeDtypeStruct(shape, jnp.float32) for shape in shapes],
        in_specs=[pl.BlockSpec(memory_space=pltpu.HBM)] * len(args),
        out_specs=[pl.BlockSpec(memory_space=pltpu.VMEM)] * len(shapes),
        scratch_shapes=scratch,
        compiler_params=pltpu.CompilerParams(vmem_limit_bytes=FORCING_VMEM),
    )(*args)


FORCING_TABLES = ("w3", "wmass", "ds", "dq", "jright", "jslope", "jright_t", "jleft", "jleft_a", "jleft_s", "jleft_t", "wfine")


def team_groups(count):
    return [[2 * c + side for c in range(count // 2)] for side in range(2)]


def shards(velocity, conv_past, metric, jacobian, element_slot):
    count = lax.axis_size("dom")
    t = {key: jnp.asarray(value) for key, value in TAB.items()}
    field = (NP, NP, LANES)
    chip = (ROWS, NP, LANES)
    half_shape = (2 * NP + 1, NP, LANES)
    edge = (EDGE, NP, LANES)
    pack, cross = call_forcing(
        element_slot, velocity, conv_past, metric, jacobian, *(t[key] for key in FORCING_TABLES)
    )
    cross = swap_cross(cross, count)
    pack = pl.pallas_call(
        stage_kernel,
        out_shape=jax.ShapeDtypeStruct(pack.shape, jnp.float32),
        in_specs=[pl.BlockSpec(memory_space=pltpu.HBM)],
        out_specs=pl.BlockSpec(memory_space=pltpu.VMEM),
        scratch_shapes=[pltpu.SemaphoreType.DMA(())],
        compiler_params=PARAMS,
    )(pack)
    (own,) = call(pair_kernel, [(7 * NP + 4, NP, LANES)], pack, cross)
    mate = swap_inner(own, count)
    div, op, level, cross = call(
        divergence_kernel,
        [chip, (2, 4) + field, (NP, LANES), (EDGE + 1, NP, LANES)],
        own, mate, t["ds"], t["qright_t"],
    )
    solve = (t["sleft"], t["sright"], t["srback"], t["sback"])
    tables = (op, t["ds"], t["qright"], t["qright_t"])
    half, inv, part = call(
        first_smooth_kernel,
        [half_shape, (2 * MODES, ES * (NP + 2)), edge],
        div, swap_cross(cross, count), level, t["spread"], t["lam"], *solve,
        scratch=SMOOTH_SCRATCH,
    )
    vectors, locals_, images = [], [], []
    for step in STEPS:
        v, local, cross = call(
            operator_kernel, [chip, chip, edge], part, swap_inner(part, count), *tables
        )
        image, half, part = call(
            functools.partial(smooth_kernel, step),
            [field, half_shape, edge],
            half, local, swap_cross(cross, count), inv, *solve,
            scratch=SMOOTH_SCRATCH,
        )
        vectors.append(v)
        locals_.append(local)
        images.append(image)
    residual, parts = call(
        early_kernel, [chip, (5, NP, LANES)], t["ws"], div, *vectors, *locals_
    )
    v, sums = call(
        last_sums_kernel,
        [chip, (count // 2, LANES)],
        part, swap_inner(part, count), op, t["ds"], t["qright"], parts, *locals_, residual, t["ws"],
    )
    sums = lax.all_to_all(sums, "dom", 0, 0, tiled=True, axis_index_groups=team_groups(count))
    local, face = call(last_operator_kernel, [chip, (NP, LANES)], v, *tables)
    (fields,) = call(
        layout_kernel,
        [(7, NP, 896)],
        swap_cross(face, count), *vectors, v, half, *images, local, t["order"],
        scratch=[pltpu.VMEM((7, NP * NP, LANES), jnp.float32)],
    )
    return tuple(call(combine_kernel, [(NP, 896), (NP, 896)], sums, fields))


def solution(mesh):
    return jax.shard_map(
        shards,
        mesh=mesh,
        in_specs=(
            P(None, None, "dom", None),
            P(None, None, "dom", None),
            P(None, "dom", None),
            P("dom", None),
            P("dom"),
        ),
        out_specs=(P("dom", None), P("dom", None)),
        check_vma=False,
    )
```

```python
import functools

import jax
import jax.numpy as jnp
import numpy as np
from jax import lax
from jax.experimental import pallas as pl
from jax.experimental.pallas import tpu as pltpu
from jax.sharding import PartitionSpec as P

NP = 8
NF = 12
ES = 16
LANES = 128
time_step = 0.25
viscosity = 0.05
mass_shift = 0.001
STEPS = (0.45, 0.3)
VMEM = 48 * 1024 * 1024
FORCING_VMEM = 56 * 1024 * 1024
ROWS = 2 * NP - 1
EDGE = NP + 1
MODES = 112


def legendre_pair(points, order):
    before = np.ones(points.shape)
    current = points * 1.0
    for level in range(2, order + 1):
        nextone = ((2 * level - 1) * points * current - (level - 1) * before) / level
        before = current
        current = nextone
    return (current, before)


def jacobi_eigen(matrix):
    size = matrix.shape[0]
    work = matrix * 1.0
    vectors = np.eye(size)
    for sweep in range(30):
        for first in range(size - 1):
            for second in range(first + 1, size):
                off = float(work[first, second])
                if abs(off) > 1e-300:
                    tau = (float(work[second, second]) - float(work[first, first])) / (2.0 * off)
                    if tau >= 0.0:
                        tangent = 1.0 / (tau + (1.0 + tau * tau) ** 0.5)
                    else:
                        tangent = -1.0 / (-tau + (1.0 + tau * tau) ** 0.5)
                    cosine = 1.0 / (1.0 + tangent * tangent) ** 0.5
                    sine = tangent * cosine
                    rotation = np.eye(size)
                    rotation[first, first] = cosine
                    rotation[second, second] = cosine
                    rotation[first, second] = sine
                    rotation[second, first] = -sine
                    work = rotation.T @ work @ rotation
                    vectors = vectors @ rotation
    diagonal_index = np.arange(size)
    return (work[diagonal_index, diagonal_index], vectors)


def base_tables(points_edge, points_fine):
    degree = points_edge - 1
    points = -np.cos(np.pi * np.arange(points_edge) / degree)
    for sweep in range(100):
        top, below = legendre_pair(points, degree)
        points = points - (points * top - below) / (points_edge * top)
    top, below = legendre_pair(points, degree)
    weight_gll = 2.0 / (degree * points_edge * top**2)
    spacing = points[:, None] - points[None, :] + np.eye(points_edge)
    barycentric = 1.0 / np.prod(spacing, axis=1)
    derivative = barycentric[None, :] / barycentric[:, None] / spacing
    derivative = derivative * (1.0 - np.eye(points_edge))
    derivative = derivative - np.eye(points_edge) * derivative.sum(axis=1)[:, None]
    fine_points = np.cos(np.pi * (np.arange(points_fine) + 0.75) / (points_fine + 0.5))
    for sweep in range(100):
        top, below = legendre_pair(fine_points, points_fine)
        slope = points_fine * (fine_points * top - below) / (fine_points * fine_points - 1.0)
        fine_points = fine_points - top / slope
    top, below = legendre_pair(fine_points, points_fine)
    slope = points_fine * (fine_points * top - below) / (fine_points * fine_points - 1.0)
    fine_weight = 2.0 / ((1.0 - fine_points * fine_points) * slope * slope)
    fine_points = fine_points[::-1]
    fine_weight = fine_weight[::-1]
    interpolate = np.ones((points_fine, points_edge))
    for column in range(points_edge):
        for other in range(points_edge):
            if other != column:
                interpolate[:, column] = (
                    interpolate[:, column]
                    * (fine_points - points[other])
                    / (points[column] - points[other])
                )
    stiffness = derivative.T @ (weight_gll[:, None] * derivative)
    extent = 3 * degree + 1
    joined_stiff = np.zeros((extent, extent))
    joined_mass = np.zeros(extent)
    for segment in range(3):
        offset = segment * degree
        joined_stiff[offset : offset + points_edge, offset : offset + points_edge] += stiffness
        joined_mass[offset : offset + points_edge] += weight_gll
    low = degree - 1
    high = 2 * degree + 2
    root_mass = np.sqrt(joined_mass[low:high])
    scaled = joined_stiff[low:high, low:high] / root_mass[:, None] / root_mass[None, :]
    scaled = 0.5 * (scaled + scaled.T)
    eigen_values, eigen_vectors = jacobi_eigen(scaled)
    solve_mat = eigen_vectors / root_mass[:, None]
    breadth = high - low
    return dict(
        derivative=derivative,
        interpolate=interpolate,
        weight=weight_gll,
        fine_weight=fine_weight,
        solve=solve_mat,
        eigen=eigen_values,
    )


def f32(value):
    return np.ascontiguousarray(value, dtype=np.float32)


def halves(value):
    value = np.asarray(value, dtype=np.float32)
    high = value.astype(jnp.bfloat16)
    rest = (value - high.astype(np.float32)).astype(jnp.bfloat16)
    return high, rest


def for_left(value):
    high, rest = halves(value)
    return np.concatenate([high, rest, high], axis=1)


def for_right(value):
    high, rest = halves(value)
    return np.concatenate([high, rest, high], axis=0)


def by_modes_right(value):
    high, rest = halves(by_modes(value, 0))
    parts = (high, rest, high)
    return np.concatenate([x[:LANES] for x in parts] + [x[LANES:] for x in parts])


def pair(value):
    return np.stack(halves(value))


def by_modes(value, axis):
    at = np.arange(ES * (NP + 2))
    order = np.concatenate([at[at % (NP + 2) < NP], at[at % (NP + 2) >= NP]])
    return np.take(value, order, axis=axis)


def make_tables():
    base = base_tables(NP, NF)
    deriv, interp, solve, eigen = base["derivative"], base["interpolate"], base["solve"], base["eigen"]
    w, wf = base["weight"], base["fine_weight"]
    out = {}
    index = np.arange(NP)

    def sublane(matrix):
        rows = [matrix[index, (index + shift) % NP] for shift in range(NP)]
        return f32(np.broadcast_to(np.stack(rows)[:, :, None], (NP, NP, LANES)))

    def lane(matrix):
        rows = [np.tile(matrix[index, (index + shift) % NP], ES) for shift in range(NP)]
        return f32(np.broadcast_to(np.stack(rows)[:, None, :], (NP, NP, LANES)))

    out["ds"] = np.stack([sublane(deriv), sublane(deriv.T)])
    out["dq"] = np.stack([lane(deriv), lane(deriv.T)])
    out["qright"] = for_right(np.kron(np.eye(ES), deriv.T))
    out["qright_t"] = for_right(np.kron(np.eye(ES), deriv))
    out["w3"] = f32(np.einsum("a,s,q->asq", w, w, w).reshape(1, 512))
    out["wmass"] = f32(np.tile(np.einsum("a,s,q->asq", w, w, w), (1, 1, ES)))
    both = interp @ deriv
    pad = np.zeros((16 - NF, NP))
    line = np.concatenate([interp, pad])
    slope = np.concatenate([both, pad])
    out["jright"] = for_right(np.kron(np.eye(ES), line.T))
    out["jslope"] = for_right(np.kron(np.eye(ES), slope.T))
    out["jright_t"] = pair(np.kron(np.eye(ES), line))
    out["jleft"] = for_left(np.kron(interp, interp))
    out["jleft_a"] = for_left(np.kron(both, interp))
    out["jleft_s"] = for_left(np.kron(interp, both))
    out["jleft_t"] = for_left(np.kron(interp, interp).T)
    wide_wf = np.concatenate([wf, np.zeros(16 - NF)])
    out["wfine"] = f32(np.kron(np.kron(wf, wf)[:, None], np.tile(wide_wf, ES)[None, :]))
    at = np.arange(7 * LANES)
    element, within = at // 56, at % 56
    order = np.stack([element * NP + within % NP, within // NP]).reshape(2, 7, 1, LANES)
    out["order"] = np.ascontiguousarray(np.broadcast_to(order, (2, 7, NP, LANES)), dtype=np.int32)
    wide = NP + 2
    left = np.zeros((MODES, 112))
    back = np.zeros((144, MODES))
    at = np.arange(wide)
    for i in range(wide):
        for j in range(wide):
            row = i * wide + j
            inside = np.outer(solve[:, i], solve[1:-1, j]).reshape(80)
            left[row, :80] = inside
            left[row, 80 + at] = solve[:, i] * solve[0, j]
            left[row, 96 + at] = solve[:, i] * solve[wide - 1, j]
            back[:80, row] = inside
            for block, s in enumerate((0, 1, wide - 2, wide - 1)):
                back[80 + 16 * block + at, row] = solve[:, i] * solve[s, j]
    out["sleft"] = for_left(left)
    out["sback"] = for_left(back)
    out["sright"] = for_right(by_modes(np.kron(np.eye(ES), solve[1:-1, :]), 1))
    out["srback"] = by_modes_right(np.kron(np.eye(ES), solve[1:-1, :].T))
    out["spread"] = f32(by_modes(np.kron(np.eye(ES), np.ones((NP, wide))), 1) / 8.0)
    lam_a = np.zeros((MODES, 1))
    lam_s = np.zeros((MODES, 1))
    lam_a[:100, 0] = np.repeat(eigen, wide)
    lam_s[:100, 0] = np.tile(eigen, wide)
    lam_q = by_modes(np.tile(eigen, ES)[None, :], 1)
    full = (MODES, ES * wide)
    out["lam"] = f32(np.stack([np.broadcast_to(lam_a, full), np.broadcast_to(lam_s, full), np.broadcast_to(lam_q, full)]))
    half = np.ones(NP)
    half[0] = half[-1] = 0.5
    out["ws"] = f32(np.broadcast_to(half[:, None], (NP, LANES)))
    return out


TAB = make_tables()
DERIV = [[float(x) for x in row] for row in base_tables(NP, NF)["derivative"].astype(np.float32)]
PARAMS = pltpu.CompilerParams(vmem_limit_bytes=VMEM)


def full_dot(left, right):
    return jnp.dot(left, right, precision=lax.Precision.HIGHEST, preferred_element_type=jnp.float32)


def short_dot(left, right):
    return jnp.dot(left, right, preferred_element_type=jnp.float32)


def split(x):
    high = x.astype(jnp.bfloat16)
    return high, (x - high.astype(jnp.float32)).astype(jnp.bfloat16)


def left_dot(table_ref, x):
    high, rest = split(x)
    return short_dot(table_ref[...], jnp.concatenate([high, high, rest], axis=0))


def right_dot(x, table_ref):
    high, rest = split(x)
    return short_dot(jnp.concatenate([high, high, rest], axis=1), table_ref[...])


def modes_dot(x, table_ref):
    high, rest = split(x)
    parts = (high, high, rest)
    whole = [y[:, :LANES] for y in parts] + [y[:, LANES:] for y in parts]
    return short_dot(jnp.concatenate(whole, axis=1), table_ref[...])


def pair_dot(x, table_ref):
    high, rest = split(x)
    return short_dot(high, table_ref[0]) + (short_dot(high, table_ref[1]) + short_dot(rest, table_ref[0]))


def roll(x, shift, axis):
    return pltpu.roll(x, shift % x.shape[axis], axis)


def d_a(x, transposed):
    rows = []
    for a in range(NP):
        total = None
        for b in range(NP):
            term = (DERIV[b][a] if transposed else DERIV[a][b]) * x[b]
            total = term if total is None else total + term
        rows.append(total)
    return jnp.stack(rows)


def d_s(x, coef):
    total = coef[0][None] * x
    for shift in range(1, NP):
        total = total + coef[shift][None] * roll(x, -shift, 1)
    return total


def d_q(x, coef):
    flat = x.reshape(-1, LANES)
    lane = lax.broadcasted_iota(jnp.int32, flat.shape, 1)
    total = coef[0][None] * x
    for shift in range(1, NP):
        index = (lane & (LANES - NP)) | ((lane + shift) & (NP - 1))
        total = total + coef[shift][None] * jnp.take_along_axis(flat, index, axis=1).reshape(x.shape)
    return total


def gradient(x, ds, dq):
    return d_a(x, False), d_s(x, ds[0]), d_q(x, dq[0])


def gradient_t(xa, xs, xq, ds, dq):
    return d_a(xa, True) + d_s(xs, ds[1]) + d_q(xq, dq[1])


def join_s(x):
    s = lax.broadcasted_iota(jnp.int32, x.shape, 1)
    from_before = roll(roll(x, NP, 2), 1, 1)
    from_after = roll(roll(x, -NP, 2), -1, 1)
    zero = jnp.zeros_like(x)
    return x + jnp.where(s == 0, from_before, jnp.where(s == NP - 1, from_after, zero))


def parity():
    return lax.rem(lax.axis_index("dom"), 2)


def swap_inner(x, count):
    return lax.ppermute(x, "dom", [(i, i ^ 1) for i in range(count)])


def swap_cross(x, count):
    pairs = [(i, (i + 1) % count if i % 2 else (i - 1) % count) for i in range(count)]
    return lax.ppermute(x, "dom", pairs)


def to_lanes(x):
    shape = (x.shape[0], NP, LANES)
    lane = lax.broadcasted_iota(jnp.int32, shape, 2)
    pieces = []
    for tile in range(4):
        first = x[:, :8, tile * LANES : (tile + 1) * LANES]
        second = x[:, 8:, tile * LANES : (tile + 1) * LANES]
        pieces.append(jnp.where(lane < 64, first, roll(second, 64, 2)))
        pieces.append(jnp.where(lane < 64, roll(first, 64, 2), second))
    y = jnp.stack(pieces, axis=1).reshape(x.shape[0] * NP, NP, LANES)
    sub = lax.broadcasted_iota(jnp.int32, y.shape, 1)
    lane = lax.broadcasted_iota(jnp.int32, y.shape, 2)
    for bit in range(3):
        step = 1 << bit
        in_sub = (sub & step) != 0
        in_lane = (lane & (step * 8)) != 0
        flat = y.reshape(-1, LANES)
        swapped = jnp.take_along_axis(flat, lane.reshape(-1, LANES) ^ (step * 8), axis=1).reshape(y.shape)
        if step == 4:
            moved = roll(swapped, step, 1)
        else:
            moved = jnp.where(in_sub, roll(swapped, step, 1), roll(swapped, -step, 1))
        y = jnp.where(in_sub == in_lane, y, moved)
    return y.reshape(x.shape[0], NP, NP, LANES)


def rows(x):
    return x.reshape(NP * NP, LANES)


def planes(x):
    return x.reshape(NP, NP, LANES)


def take_lanes(x, index):
    flat = x.reshape(-1, LANES)
    tiled = jnp.broadcast_to(index[None], x.shape).reshape(-1, LANES)
    return jnp.take_along_axis(flat, tiled, axis=1).reshape(x.shape)


def forcing_kernel(slot_in, vel_in, past_in, metric_in, jac_in, w3_in, wmass_in, ds_in, dq_in, jright_in, jslope_in, jright_t_in, jleft_in, jleft_a_in, jleft_s_in, jleft_t_in, wfine_in, pack_out, cross_out, slot_ref, vel_ref, past_ref, metric_ref, jac_ref, w3_ref, wmass_ref, ds_ref, dq_ref, jright_ref, jslope_ref, jright_t_ref, jleft_ref, jleft_a_ref, jleft_s_ref, jleft_t_ref, wfine_ref, pack_ref, cross_ref, sems, out_sems):
    sources = (slot_in, vel_in, past_in, metric_in, jac_in, w3_in, wmass_in, ds_in, dq_in, jright_in, jslope_in, jright_t_in, jleft_in, jleft_a_in, jleft_s_in, jleft_t_in, wfine_in)
    targets = (slot_ref, vel_ref, past_ref, metric_ref, jac_ref, w3_ref, wmass_ref, ds_ref, dq_ref, jright_ref, jslope_ref, jright_t_ref, jleft_ref, jleft_a_ref, jleft_s_ref, jleft_t_ref, wfine_ref)
    copies = [pltpu.make_async_copy(x, y, sems.at[k]) for k, (x, y) in enumerate(zip(sources, targets))]
    for copy in copies:
        copy.start()
    for copy in copies[:6]:
        copy.wait()
    even = parity() == 0
    jac = jac_ref[...]
    new, mid, old = vel_ref[0], vel_ref[1], vel_ref[2]
    guess = 3.0 * (new - mid) + old
    direct = (jac * w3_ref[...])[None] * (-10.0 * new + 16.0 * mid - 6.0 * old) + 3.0 * past_ref[0] - past_ref[1]
    lanes = to_lanes(jnp.concatenate([new, guess, direct, metric_ref[...], jac[None]], axis=0))
    new, guess, direct, metric, jac = lanes[0:3], lanes[3:6], lanes[6:9], lanes[9:12], lanes[12]
    leaving = []

    def send(k, value):
        at = pl.ds(NP * k, NP)
        pack_ref[at] = value
        copy = pltpu.make_async_copy(pack_ref.at[at], pack_out.at[at], out_sems.at[k])
        copy.start()
        leaving.append(copy)

    for copy in copies[6:]:
        copy.wait()
    mass = jac * wmass_ref[...]
    lane = lax.broadcasted_iota(jnp.int32, (NP, LANES), 1)
    index = jnp.zeros((NP, LANES), jnp.int32)
    for e in range(ES):
        index = jnp.where((lane >> 3) == slot_ref[e], e * NP, index)
    index = index + (lane & 7)
    sorted_mass = take_lanes(mass, index)
    joined = join_s(sorted_mass)
    cross_ref[3] = jnp.where(even, joined[0], joined[NP - 1])
    send(3, sorted_mass)
    for k in range(3):
        send(4 + k, take_lanes(metric[k], index))
    ds, dq = ds_ref[...], dq_ref[...]
    moved = [rows(new[i]) for i in range(3)]
    plain = moved + [rows(jac)] + [rows(new[d] * metric[d]) for d in range(3)]
    wide = right_dot(jnp.concatenate(plain, axis=0), jright_ref)
    slope = right_dot(jnp.concatenate(moved, axis=0), jslope_ref)
    scale = left_dot(jleft_ref, wide[192:256]) * wfine_ref[...]
    carry = [left_dot(jleft_ref, wide[256 + 64 * d : 320 + 64 * d]) for d in range(3)]
    products = []
    for i in range(3):
        part = wide[64 * i : 64 * i + 64]
        total = carry[0] * left_dot(jleft_a_ref, part) + carry[1] * left_dot(jleft_s_ref, part)
        total = total + carry[2] * left_dot(jleft_ref, slope[64 * i : 64 * i + 64])
        products.append(scale * total)
    coarse = left_dot(jleft_t_ref, jnp.concatenate(products, axis=1))
    coarse = pair_dot(jnp.concatenate([coarse[:, 256 * i : 256 * i + 256] for i in range(3)], axis=0), jright_t_ref)
    factor = [mass * metric[d] * metric[d] for d in range(3)]
    result = []
    for i in range(3):
        ga, gs, gq = gradient(guess[i], ds, dq)
        stiff = gradient_t(factor[0] * ga, factor[1] * gs, factor[2] * gq, ds, dq)
        result.append(direct[i] - 3.0 * planes(coarse[64 * i : 64 * i + 64]) - viscosity * stiff)
    for k in range(3):
        joined = join_s(take_lanes(result[k], index))
        cross_ref[k] = jnp.where(even, joined[0], joined[NP - 1])
        send(k, joined)
    copy = pltpu.make_async_copy(cross_ref, cross_out, out_sems.at[7])
    copy.start()
    for copy in leaving + [copy]:
        copy.wait()


def stage_kernel(pack_ref, out_ref, sem):
    copy = pltpu.make_async_copy(pack_ref, out_ref, sem)
    copy.start()
    copy.wait()


def pair_kernel(pack_ref, cross_in, out_ref):
    out_ref[: 7 * NP] = pack_ref[...]
    out_ref[7 * NP :] = cross_in[...]


def chip_rows(first, second):
    return jnp.concatenate([first[:-1], (first[-1] + second[0])[None], second[1:]], axis=0)


def own_rows(even, x):
    return jnp.where(even, x[:NP], x[NP - 1 :])


def edge_rows(even, x):
    return jnp.where(even, x[:EDGE], x[ROWS - EDGE :])


def divergence_kernel(own_ref, mate_ref, ds_ref, qright_t_ref, div_ref, op_ref, level_ref, cross_ref):
    even = parity() == 0
    own, mate = own_ref[...], mate_ref[...]
    packs = [jnp.where(even, own, mate), jnp.where(even, mate, own)]
    parts = [[pack[NP * k : NP * k + NP] for k in range(7)] for pack in packs]
    low, high = packs[0][7 * NP :], packs[1][7 * NP :]
    sides = []
    for k in range(4):
        first, second = parts[0][k], parts[1][k]
        if k == 3:
            first, second = join_s(first), join_s(second)
        whole = chip_rows(first, second)
        sides.append(jnp.concatenate([(whole[0] + low[k])[None], whole[1:-1], (whole[-1] + high[k])[None]], axis=0))
    inv = 1.0 / sides[3]
    accel = [sides[d] * inv for d in range(3)]
    div, last, levels = [], [], []
    for layer in range(2):
        mass = parts[layer][3]
        at = (NP - 1) * layer
        sums = []
        terms = []
        for d in range(3):
            one = mass * parts[layer][4 + d]
            two = one * parts[layer][4 + d]
            op_ref[layer, d] = two
            sums.append(jnp.sum(rows(two), axis=0, keepdims=True))
            terms.append(one * accel[d][at : at + NP])
        op_ref[layer, 3] = mass_shift * mass
        sums.append(jnp.sum(rows(mass), axis=0, keepdims=True))
        sums.append(jnp.zeros((4, LANES), jnp.float32))
        levels.append(jnp.concatenate(sums, axis=0))
        div.append(d_a(terms[0], True) + d_s(terms[1], ds_ref[1]))
        last.append(rows(terms[2]))
    last = right_dot(jnp.concatenate(last, axis=0), qright_t_ref)
    div = [join_s(x + planes(last[64 * k : 64 * k + 64])) for k, x in enumerate(div)]
    whole = chip_rows(div[0], div[1])
    div_ref[...] = whole
    cross_ref[:EDGE] = edge_rows(even, whole)
    level = jnp.where(even, levels[0], levels[1])
    level_ref[...] = level
    cross_ref[EDGE] = level


def half_window(even, local, received):
    edge = received[:EDGE]
    low = jnp.concatenate([edge[:-1], (edge[-1] + local[0])[None], local[1:EDGE]], axis=0)
    high = jnp.concatenate([local[ROWS - EDGE : -1], (local[-1] + edge[0])[None], edge[1:]], axis=0)
    return jnp.where(even, low, high)


def own_of_half(even, x):
    return jnp.where(even, x[NP : 2 * NP], x[1 : NP + 1])


def inverse_levels(levels, spread_ref, lam_ref):
    result = []
    for level in levels:
        level = full_dot(level, spread_ref[...])
        denom = level[0:1] * lam_ref[0] + level[1:2] * lam_ref[1] + level[2:3] * lam_ref[2] + mass_shift * level[3:4]
        result.append(1.0 / denom)
    return result


def schwarz(half, even, inv_ref, sleft_ref, sright_ref, srback_ref, sback_ref, scratch_ref, sum_ref):
    wide = NP + 2
    scratch_ref[...] = half.reshape((2 * NP + 1) * NP, LANES)
    none = jnp.zeros((16 - wide, LANES), jnp.float32)
    columns = []
    for layer in range(2):
        at = (NP - 1) * NP * layer
        before = roll(scratch_ref[pl.ds(at + NP - 2, wide, stride=NP), :], NP, 1)
        after = roll(scratch_ref[pl.ds(at + 1, wide, stride=NP), :], -NP, 1)
        own = half[(NP - 1) * layer : (NP - 1) * layer + wide].reshape(wide * NP, LANES)
        columns.append(jnp.concatenate([own, before, none, after, none], axis=0))
    spectra = [left_dot(sleft_ref, x) for x in columns]
    spectra = [right_dot(x, sright_ref) for x in spectra]
    spectra = [x * inv_ref[MODES * k : MODES * k + MODES] for k, x in enumerate(spectra)]
    spectra = [modes_dot(x, srback_ref) for x in spectra]
    blocks = [left_dot(sback_ref, x) for x in spectra]
    z = []
    for layer in range(2):
        part = blocks[layer]
        sum_ref[layer] = part[:80]
        for block, (s, shift) in enumerate(((NP - 2, -NP), (NP - 1, -NP), (0, NP), (1, NP))):
            rows_at = pl.ds(s, wide, stride=NP)
            start = 80 + 16 * block
            sum_ref[layer, rows_at, :] = sum_ref[layer, rows_at, :] + roll(part[start : start + wide], shift, 1)
        z.append(sum_ref[layer].reshape(wide, NP, LANES))
    upper = jnp.concatenate([z[0][8:] + z[1][1:3], z[1][3:]], axis=0)
    lower = jnp.concatenate([z[0][:7], z[0][7:9] + z[1][:2]], axis=0)
    return jnp.where(even, upper, lower)


def join_sides(even, own, mate):
    first, second = jnp.where(even, own, mate), jnp.where(even, mate, own)
    return jnp.concatenate([first[:6], first[6:] + second[:3], second[3:]], axis=0)


def operate(v, op_ref, ds_ref, qright_ref, qright_t_ref):
    ds = ds_ref[...]
    layers = [v[(NP - 1) * k : (NP - 1) * k + NP] for k in range(2)]
    gq = right_dot(jnp.concatenate([rows(x) for x in layers], axis=0), qright_ref)
    hq = [op_ref[k, 2] * planes(gq[64 * k : 64 * k + 64]) for k in range(2)]
    back = right_dot(jnp.concatenate([rows(x) for x in hq], axis=0), qright_t_ref)
    parts = []
    for k, x in enumerate(layers):
        local = d_a(op_ref[k, 0] * d_a(x, False), True) + d_s(op_ref[k, 1] * d_s(x, ds[0]), ds[1])
        parts.append(join_s(local + (op_ref[k, 3] * x + planes(back[64 * k : 64 * k + 64]))))
    return chip_rows(parts[0], parts[1])


def first_smooth_kernel(div_ref, received_ref, level_ref, spread_ref, lam_ref, sleft_ref, sright_ref, srback_ref, sback_ref, half_ref, inv_ref, part_ref, scratch_ref, sum_ref):
    even = parity() == 0
    half = half_window(even, div_ref[...], received_ref)
    half_ref[...] = half
    other = received_ref[EDGE]
    own = level_ref[...]
    levels = [jnp.where(even, other, own), jnp.where(even, own, other)]
    for k, inv in enumerate(inverse_levels(levels, spread_ref, lam_ref)):
        inv_ref[MODES * k : MODES * k + MODES] = inv
    part_ref[...] = schwarz(half, even, inv_ref, sleft_ref, sright_ref, srback_ref, sback_ref, scratch_ref, sum_ref)


def smooth_kernel(step, before_ref, local_ref, received_ref, inv_ref, sleft_ref, sright_ref, srback_ref, sback_ref, own_image_ref, half_ref, part_ref, scratch_ref, sum_ref):
    even = parity() == 0
    image = half_window(even, local_ref[...], received_ref)
    half = before_ref[...] - step * image
    half_ref[...] = half
    part_ref[...] = schwarz(half, even, inv_ref, sleft_ref, sright_ref, srback_ref, sback_ref, scratch_ref, sum_ref)
    own_image_ref[...] = own_of_half(even, image)


def operator_kernel(part_ref, mate_ref, op_ref, ds_ref, qright_ref, qright_t_ref, v_ref, local_ref, cross_ref):
    even = parity() == 0
    v = join_sides(even, part_ref[...], mate_ref[...])
    v_ref[...] = v
    local = operate(v, op_ref, ds_ref, qright_ref, qright_t_ref)
    local_ref[...] = local
    cross_ref[...] = edge_rows(even, local)


def fold(parts):
    lane = lax.broadcasted_iota(jnp.int32, (NP, LANES), 1)
    parts = parts + [jnp.zeros((NP, LANES), jnp.float32)] * (ES - len(parts))
    for step in (8, 16, 32, 64):
        chosen = (lane & step) != 0
        parts = [
            jnp.where(chosen, b, a) + roll(jnp.where(chosen, a, b), step, 1)
            for a, b in zip(parts[::2], parts[1::2])
        ]
    return parts[0]


def early_kernel(ws_ref, div_ref, v0_ref, v1_ref, l0_ref, l1_ref, residual_ref, parts_ref):
    ws = ws_ref[...]
    l0, l1 = l0_ref[...], l1_ref[...]
    residual = div_ref[...] - STEPS[0] * l0 - STEPS[1] * l1
    residual_ref[...] = residual
    v0, v1 = v0_ref[...], v1_ref[...]
    for k, (left, right) in enumerate(((v0, l0), (v0, l1), (v1, l1), (v0, residual), (v1, residual))):
        parts_ref[k] = jnp.sum(left * right, axis=0) * ws


def last_sums_kernel(part_ref, mate_ref, op_ref, ds_ref, qright_ref, parts_ref, l0_ref, l1_ref, residual_ref, ws_ref, v_ref, sums_ref):
    even = parity() == 0
    v = join_sides(even, part_ref[...], mate_ref[...])
    v_ref[...] = v
    layers = [v[(NP - 1) * k : (NP - 1) * k + NP] for k in range(2)]
    gq = right_dot(jnp.concatenate([rows(x) for x in layers], axis=0), qright_ref)
    energy = None
    for k, x in enumerate(layers):
        ga, gs, gq_k = d_a(x, False), d_s(x, ds_ref[0]), planes(gq[64 * k : 64 * k + 64])
        part = op_ref[k, 0] * ga * ga + op_ref[k, 1] * gs * gs + op_ref[k, 2] * gq_k * gq_k + op_ref[k, 3] * x * x
        part = jnp.sum(part, axis=0)
        energy = part if energy is None else energy + part
    ws = ws_ref[...]
    new = [jnp.sum(x[...] * v, axis=0) * ws for x in (l0_ref, l1_ref, residual_ref)]
    p = [parts_ref[k] for k in range(5)]
    folded = fold([p[0], p[1], new[0], p[2], new[1], energy, p[3], p[4], new[2]])
    line = jnp.broadcast_to(jnp.sum(folded, axis=0, keepdims=True), (NP, LANES))
    for k in range(sums_ref.shape[0] // NP):
        sums_ref[NP * k : NP * k + NP] = line


def last_operator_kernel(v_ref, op_ref, ds_ref, qright_ref, qright_t_ref, local_ref, face_ref):
    even = parity() == 0
    local = operate(v_ref[...], op_ref, ds_ref, qright_ref, qright_t_ref)
    local_ref[...] = local
    face_ref[...] = jnp.where(even, local[0], local[-1])


def to_output(x, order_ref, scratch_ref, slot):
    scratch_ref[slot] = rows(x)
    by_s = [scratch_ref[slot, pl.ds(s, NP, stride=NP), :] for s in range(NP - 1)]
    tiles = []
    for tile in range(7):
        index, s = order_ref[0, tile], order_ref[1, tile]
        value = jnp.take_along_axis(by_s[0], index, axis=1)
        for k in range(1, NP - 1):
            value = jnp.where(s == k, jnp.take_along_axis(by_s[k], index, axis=1), value)
        tiles.append(value)
    return jnp.concatenate(tiles, axis=1)


def layout_kernel(face_ref, v0_ref, v1_ref, v2_ref, half_ref, w0_ref, w1_ref, local_ref, order_ref, out_ref, scratch_ref):
    even = parity() == 0
    face = face_ref[...]
    local = own_rows(even, local_ref[...])
    first = jnp.where(even, local[0] + face, local[0])
    last = jnp.where(even, local[-1], local[-1] + face)
    w2 = jnp.concatenate([first[None], local[1:-1], last[None]], axis=0)
    fields = [own_rows(even, x[...]) for x in (v0_ref, v1_ref, v2_ref)]
    fields.extend((own_of_half(even, half_ref[...]), w0_ref[...], w1_ref[...], w2))
    for k, x in enumerate(fields):
        out_ref[k] = to_output(x, order_ref, scratch_ref, k)


def combine_kernel(sums_ref, fields_ref, p_ref, r_ref):
    line = jnp.sum(sums_ref[...], axis=0, keepdims=True)
    for step in (4, 2, 1):
        line = line + roll(line, -step, 1)
    shape = (NP, LANES)
    h00, h01, h02, h11, h12, h22, g0, g1, g2 = [jnp.broadcast_to(line[:, NP * k : NP * k + 1], shape) for k in range(9)]
    scale = 1.0 / h00
    m1, m2, m0 = h01 * scale, h02 * scale, g0 * scale
    k11, k12, k22 = h11 - m1 * h01, h12 - m1 * h02, h22 - m2 * h02
    f1, f2 = g1 - m1 * g0, g2 - m2 * g0
    second = 1.0 / k11
    n2 = k12 * second
    c2 = (f2 - n2 * f1) / (k22 - n2 * k12)
    c1 = f1 * second - n2 * c2
    c0 = m0 - m1 * c1 - m2 * c2
    for tile in range(7):
        x = [fields_ref[k, :, LANES * tile : LANES * tile + LANES] for k in range(7)]
        p_ref[:, LANES * tile : LANES * tile + LANES] = (c0 + STEPS[0]) * x[0] + (c1 + STEPS[1]) * x[1] + c2 * x[2]
        r_ref[:, LANES * tile : LANES * tile + LANES] = x[3] - (c0 * x[4] + c1 * x[5] + c2 * x[6])


def call(kernel, shapes, *args, scratch=()):
    return pl.pallas_call(
        kernel,
        out_shape=[jax.ShapeDtypeStruct(shape, jnp.float32) for shape in shapes],
        in_specs=[pl.BlockSpec(memory_space=pltpu.VMEM)] * len(args),
        out_specs=[pl.BlockSpec(memory_space=pltpu.VMEM)] * len(shapes),
        scratch_shapes=scratch,
        compiler_params=PARAMS,
    )(*args)


SMOOTH_SCRATCH = (
    pltpu.VMEM(((2 * NP + 1) * NP, LANES), jnp.float32),
    pltpu.VMEM((2, (NP + 2) * NP, LANES), jnp.float32),
)


def call_forcing(*args):
    shapes = [(7 * NP, NP, LANES), (4, NP, LANES)]
    scratch = [pltpu.SMEM(args[0].shape, jnp.int32)]
    scratch.extend(pltpu.VMEM(x.shape, x.dtype) for x in args[1:])
    scratch.extend(pltpu.VMEM(shape, jnp.float32) for shape in shapes)
    scratch.append(pltpu.SemaphoreType.DMA((len(args),)))
    scratch.append(pltpu.SemaphoreType.DMA((8,)))
    return pl.pallas_call(
        forcing_kernel,
        out_shape=[jax.ShapeDtypeStruct(shape, jnp.float32) for shape in shapes],
        in_specs=[pl.BlockSpec(memory_space=pltpu.HBM)] * len(args),
        out_specs=[pl.BlockSpec(memory_space=pltpu.HBM)] * len(shapes),
        scratch_shapes=scratch,
        compiler_params=pltpu.CompilerParams(vmem_limit_bytes=FORCING_VMEM),
    )(*args)


FORCING_TABLES = ("w3", "wmass", "ds", "dq", "jright", "jslope", "jright_t", "jleft", "jleft_a", "jleft_s", "jleft_t", "wfine")


def team_groups(count):
    return [[2 * c + side for c in range(count // 2)] for side in range(2)]


def shards(velocity, conv_past, metric, jacobian, element_slot):
    count = lax.axis_size("dom")
    t = {key: jnp.asarray(value) for key, value in TAB.items()}
    field = (NP, NP, LANES)
    chip = (ROWS, NP, LANES)
    half_shape = (2 * NP + 1, NP, LANES)
    edge = (EDGE, NP, LANES)
    pack, cross = call_forcing(
        element_slot, velocity, conv_past, metric, jacobian, *(t[key] for key in FORCING_TABLES)
    )
    cross = swap_cross(cross, count)
    pack = pl.pallas_call(
        stage_kernel,
        out_shape=jax.ShapeDtypeStruct(pack.shape, jnp.float32),
        in_specs=[pl.BlockSpec(memory_space=pltpu.HBM)],
        out_specs=pl.BlockSpec(memory_space=pltpu.VMEM),
        scratch_shapes=[pltpu.SemaphoreType.DMA(())],
        compiler_params=PARAMS,
    )(pack)
    (own,) = call(pair_kernel, [(7 * NP + 4, NP, LANES)], pack, cross)
    mate = swap_inner(own, count)
    div, op, level, cross = call(
        divergence_kernel,
        [chip, (2, 4) + field, (NP, LANES), (EDGE + 1, NP, LANES)],
        own, mate, t["ds"], t["qright_t"],
    )
    solve = (t["sleft"], t["sright"], t["srback"], t["sback"])
    tables = (op, t["ds"], t["qright"], t["qright_t"])
    half, inv, part = call(
        first_smooth_kernel,
        [half_shape, (2 * MODES, ES * (NP + 2)), edge],
        div, swap_cross(cross, count), level, t["spread"], t["lam"], *solve,
        scratch=SMOOTH_SCRATCH,
    )
    vectors, locals_, images = [], [], []
    for step in STEPS:
        v, local, cross = call(
            operator_kernel, [chip, chip, edge], part, swap_inner(part, count), *tables
        )
        image, half, part = call(
            functools.partial(smooth_kernel, step),
            [field, half_shape, edge],
            half, local, swap_cross(cross, count), inv, *solve,
            scratch=SMOOTH_SCRATCH,
        )
        vectors.append(v)
        locals_.append(local)
        images.append(image)
    residual, parts = call(
        early_kernel, [chip, (5, NP, LANES)], t["ws"], div, *vectors, *locals_
    )
    v, sums = call(
        last_sums_kernel,
        [chip, (count // 2, LANES)],
        part, swap_inner(part, count), op, t["ds"], t["qright"], parts, *locals_, residual, t["ws"],
    )
    sums = lax.all_to_all(sums, "dom", 0, 0, tiled=True, axis_index_groups=team_groups(count))
    local, face = call(last_operator_kernel, [chip, (NP, LANES)], v, *tables)
    (fields,) = call(
        layout_kernel,
        [(7, NP, 896)],
        swap_cross(face, count), *vectors, v, half, *images, local, t["order"],
        scratch=[pltpu.VMEM((7, NP * NP, LANES), jnp.float32)],
    )
    return tuple(call(combine_kernel, [(NP, 896), (NP, 896)], sums, fields))


def solution(mesh):
    return jax.shard_map(
        shards,
        mesh=mesh,
        in_specs=(
            P(None, None, "dom", None),
            P(None, None, "dom", None),
            P(None, "dom", None),
            P("dom", None),
            P("dom"),
        ),
        out_specs=(P("dom", None), P("dom", None)),
        check_vma=False,
    )
```
